32 devices in a mesh: grp: 2 (over y), gx: 4 (over z), gy: 4 (over x, core).
Axes of the slice: x: 2, y: 2, z: 4, core: 2. Of those that a mesh axis runs over, the one named last changes fastest.
Arguments:
- counts: int32 [256, 256, 256], P(('grp', 'gx'), 'gy'), parts along dimension 0, may hold values from -40 to 999
Outputs:
- denoised: float32 [256, 256, 256], P(('grp', 'gx'), 'gy'), parts along dimension 0
The draws below stay inside these ranges and needn't reach their ends.
There are 2 independent parts, one for each index of `grp`. The reference program is written for one: setup_inputs(seed, part) draws one part's arguments, and reference() takes and returns one part's arrays. A program takes and returns all parts, laid end to end along the dimension named above; each array names one. Nothing has to cross between parts.
All inputs are finite; a program needn't handle non-finite values.
Results may differ from the reference program's by a relative error of at most 0.00005.
Values sent between devices are 32-bit elements; how exact they have to be, the bound alone decides.
No kernel may reach another device: no remote copies, remote signals or barrier semaphores. Data moves between devices by JAX's collectives and lax.ppermute only.
A program may use at most 64 MiB of HBM per device.

```python
import math
import jax
import jax.numpy as jnp
from jax import lax

NT = 256
LEVELS = 3
ITERS = 2
NX = 128
NY = 256


def plant(entries, own_key, low, top_value):
    place = [jax.random.randint(jax.random.fold_in(own_key, axis), (), 0, length) for axis, length in enumerate(entries.shape)]
    longest = entries.shape.index(max(entries.shape))
    beside = place[:longest] + [(place[longest] + 1) % entries.shape[longest]] + place[longest + 1:]
    return entries.at[tuple(place)].set(low).at[tuple(beside)].set(top_value)


def setup_inputs(seed: int = 0, part: int = 0) -> dict:
    keys = jax.random.split(jax.random.key(seed), 2)
    own_keys = jax.random.split(jax.random.fold_in(keys[1], part), 2)
    counts = plant(jax.random.randint(own_keys[0], (NX, NY, NT), -40, 1000), jax.random.fold_in(own_keys[0], 1), -40, 999).astype(jnp.int32)
    return {"counts": counts}


ROOT_THREE = math.sqrt(3.0)
TAP_SCALE = 4.0 * math.sqrt(2.0)
LOW_TAPS = [(1.0 + ROOT_THREE) / TAP_SCALE, (3.0 + ROOT_THREE) / TAP_SCALE, (3.0 - ROOT_THREE) / TAP_SCALE, (1.0 - ROOT_THREE) / TAP_SCALE]
HIGH_TAPS = [LOW_TAPS[3], -LOW_TAPS[2], LOW_TAPS[1], -LOW_TAPS[0]]
STEP_SIZE = 1.0
THRESHOLD = 0.1

def analyse(values, axis_dim):
    length = values.shape[axis_dim]
    low_part = None
    high_part = None
    for tap_index in range(4):
        rolled = jnp.roll(values, -tap_index, axis=axis_dim)
        picked = lax.slice_in_dim(rolled, 0, length, 2, axis_dim)
        if low_part is None:
            low_part = LOW_TAPS[tap_index] * picked
            high_part = HIGH_TAPS[tap_index] * picked
        else:
            low_part = low_part + LOW_TAPS[tap_index] * picked
            high_part = high_part + HIGH_TAPS[tap_index] * picked
    return (low_part, high_part)

def synthesise(low_part, high_part, axis_dim):
    summed = None
    for tap_index in range(4):
        weighted = LOW_TAPS[tap_index] * low_part + HIGH_TAPS[tap_index] * high_part
        spread = jnp.stack([weighted, jnp.zeros_like(weighted)], axis=axis_dim + 1)
        new_shape = list(weighted.shape)
        new_shape[axis_dim] = new_shape[axis_dim] * 2
        spread = spread.reshape(new_shape)
        rolled = jnp.roll(spread, tap_index, axis=axis_dim)
        summed = rolled if summed is None else summed + rolled
    return summed

def forward_all(volume):
    details = []
    approx = volume
    for level_no in range(LEVELS):
        subbands = []
        for x_band in analyse(approx, 0):
            for y_band in analyse(x_band, 1):
                t_low, t_high = analyse(y_band, 2)
                subbands.append(t_low)
                subbands.append(t_high)
        approx = subbands[0]
        details.append(subbands[1:])
    return (details, approx)

def inverse_all(details, approx):
    current = approx
    for level_no in reversed(range(LEVELS)):
        subbands = [current] + list(details[level_no])
        x_parts = []
        for x_pick in range(2):
            y_parts = []
            for y_pick in range(2):
                first = subbands[4 * x_pick + 2 * y_pick]
                second = subbands[4 * x_pick + 2 * y_pick + 1]
                y_parts.append(synthesise(first, second, 2))
            x_parts.append(synthesise(y_parts[0], y_parts[1], 1))
        current = synthesise(x_parts[0], x_parts[1], 0)
    return current

def shrink(values):
    return values - jnp.clip(values, -THRESHOLD, THRESHOLD)

def reference(counts):
    scaled = counts.astype(jnp.float32)
    observed = scaled * (1.0 / 64.0)
    weight = 1.0 / (1.0 + jnp.abs(scaled) * (1.0 / 64.0))
    grad_details, grad_approx = forward_all(-(weight * observed))
    details = [[shrink(-STEP_SIZE * entry) for entry in level_bands] for level_bands in grad_details]
    approx = -STEP_SIZE * grad_approx
    for turn_no in range(ITERS - 1):
        rebuilt = inverse_all(details, approx)
        grad_details, grad_approx = forward_all(weight * (rebuilt - observed))
        details = [[shrink(old_entry - STEP_SIZE * new_entry) for old_entry, new_entry in zip(old_bands, new_bands)] for old_bands, new_bands in zip(details, grad_details)]
        approx = approx - STEP_SIZE * grad_approx
    return inverse_all(details, approx)
```

```python
import functools
import math

import jax
import jax.numpy as jnp
import ml_dtypes
import numpy as np
from jax import lax
from jax.experimental import pallas as pl
from jax.experimental.pallas import tpu as pltpu
from jax.sharding import PartitionSpec as P

R3 = math.sqrt(3.0)
H0 = (1.0 + R3) / (4.0 * math.sqrt(2.0))
RHO = (1.0 - R3) / (1.0 + R3)
LOW_TAPS = [H0 * t for t in (1.0, R3, -R3 * RHO, RHO)]
HIGH_TAPS = [LOW_TAPS[3], -LOW_TAPS[2], LOW_TAPS[1], -LOW_TAPS[0]]
KAPPA = -R3 * (1.0 + RHO * RHO)
THRESHOLD = 0.1
LANES = 128


def shifted(x, axis, by):
    count = lax.axis_size(axis)
    return lax.ppermute(x, axis, [(i, (i + by) % count) for i in range(count)])


def time_matrix(length, width):
    matrix = np.zeros((width, width), np.float64)
    half = length // 2
    for k in range(half):
        for j in range(4):
            matrix[(2 * k + j) % length, k] += LOW_TAPS[j] * H0 * H0
            matrix[(2 * k + j) % length, half + k] += HIGH_TAPS[j] * H0 * H0
    return matrix


def parts_of(matrix):
    single = matrix.astype(np.float32)
    high = single.astype(ml_dtypes.bfloat16)
    low = (single - high.astype(np.float32)).astype(ml_dtypes.bfloat16)
    return np.stack([high, low])


def dot_parts(x, m_ref):
    high = x.astype(jnp.bfloat16)
    low = (x - high.astype(jnp.float32)).astype(jnp.bfloat16)
    dot = functools.partial(jnp.dot, preferred_element_type=jnp.float32)
    return dot(high, m_ref[0]) + (dot(low, m_ref[0]) + dot(high, m_ref[1]))


def ceil8(n):
    return (n + 7) // 8 * 8


class Sizes:
    def __init__(self, x, y, t):
        self.x, self.y, self.t = x, y, t
        self.lx = [x // 2 + 1, x // 4 + 2, x // 8 + 2]
        self.ly = [y // 2 + 1, y // 4 + 2, y // 8 + 2]
        self.py = [ceil8(n) for n in self.ly]
        p1, p2, p3 = self.py
        self.g = [(self.lx[0], 2, 4, p1, LANES), (self.lx[1], 2, 2, p2, LANES), (self.lx[2], 2, 2, p3, LANES)]
        self.zin = [y, p1, p2]
        self.zbase = [6, 5, 6]
        self.zrows = [ceil8(2 * (p - 1) + 4 + b) for p, b in zip(self.py, self.zbase)]
        self.xp = 4 * p1 + 2 * 2 * p2 + 3 * 2 * p3
        self.xn = 4 * p1 + 3 * 2 * p2 + 3 * 2 * p3
        n1, n2, n3 = self.lx[0] * 4, self.lx[1] * 2, self.lx[2] * 2
        self.yp = ceil8(n1 + 2 * n2 + 3 * n3)
        self.yn = ceil8(n1 + 3 * n2 + 3 * n3)


def lattice(v0, v1, v2, v3):
    a = v0 + R3 * v1
    b = v3 - R3 * v2
    return a + RHO * b, RHO * a - b


def lattice_t(low_next, high_next, low_here, high_here):
    a = low_next + RHO * high_next
    b = RHO * low_here - high_here
    return a - R3 * b, R3 * a + b


def x_lattice_static(rows, shape):
    v = [jnp.zeros(shape, jnp.float32) if r is None else r for r in rows]
    return lattice(*v)


def y_analysis(z_ref, index, base, count, low_ref, low_index, high_ref, high_index):
    v = [z_ref[index + (pl.ds(base + j, count, stride=2), slice(None))] for j in range(4)]
    low, high = lattice(*v)
    low_ref[low_index] = low
    high_ref[high_index] = high


def forward(sz, u_ref, f1, f2, f3, g1, g2, g3, a1, z1, a2, z2, a3, z3):
    x, y, t = sz.x, sz.y, sz.t
    half = t // 2

    def rows_x(s, carry):
        low, high = lattice(*[u_ref[2 * s + j] for j in range(4)])
        a1[s, 0] = low
        a1[s, 1] = high
        return carry

    lax.fori_loop(0, sz.lx[0], rows_x, 0)

    step = 6
    for s0 in range(0, sz.lx[0], step):
        n = min(step, sz.lx[0] - s0)
        out = dot_parts(a1[s0 : s0 + n].reshape(n * 2 * y, t), f1).reshape(n, 2, y, t)
        z1[s0 : s0 + n, :, 0, 8 : 8 + y, :] = out[..., :half]
        z1[s0 : s0 + n, :, 1, 8 : 8 + y, :] = out[..., half:]

    def cols_1(s, carry):
        z1[s, :, :, 0:8, :] = jnp.zeros((2, 2, 8, LANES), jnp.float32)
        tail = sz.zrows[0] - 8 - y
        z1[s, :, :, 8 + y :, :] = jnp.zeros((2, 2, tail, LANES), jnp.float32)
        for xb in range(2):
            for tb in range(2):
                y_analysis(z1, (s, xb, tb), sz.zbase[0], sz.py[0], g1, (s, xb, tb), g1, (s, xb, 2 + tb))
        return carry

    lax.fori_loop(0, sz.lx[0], cols_1, 0)

    for level, (src, offset, a, z, f, g) in enumerate(((g1, 3, a2, z2, f2, g2), (g2, 2, a3, z3, f3, g3)), 1):
        rows_in, count = sz.lx[level - 1], sz.lx[level]
        p_in, p_out = sz.py[level - 1], sz.py[level]
        for s in range(count):
            picks = [2 * s + j - offset for j in range(4)]
            rows = [src[i, 0, 0] if 0 <= i < rows_in else None for i in picks]
            low, high = x_lattice_static(rows, (p_in, LANES))
            a[s, 0] = low
            a[s, 1] = high
        out = dot_parts(a[...].reshape(count * 2 * p_in, LANES), f)
        z[:, :, 0:8, :] = jnp.zeros((count, 2, 8, LANES), jnp.float32)
        z[:, :, 8 : 8 + p_in, :] = out.reshape(count, 2, p_in, LANES)
        tail = sz.zrows[level] - 8 - p_in
        if tail:
            z[:, :, 8 + p_in :, :] = jnp.zeros((count, 2, tail, LANES), jnp.float32)
        for s in range(count):
            for xb in range(2):
                y_analysis(z, (s, xb), sz.zbase[level], p_out, g, (s, xb, 0), g, (s, xb, 1))


def pack_x(sz, g1, g2, g3, mp, mn):
    p1, p2, p3 = sz.py

    def put(ref, pieces):
        at = 0
        for piece, rows in pieces:
            ref[at : at + rows] = piece.reshape(rows, LANES)
            at += rows

    l2, l3 = sz.lx[1], sz.lx[2]
    put(mp, [(g1[0, 1], 4 * p1), (g2[0, 1], 2 * p2), (g2[1, 1], 2 * p2),
             (g3[0, 1], 2 * p3), (g3[1, 0], 2 * p3), (g3[1, 1], 2 * p3)])
    put(mn, [(g1[sz.lx[0] - 1, 0], 4 * p1), (g2[l2 - 2, 0], 2 * p2), (g2[l2 - 2, 1], 2 * p2), (g2[l2 - 1, 0], 2 * p2),
             (g3[l3 - 2, 0], 2 * p3), (g3[l3 - 2, 1], 2 * p3), (g3[l3 - 1, 0], 2 * p3)])


def fix_x(sz, g1, g2, g3, rn, rp):
    p1, p2, p3 = sz.py
    l1, l2, l3 = sz.lx

    def take(ref, at, n, p):
        return ref[at : at + n * p].reshape(n, p, LANES)

    high = take(rn, 0, 4, p1)
    g1[l1 - 1, 0] += -RHO * high
    g1[l1 - 1, 1] += high
    low = take(rp, 0, 4, p1)
    g1[0, 0] += low
    g1[0, 1] += RHO * low
    at = 4 * p1
    h0 = take(rn, at, 2, p2)
    h1 = take(rn, at + 2 * p2, 2, p2)
    g2[l2 - 2, 0] += -RHO * h0
    g2[l2 - 2, 1] += h0
    g2[l2 - 1, 0] += KAPPA * h0 - RHO * h1
    g2[l2 - 1, 1] += h1
    w0 = take(rp, at, 2, p2)
    w1 = take(rp, at + 2 * p2, 2, p2)
    w2 = take(rp, at + 4 * p2, 2, p2)
    g2[0, 0] += w0
    g2[0, 1] += w1
    g2[1, 0] += w2
    g2[1, 1] += RHO * w2
    an = at + 4 * p2
    h0 = take(rn, an, 2, p3)
    g3[l3 - 2, 0] += -RHO * h0
    g3[l3 - 2, 1] += h0
    g3[l3 - 1, 0] += take(rn, an + 2 * p3, 2, p3)
    g3[l3 - 1, 1] += take(rn, an + 4 * p3, 2, p3)
    ap = at + 6 * p2
    g3[0, 0] += take(rp, ap, 2, p3)
    g3[0, 1] += take(rp, ap + 2 * p3, 2, p3)
    w2 = take(rp, ap + 4 * p3, 2, p3)
    g3[1, 0] += w2
    g3[1, 1] += RHO * w2


def pack_y(sz, g1, g2, g3, mp, mn):
    k1, k2, k3 = sz.ly
    at_p = at_n = 0
    for s in range(sz.lx[0]):
        for xb in range(2):
            for tb in range(2):
                mp[at_p : at_p + 1] = g1[s, xb, 2 + tb, 0:1]
                mn[at_n : at_n + 1] = g1[s, xb, tb, k1 - 1 : k1]
                at_p += 1
                at_n += 1
    for s in range(sz.lx[1]):
        for xb in range(2):
            mp[at_p : at_p + 2] = g2[s, xb, 1, 0:2]
            mn[at_n : at_n + 2] = g2[s, xb, 0, k2 - 2 : k2]
            mn[at_n + 2 : at_n + 3] = g2[s, xb, 1, k2 - 2 : k2 - 1]
            at_p += 2
            at_n += 3
    for s in range(sz.lx[2]):
        for xb in range(2):
            mp[at_p : at_p + 2] = g3[s, xb, 1, 0:2]
            mp[at_p + 2 : at_p + 3] = g3[s, xb, 0, 1:2]
            mn[at_n : at_n + 2] = g3[s, xb, 0, k3 - 2 : k3]
            mn[at_n + 2 : at_n + 3] = g3[s, xb, 1, k3 - 2 : k3 - 1]
            at_p += 3
            at_n += 3
    if at_p < sz.yp:
        mp[at_p:] = jnp.zeros((sz.yp - at_p, LANES), jnp.float32)
    if at_n < sz.yn:
        mn[at_n:] = jnp.zeros((sz.yn - at_n, LANES), jnp.float32)


def fix_y(sz, g1, g2, g3, rn, rp):
    k1, k2, k3 = sz.ly
    at_p = at_n = 0

    def add(g, index, row, value):
        g[index + (slice(row, row + 1), slice(None))] += value

    for s in range(sz.lx[0]):
        for xb in range(2):
            for tb in range(2):
                high = rn[at_n : at_n + 1]
                add(g1, (s, xb, tb), k1 - 1, -RHO * high)
                add(g1, (s, xb, 2 + tb), k1 - 1, high)
                low = rp[at_p : at_p + 1]
                add(g1, (s, xb, tb), 0, low)
                add(g1, (s, xb, 2 + tb), 0, RHO * low)
                at_p += 1
                at_n += 1
    for s in range(sz.lx[1]):
        for xb in range(2):
            h0, h1 = rn[at_n : at_n + 1], rn[at_n + 1 : at_n + 2]
            add(g2, (s, xb, 0), k2 - 2, -RHO * h0)
            add(g2, (s, xb, 1), k2 - 2, h0)
            add(g2, (s, xb, 0), k2 - 1, KAPPA * h0 - RHO * h1)
            add(g2, (s, xb, 1), k2 - 1, h1)
            w0, w2, w1 = (rp[at_p + i : at_p + i + 1] for i in range(3))
            add(g2, (s, xb, 0), 0, w0)
            add(g2, (s, xb, 1), 0, w1)
            add(g2, (s, xb, 0), 1, w2)
            add(g2, (s, xb, 1), 1, RHO * w2)
            at_n += 2
            at_p += 3
    for s in range(sz.lx[2]):
        for xb in range(2):
            h0, h1, l1 = (rn[at_n + i : at_n + i + 1] for i in range(3))
            add(g3, (s, xb, 0), k3 - 2, -RHO * h0)
            add(g3, (s, xb, 1), k3 - 2, h0)
            add(g3, (s, xb, 0), k3 - 1, l1)
            add(g3, (s, xb, 1), k3 - 1, h1)
            w0, w2, w1 = (rp[at_p + i : at_p + i + 1] for i in range(3))
            add(g3, (s, xb, 0), 0, w0)
            add(g3, (s, xb, 1), 0, w1)
            add(g3, (s, xb, 0), 1, w2)
            add(g3, (s, xb, 1), 1, RHO * w2)
            at_n += 3
            at_p += 3


def shrink(v):
    return v - jnp.clip(v, -THRESHOLD, THRESHOLD)


def y_synthesis(low, high, count, t_ref, v_ref, index, start):
    a = low + RHO * high
    b = RHO * low - high
    t_ref[...] = a
    a = t_ref[1 : 1 + count]
    b = b[:count]
    v_ref[index + (pl.ds(start, count, stride=2), slice(None))] = a - R3 * b
    v_ref[index + (pl.ds(start + 1, count, stride=2), slice(None))] = R3 * a + b


def lane_below(limit, shape):
    return lax.broadcasted_iota(jnp.int32, shape, 1) < limit


def inverse(sz, details, emit, i1, i2, i3, ta, v3, b3, v2, b2, v1, b1):
    y, t = sz.y, sz.t
    half = t // 2
    p1, p2, p3 = sz.py
    l1, l2, l3 = sz.lx
    third = lane_below(t // 8, (p3, LANES))

    for s in range(l3):
        for xb in range(2):
            low = details(2, s, xb, 0, third if xb == 0 else None)
            high = details(2, s, xb, 1, None)
            y_synthesis(low, high, sz.ly[1] // 2, ta.at[2, s, xb, 0:p3], v3, (s, xb), 0)
    b3[...] = dot_parts(v3[...].reshape(l3 * 2 * p2, LANES), i3).reshape(l3, 2, p2, LANES)

    second = lane_below(t // 4, (p2, LANES))
    for p in range(l2 // 2):
        even, odd = lattice_t(b3[p + 1, 0], b3[p + 1, 1], b3[p, 0], b3[p, 1])
        for s, coarse in ((2 * p, even), (2 * p + 1, odd)):
            for xb in range(2):
                low = details(1, s, xb, 0, None)
                if xb == 0:
                    low = jnp.where(second, coarse, low)
                high = details(1, s, xb, 1, None)
                y_synthesis(low, high, (sz.ly[0] + 1) // 2, ta.at[1, s, xb, 0:p2], v2, (s, xb), 7)
    b2[...] = dot_parts(v2[:, :, 8 : 8 + p1, :].reshape(l2 * 2 * p1, LANES), i2).reshape(l2, 2, p1, LANES)

    def level_1(s, coarse):
        for xb in range(2):
            for tb in range(2):
                if xb == 0 and tb == 0:
                    low = coarse
                else:
                    low = details(0, s, xb, tb, None)
                high = details(0, s, xb, 2 + tb, None)
                y_synthesis(low, high, y // 2, ta.at[0, s, xb * 2 + tb, 0:p1], v1, (s, xb, tb), 0)

    def coarse_rows(p):
        return lattice_t(b2[p + 1, 0], b2[p + 1, 1], b2[p, 0], b2[p, 1])

    level_1(0, coarse_rows(0)[1])

    def pair_1(p, carry):
        even, odd = coarse_rows(p)
        level_1(2 * p - 1, even)
        level_1(2 * p, odd)
        return carry

    lax.fori_loop(1, l2 - 1, pair_1, 0)

    step = 6
    for s0 in range(0, l1, step):
        n = min(step, l1 - s0)
        v = jnp.concatenate([v1[s0 : s0 + n, :, 0], v1[s0 : s0 + n, :, 1]], axis=-1)
        b1[s0 : s0 + n] = dot_parts(v.reshape(n * 2 * y, t), i1).reshape(n, 2, y, t)

    def rows_x(p, carry):
        even, odd = lattice_t(b1[p + 1, 0], b1[p + 1, 1], b1[p, 0], b1[p, 1])
        emit(p, even, odd)
        return carry

    lax.fori_loop(0, sz.x // 2, rows_x, 0)


def border(sz, u_ref):
    zeros = jnp.zeros((2, sz.y, sz.t), jnp.float32)
    u_ref[0:2] = zeros
    u_ref[sz.x + 2 : sz.x + 4] = zeros


def first_kernel(sz, c_ref, f1, f2, f3, w_ref, g1, g2, g3, mp, mn, u, *scratch):
    border(sz, u)

    def rows(x, carry):
        value = c_ref[x].astype(jnp.float32) * (1.0 / 64.0)
        weight = 1.0 / (1.0 + jnp.abs(value))
        w_ref[x] = weight
        u[x + 2] = weight * value
        return carry

    lax.fori_loop(0, sz.x, rows, 0)
    forward(sz, u, f1, f2, f3, g1, g2, g3, *scratch)
    pack_x(sz, g1, g2, g3, mp, mn)


def edge_kernel(sz, g1i, g2i, g3i, rn, rp, g1, g2, g3, mp, mn):
    fix_x(sz, g1, g2, g3, rn, rp)
    pack_y(sz, g1, g2, g3, mp, mn)


def middle_kernel(sz, g1i, g2i, g3i, rn, rp, w_ref, f1, f2, f3, i1, i2, i3,
                  g1, g2, g3, q1, q2, q3, mp, mn, u, ta, v3, b3, v2, b2, v1, b1, *scratch):
    fix_y(sz, g1, g2, g3, rn, rp)
    border(sz, u)

    def details(level, s, xb, q, approx_lanes):
        value = (g1, g2, g3)[level][s, xb, q]
        small = shrink(value)
        return small if approx_lanes is None else jnp.where(approx_lanes, value, small)

    def emit(p, even, odd):
        u[2 * p + 2] = w_ref[2 * p] * even
        u[2 * p + 3] = w_ref[2 * p + 1] * odd

    inverse(sz, details, emit, i1, i2, i3, ta, v3, b3, v2, b2, v1, b1)
    forward(sz, u, f1, f2, f3, q1, q2, q3, *scratch)
    pack_x(sz, q1, q2, q3, mp, mn)


def last_kernel(sz, q1i, q2i, q3i, rn, rp, g1, g2, g3, i1, i2, i3, q1, q2, q3, out, ta, v3, b3, v2, b2, v1, b1):
    fix_y(sz, q1, q2, q3, rn, rp)

    def details(level, s, xb, q, approx_lanes):
        first = (g1, g2, g3)[level][s, xb, q]
        second = (q1, q2, q3)[level][s, xb, q]
        small = shrink(shrink(first) + (first - second))
        if approx_lanes is None:
            return small
        return jnp.where(approx_lanes, first + (first - second), small)

    def emit(p, even, odd):
        out[2 * p] = even
        out[2 * p + 1] = odd

    inverse(sz, details, emit, i1, i2, i3, ta, v3, b3, v2, b2, v1, b1)


def call(kernel, sz, outs, scratch, aliases, *args):
    vmem = pl.BlockSpec(memory_space=pltpu.VMEM)
    return pl.pallas_call(
        functools.partial(kernel, sz),
        out_shape=[jax.ShapeDtypeStruct(s, jnp.float32) for s in outs],
        in_specs=[vmem] * len(args),
        out_specs=[vmem] * len(outs),
        scratch_shapes=[pltpu.VMEM(s, jnp.float32) for s in scratch],
        input_output_aliases=aliases,
        compiler_params=pltpu.CompilerParams(vmem_limit_bytes=36 * 2**20),
    )(*args)


def on_device(counts):
    sz = Sizes(*counts.shape)
    t = sz.t
    fw = [time_matrix(t, t), time_matrix(t // 2, LANES), time_matrix(t // 4, LANES)]
    f = [jnp.asarray(parts_of(m)) for m in fw]
    i = [jnp.asarray(parts_of(m.T)) for m in fw]
    l1, l2, l3 = sz.lx
    p1, p2, p3 = sz.py
    wide = (sz.x, sz.y, sz.t)
    u = (sz.x + 4, sz.y, sz.t)
    fw_scratch = [(l1, 2, sz.y, t), (l1, 2, 2, sz.zrows[0], LANES), (l2, 2, p1, LANES), (l2, 2, sz.zrows[1], LANES),
                  (l3, 2, p2, LANES), (l3, 2, sz.zrows[2], LANES)]
    bw_scratch = [(3, l1, 4, p1 + 8, LANES), (l3, 2, p2, LANES), (l3, 2, p2, LANES), (l2, 2, p1 + 8, LANES),
                  (l2, 2, p1, LANES), (l1, 2, 2, sz.y, LANES), (l1, 2, sz.y, t)]
    to_prev, to_next = (sz.xp, LANES), (sz.xn, LANES)
    y_prev, y_next = (sz.yp, LANES), (sz.yn, LANES)
    same = {0: 0, 1: 1, 2: 2}

    def exchange(g, mp, mn):
        rn = shifted(mp, "gx", -1)
        rp = shifted(mn, "gx", 1)
        *g, mp, mn = call(edge_kernel, sz, sz.g + [y_prev, y_next], [], same, *g, rn, rp)
        return g, shifted(mp, "gy", -1), shifted(mn, "gy", 1)

    weight, *g, mp, mn = call(first_kernel, sz, [wide] + sz.g + [to_prev, to_next], [u] + fw_scratch, {}, counts, *f)
    g, rn, rp = exchange(g, mp, mn)
    *rest, mp, mn = call(middle_kernel, sz, sz.g + sz.g + [to_prev, to_next], [u] + bw_scratch + fw_scratch, same,
                         *g, rn, rp, weight, *f, *i)
    g, q = rest[:3], rest[3:]
    q, rn, rp = exchange(q, mp, mn)
    return call(last_kernel, sz, sz.g + [wide], bw_scratch, same, *q, rn, rp, *g, *i)[3]


def solution(mesh):
    spec = P(("grp", "gx"), "gy", None)
    return jax.shard_map(on_device, mesh=mesh, in_specs=(spec,), out_specs=spec, check_vma=False)
```

```python
import functools
import math

import jax
import jax.numpy as jnp
import numpy as np
from jax import lax
from jax.experimental import pallas as pl
from jax.experimental.pallas import tpu as pltpu
from jax.sharding import PartitionSpec as P

R3 = math.sqrt(3.0)
H0 = (1.0 + R3) / (4.0 * math.sqrt(2.0))
RHO = (1.0 - R3) / (1.0 + R3)
LOW_TAPS = [H0 * t for t in (1.0, R3, -R3 * RHO, RHO)]
HIGH_TAPS = [LOW_TAPS[3], -LOW_TAPS[2], LOW_TAPS[1], -LOW_TAPS[0]]
KAPPA = -R3 * (1.0 + RHO * RHO)
THRESHOLD = 0.1
LANES = 128


def shifted(x, axis, by):
    count = lax.axis_size(axis)
    return lax.ppermute(x, axis, [(i, (i + by) % count) for i in range(count)])


def time_matrix(length, width):
    matrix = np.zeros((width, width), np.float64)
    half = length // 2
    for k in range(half):
        for j in range(4):
            matrix[(2 * k + j) % length, k] += LOW_TAPS[j] * H0 * H0
            matrix[(2 * k + j) % length, half + k] += HIGH_TAPS[j] * H0 * H0
    return matrix


def pack_matrices(first, second, third):
    packed = np.zeros((first.shape[0] + LANES, first.shape[0]), np.float32)
    packed[: first.shape[0]] = first
    packed[first.shape[0] :, :LANES] = second
    packed[first.shape[0] :, LANES : 2 * LANES] = third
    return packed


def split(x):
    high = x.astype(jnp.bfloat16)
    return high, (x - high.astype(jnp.float32)).astype(jnp.bfloat16)


def unpack_matrices(packed, m1, m2, m3):
    t = packed.shape[1]
    m1[0], m1[1] = split(packed[:t])
    m2[0], m2[1] = split(packed[t:, :LANES])
    m3[0], m3[1] = split(packed[t:, LANES : 2 * LANES])


def dot_parts(x, m_ref):
    high, low = split(x)
    dot = functools.partial(jnp.dot, preferred_element_type=jnp.float32)
    return dot(high, m_ref[0]) + (dot(low, m_ref[0]) + dot(high, m_ref[1]))


def ceil8(n):
    return (n + 7) // 8 * 8


class Sizes:
    def __init__(self, x, y, t):
        self.x, self.y, self.t = x, y, t
        self.lx = [x // 2 + 1, x // 4 + 2, x // 8 + 2]
        self.ly = [y // 2 + 1, y // 4 + 2, y // 8 + 2]
        self.py = [ceil8(n) for n in self.ly]
        p1, p2, p3 = self.py
        self.g = [(self.lx[0], 2, 4, p1, LANES), (self.lx[1], 2, 2, p2, LANES), (self.lx[2], 2, 2, p3, LANES)]
        self.zin = [y, p1, p2]
        self.zbase = [6, 5, 6]
        self.zrows = [ceil8(2 * (p - 1) + 4 + b) for p, b in zip(self.py, self.zbase)]
        self.main = [y // 2, y // 4, y // 8]
        self.xp_pieces = [4, 4, 3]
        self.xn_pieces = [4, 6, 3]
        self.xp = self.x_rows(self.xp_pieces)
        self.xn = self.x_rows(self.xn_pieces)
        n1, n2, n3 = self.lx[0] * 4, self.lx[1] * 2, self.lx[2] * 2
        self.yp = ceil8(n1 + 2 * n2 + 3 * n3)
        self.yn = ceil8(n1 + 3 * n2 + 3 * n3)


    def x_rows(self, pieces):
        return ceil8(sum(n * w for n, w in zip(pieces, self.ly)))

    def x_offsets(self, pieces):
        at = 0
        mains, extras = [], []
        for n, m in zip(pieces, self.main):
            mains.append([at + i * m for i in range(n)])
            at += n * m
        for n, m, w in zip(pieces, self.main, self.ly):
            extras.append([at + i * (w - m) for i in range(n)])
            at += n * (w - m)
        return [list(zip(a, b)) for a, b in zip(mains, extras)]


def lattice(v0, v1, v2, v3):
    a = v0 + R3 * v1
    b = v3 - R3 * v2
    return a + RHO * b, RHO * a - b


def lattice_t(low_next, high_next, low_here, high_here):
    a = low_next + RHO * high_next
    b = RHO * low_here - high_here
    return a - R3 * b, R3 * a + b


def x_lattice_static(rows, shape):
    v = [jnp.zeros(shape, jnp.float32) if r is None else r for r in rows]
    return lattice(*v)


def y_analysis(z_ref, index, base, count, low_ref, low_index, high_ref, high_index):
    v = [z_ref[index + (pl.ds(base + j, count, stride=2), slice(None))] for j in range(4)]
    low, high = lattice(*v)
    low_ref[low_index] = low
    high_ref[high_index] = high


def forward(sz, u_ref, f1, f2, f3, g1, g2, g3, a1, z1, a2, z2, a3, z3):
    x, y, t = sz.x, sz.y, sz.t
    half = t // 2

    def rows_x(s, carry):
        low, high = lattice(*[u_ref[2 * s + j] for j in range(4)])
        a1[s, 0] = low
        a1[s, 1] = high
        return carry

    lax.fori_loop(0, sz.lx[0], rows_x, 0)

    step = 6
    for s0 in range(0, sz.lx[0], step):
        n = min(step, sz.lx[0] - s0)
        out = dot_parts(a1[s0 : s0 + n].reshape(n * 2 * y, t), f1).reshape(n, 2, y, t)
        z1[s0 : s0 + n, :, 0, 8 : 8 + y, :] = out[..., :half]
        z1[s0 : s0 + n, :, 1, 8 : 8 + y, :] = out[..., half:]

    def cols_1(s, carry):
        z1[s, :, :, 0:8, :] = jnp.zeros((2, 2, 8, LANES), jnp.float32)
        tail = sz.zrows[0] - 8 - y
        z1[s, :, :, 8 + y :, :] = jnp.zeros((2, 2, tail, LANES), jnp.float32)
        for xb in range(2):
            for tb in range(2):
                y_analysis(z1, (s, xb, tb), sz.zbase[0], sz.py[0], g1, (s, xb, tb), g1, (s, xb, 2 + tb))
        return carry

    lax.fori_loop(0, sz.lx[0], cols_1, 0)

    for level, (src, offset, a, z, f, g) in enumerate(((g1, 3, a2, z2, f2, g2), (g2, 2, a3, z3, f3, g3)), 1):
        rows_in, count = sz.lx[level - 1], sz.lx[level]
        p_in, p_out = sz.py[level - 1], sz.py[level]
        for s in range(count):
            picks = [2 * s + j - offset for j in range(4)]
            rows = [src[i, 0, 0] if 0 <= i < rows_in else None for i in picks]
            low, high = x_lattice_static(rows, (p_in, LANES))
            a[s, 0] = low
            a[s, 1] = high
        out = dot_parts(a[...].reshape(count * 2 * p_in, LANES), f)
        z[:, :, 0:8, :] = jnp.zeros((count, 2, 8, LANES), jnp.float32)
        z[:, :, 8 : 8 + p_in, :] = out.reshape(count, 2, p_in, LANES)
        tail = sz.zrows[level] - 8 - p_in
        if tail:
            z[:, :, 8 + p_in :, :] = jnp.zeros((count, 2, tail, LANES), jnp.float32)
        for s in range(count):
            for xb in range(2):
                y_analysis(z, (s, xb), sz.zbase[level], p_out, g, (s, xb, 0), g, (s, xb, 1))


def pack_x(sz, g1, g2, g3, mp, mn):
    l1, l2, l3 = sz.lx
    lower = lane_below(LANES // 2, (1, LANES))

    def put(ref, pieces, level, items):
        m, w = sz.main[level], sz.ly[level]
        for (main, extra), item in zip(sz.x_offsets(pieces)[level], items):
            for at, lo, hi in ((main, 0, m), (extra, m, w)):
                if level < 2:
                    value = item[lo:hi]
                else:
                    value = jnp.where(lower, item[0, lo:hi], pltpu.roll(item[1, lo:hi], LANES // 2, 1))
                ref[at : at + hi - lo] = value

    put(mp, sz.xp_pieces, 0, [g1.at[0, 1, q] for q in range(4)])
    put(mn, sz.xn_pieces, 0, [g1.at[l1 - 1, 0, q] for q in range(4)])
    put(mp, sz.xp_pieces, 1, [g2.at[s, 1, q] for s in (0, 1) for q in (0, 1)])
    put(mn, sz.xn_pieces, 1, [g2.at[s, b, q] for s, b in ((l2 - 2, 0), (l2 - 2, 1), (l2 - 1, 0)) for q in (0, 1)])
    put(mp, sz.xp_pieces, 2, [g3.at[0, 1], g3.at[1, 0], g3.at[1, 1]])
    put(mn, sz.xn_pieces, 2, [g3.at[l3 - 2, 0], g3.at[l3 - 2, 1], g3.at[l3 - 1, 0]])


def fix_x(sz, g1, g2, g3, rn, rp):
    l1, l2, l3 = sz.lx
    lower = lane_below(LANES // 2, (1, LANES))

    def take(ref, pieces, level, lo, hi):
        part = 0 if lo == 0 else 1
        return [ref[at[part] : at[part] + hi - lo] for at in sz.x_offsets(pieces)[level]]

    def halves(value):
        return [jnp.where(lower, v, 0.0) for v in (value, pltpu.roll(value, LANES // 2, 1))]

    for level in range(3):
        m, w = sz.main[level], sz.ly[level]
        for lo, hi in ((0, m), (m, w)):
            n = take(rn, sz.xp_pieces, level, lo, hi)
            p = take(rp, sz.xn_pieces, level, lo, hi)
            if level == 0:
                for q in range(4):
                    g1[l1 - 1, 0, q, lo:hi] += -RHO * n[q]
                    g1[l1 - 1, 1, q, lo:hi] += n[q]
                    g1[0, 0, q, lo:hi] += p[q]
                    g1[0, 1, q, lo:hi] += RHO * p[q]
            elif level == 1:
                for q in range(2):
                    h0, h1 = n[q], n[2 + q]
                    g2[l2 - 2, 0, q, lo:hi] += -RHO * h0
                    g2[l2 - 2, 1, q, lo:hi] += h0
                    g2[l2 - 1, 0, q, lo:hi] += KAPPA * h0 - RHO * h1
                    g2[l2 - 1, 1, q, lo:hi] += h1
                    g2[0, 0, q, lo:hi] += p[q]
                    g2[0, 1, q, lo:hi] += p[2 + q]
                    g2[1, 0, q, lo:hi] += p[4 + q]
                    g2[1, 1, q, lo:hi] += RHO * p[4 + q]
            else:
                n, p = [halves(v) for v in n], [halves(v) for v in p]
                for q in range(2):
                    g3[l3 - 2, 0, q, lo:hi] += -RHO * n[0][q]
                    g3[l3 - 2, 1, q, lo:hi] += n[0][q]
                    g3[l3 - 1, 0, q, lo:hi] += n[1][q]
                    g3[l3 - 1, 1, q, lo:hi] += n[2][q]
                    g3[0, 0, q, lo:hi] += p[0][q]
                    g3[0, 1, q, lo:hi] += p[1][q]
                    g3[1, 0, q, lo:hi] += p[2][q]
                    g3[1, 1, q, lo:hi] += RHO * p[2][q]


def pack_y(sz, g1, g2, g3, mp, mn):
    k1, k2, k3 = sz.ly
    at_p = at_n = 0
    for s in range(sz.lx[0]):
        for xb in range(2):
            for tb in range(2):
                mp[at_p : at_p + 1] = g1[s, xb, 2 + tb, 0:1]
                mn[at_n : at_n + 1] = g1[s, xb, tb, k1 - 1 : k1]
                at_p += 1
                at_n += 1
    for s in range(sz.lx[1]):
        for xb in range(2):
            mp[at_p : at_p + 2] = g2[s, xb, 1, 0:2]
            mn[at_n : at_n + 2] = g2[s, xb, 0, k2 - 2 : k2]
            mn[at_n + 2 : at_n + 3] = g2[s, xb, 1, k2 - 2 : k2 - 1]
            at_p += 2
            at_n += 3
    for s in range(sz.lx[2]):
        for xb in range(2):
            mp[at_p : at_p + 2] = g3[s, xb, 1, 0:2]
            mp[at_p + 2 : at_p + 3] = g3[s, xb, 0, 1:2]
            mn[at_n : at_n + 2] = g3[s, xb, 0, k3 - 2 : k3]
            mn[at_n + 2 : at_n + 3] = g3[s, xb, 1, k3 - 2 : k3 - 1]
            at_p += 3
            at_n += 3
    if at_p < sz.yp:
        mp[at_p:] = jnp.zeros((sz.yp - at_p, LANES), jnp.float32)
    if at_n < sz.yn:
        mn[at_n:] = jnp.zeros((sz.yn - at_n, LANES), jnp.float32)


def fix_y(sz, g1, g2, g3, rn, rp):
    k1, k2, k3 = sz.ly
    at_p = at_n = 0

    def add(g, index, row, value):
        g[index + (slice(row, row + 1), slice(None))] += value

    for s in range(sz.lx[0]):
        for xb in range(2):
            for tb in range(2):
                high = rn[at_n : at_n + 1]
                add(g1, (s, xb, tb), k1 - 1, -RHO * high)
                add(g1, (s, xb, 2 + tb), k1 - 1, high)
                low = rp[at_p : at_p + 1]
                add(g1, (s, xb, tb), 0, low)
                add(g1, (s, xb, 2 + tb), 0, RHO * low)
                at_p += 1
                at_n += 1
    for s in range(sz.lx[1]):
        for xb in range(2):
            h0, h1 = rn[at_n : at_n + 1], rn[at_n + 1 : at_n + 2]
            add(g2, (s, xb, 0), k2 - 2, -RHO * h0)
            add(g2, (s, xb, 1), k2 - 2, h0)
            add(g2, (s, xb, 0), k2 - 1, KAPPA * h0 - RHO * h1)
            add(g2, (s, xb, 1), k2 - 1, h1)
            w0, w2, w1 = (rp[at_p + i : at_p + i + 1] for i in range(3))
            add(g2, (s, xb, 0), 0, w0)
            add(g2, (s, xb, 1), 0, w1)
            add(g2, (s, xb, 0), 1, w2)
            add(g2, (s, xb, 1), 1, RHO * w2)
            at_n += 2
            at_p += 3
    for s in range(sz.lx[2]):
        for xb in range(2):
            h0, h1, l1 = (rn[at_n + i : at_n + i + 1] for i in range(3))
            add(g3, (s, xb, 0), k3 - 2, -RHO * h0)
            add(g3, (s, xb, 1), k3 - 2, h0)
            add(g3, (s, xb, 0), k3 - 1, l1)
            add(g3, (s, xb, 1), k3 - 1, h1)
            w0, w2, w1 = (rp[at_p + i : at_p + i + 1] for i in range(3))
            add(g3, (s, xb, 0), 0, w0)
            add(g3, (s, xb, 1), 0, w1)
            add(g3, (s, xb, 0), 1, w2)
            add(g3, (s, xb, 1), 1, RHO * w2)
            at_n += 3
            at_p += 3


def shrink(v):
    return v - jnp.clip(v, -THRESHOLD, THRESHOLD)


def y_synthesis(low, high, count, t_ref, v_ref, index, start):
    a = low + RHO * high
    b = RHO * low - high
    t_ref[...] = a
    a = t_ref[1 : 1 + count]
    b = b[:count]
    v_ref[index + (pl.ds(start, count, stride=2), slice(None))] = a - R3 * b
    v_ref[index + (pl.ds(start + 1, count, stride=2), slice(None))] = R3 * a + b


def lane_below(limit, shape):
    return lax.broadcasted_iota(jnp.int32, shape, 1) < limit


def level_1_columns(sz, details, s, xb, tb, coarse, ta, v1, index):
    low = coarse if coarse is not None else details(0, s, xb, tb, None)
    high = details(0, s, xb, 2 + tb, None)
    y_synthesis(low, high, sz.y // 2, ta.at[s, xb * 2 + tb, 0 : sz.py[0]], v1, index, 0)


def times_back(sz, v_low, v_high, i1):
    v = jnp.concatenate([v_low, v_high], axis=-1)
    return dot_parts(v.reshape(-1, sz.t), i1).reshape(v.shape)


def inner_inverse(sz, details, i1, va, ba, ta, v1):
    l1 = sz.lx[0]

    def rows(s, carry):
        level_1_columns(sz, details, s, 0, 1, None, ta, va, (s,))
        level_1_columns(sz, details, s, 1, 0, None, ta, v1, (s, 0))
        level_1_columns(sz, details, s, 1, 1, None, ta, v1, (s, 1))
        return carry

    lax.fori_loop(1, l1 - 1, rows, 0)
    step = 8
    for s0 in range(1, l1 - 1, step):
        n = min(step, l1 - 1 - s0)
        ba[s0 : s0 + n] = times_back(sz, v1[s0 : s0 + n, 0], v1[s0 : s0 + n, 1], i1)


def inverse(sz, details, emit, va, ba, i1, i2, i3, ta1, ta, v3, b3, v2, b2, v1, b1, ve):
    y, t = sz.y, sz.t
    p1, p2, p3 = sz.py
    l1, l2, l3 = sz.lx
    third = lane_below(t // 8, (p3, LANES))

    for e, s in enumerate((0, l1 - 1)):
        level_1_columns(sz, details, s, 0, 1, None, ta1, va, (s,))
        level_1_columns(sz, details, s, 1, 0, None, ta1, ve, (e, 0))
        level_1_columns(sz, details, s, 1, 1, None, ta1, ve, (e, 1))

    for s in range(l3):
        for xb in range(2):
            low = details(2, s, xb, 0, third if xb == 0 else None)
            high = details(2, s, xb, 1, None)
            y_synthesis(low, high, sz.ly[1] // 2, ta.at[1, s, xb, 0:p3], v3, (s, xb), 0)
    b3[...] = dot_parts(v3[...].reshape(l3 * 2 * p2, LANES), i3).reshape(l3, 2, p2, LANES)

    second = lane_below(t // 4, (p2, LANES))
    for p in range(l2 // 2):
        even, odd = lattice_t(b3[p + 1, 0], b3[p + 1, 1], b3[p, 0], b3[p, 1])
        for s, coarse in ((2 * p, even), (2 * p + 1, odd)):
            for xb in range(2):
                low = details(1, s, xb, 0, None)
                if xb == 0:
                    low = jnp.where(second, coarse, low)
                high = details(1, s, xb, 1, None)
                y_synthesis(low, high, (sz.ly[0] + 1) // 2, ta.at[0, s, xb, 0:p2], v2, (s, xb), 7)
    b2[...] = dot_parts(v2[:, :, 8 : 8 + p1, :].reshape(l2 * 2 * p1, LANES), i2).reshape(l2, 2, p1, LANES)

    edge = times_back(sz, ve[:, 0], ve[:, 1], i1)
    ba[0] = edge[0]
    ba[l1 - 1] = edge[1]

    def coarse_rows(p):
        return lattice_t(b2[p + 1, 0], b2[p + 1, 1], b2[p, 0], b2[p, 1])

    level_1_columns(sz, details, 0, 0, 0, coarse_rows(0)[1], ta1, v1, (0,))

    def pair_1(p, carry):
        even, odd = coarse_rows(p)
        level_1_columns(sz, details, 2 * p - 1, 0, 0, even, ta1, v1, (2 * p - 1,))
        level_1_columns(sz, details, 2 * p, 0, 0, odd, ta1, v1, (2 * p,))
        return carry

    lax.fori_loop(1, l2 - 1, pair_1, 0)

    step = 9
    for s0 in range(0, l1, step):
        n = min(step, l1 - s0)
        b1[s0 : s0 + n] = times_back(sz, v1[s0 : s0 + n], va[s0 : s0 + n], i1)

    def rows_x(p, carry):
        even, odd = lattice_t(b1[p + 1], ba[p + 1], b1[p], ba[p])
        emit(p, even, odd)
        return carry

    return rows_x


def border(sz, u_ref):
    zeros = jnp.zeros((2, sz.y, sz.t), jnp.float32)
    u_ref[0:2] = zeros
    u_ref[sz.x + 2 : sz.x + 4] = zeros


def first_kernel(sz, c_hbm, f_hbm, w_ref, g1, g2, g3, mp, mn, c, fv, f1, f2, f3, u, sems, *scratch):
    step = 8
    chunks = range(0, sz.x, step)
    copies = [pltpu.make_async_copy(c_hbm.at[x0 : x0 + step], c.at[x0 : x0 + step], sems.at[i])
              for i, x0 in enumerate(chunks)]
    matrices = pltpu.make_async_copy(f_hbm, fv, sems.at[len(copies)])
    for copy in copies + [matrices]:
        copy.start()
    border(sz, u)

    def rows(x, carry):
        value = c[x].astype(jnp.float32) * (1.0 / 64.0)
        weight = 1.0 / (1.0 + jnp.abs(value))
        w_ref[x] = weight
        u[x + 2] = weight * value
        return carry

    for x0, copy in zip(chunks, copies):
        copy.wait()
        lax.fori_loop(x0, x0 + step, rows, 0)
    matrices.wait()
    unpack_matrices(fv, f1, f2, f3)
    forward(sz, u, f1, f2, f3, g1, g2, g3, *scratch)
    pack_y(sz, g1, g2, g3, mp, mn)


def edge_kernel(sz, g1i, g2i, g3i, rn, rp, g1, g2, g3, mp, mn):
    fix_y(sz, g1, g2, g3, rn, rp)
    pack_x(sz, g1, g2, g3, mp, mn)


def first_details(g1, g2, g3):
    def details(level, s, xb, q, approx_lanes):
        value = (g1, g2, g3)[level][s, xb, q]
        small = shrink(value)
        return small if approx_lanes is None else jnp.where(approx_lanes, value, small)

    return details


def second_details(g1, g2, g3, q1, q2, q3):
    def details(level, s, xb, q, approx_lanes):
        first = (g1, g2, g3)[level][s, xb, q]
        second = (q1, q2, q3)[level][s, xb, q]
        small = shrink(shrink(first) + (first - second))
        if approx_lanes is None:
            return small
        return jnp.where(approx_lanes, first + (first - second), small)

    return details


def inner_first_kernel(sz, g1, iv, va, ba, i1, i2, i3, ta, v1):
    unpack_matrices(iv, i1, i2, i3)
    inner_inverse(sz, first_details(g1, None, None), i1, va, ba, ta, v1)


def inner_last_kernel(sz, g1, q1, iv, va, ba, i1, i2, i3, ta, v1):
    unpack_matrices(iv, i1, i2, i3)
    inner_inverse(sz, second_details(g1, None, None, q1, None, None), i1, va, ba, ta, v1)


def middle_kernel(sz, g1i, g2i, g3i, vai, bai, rn, rp, w_ref, fv, iv, g1, g2, g3, va, ba, q1, q2, q3, mp, mn,
                  u, f1, f2, f3, i1, i2, i3, ta1, ta, v3, b3, v2, b2, v1, b1, ve, *scratch):
    unpack_matrices(fv, f1, f2, f3)
    unpack_matrices(iv, i1, i2, i3)
    fix_x(sz, g1, g2, g3, rn, rp)
    border(sz, u)

    def emit(p, even, odd):
        u[2 * p + 2] = w_ref[2 * p] * even
        u[2 * p + 3] = w_ref[2 * p + 1] * odd

    rows = inverse(sz, first_details(g1, g2, g3), emit, va, ba, i1, i2, i3, ta1, ta, v3, b3, v2, b2, v1, b1, ve)
    lax.fori_loop(0, sz.x // 2, rows, 0)
    forward(sz, u, f1, f2, f3, q1, q2, q3, *scratch)
    pack_y(sz, q1, q2, q3, mp, mn)


def last_kernel(sz, q1i, q2i, q3i, vai, bai, rn, rp, g1, g2, g3, iv, q1, q2, q3, va, ba, out_hbm,
                out, sems, i1, i2, i3, ta1, ta, v3, b3, v2, b2, v1, b1, ve):
    unpack_matrices(iv, i1, i2, i3)
    fix_x(sz, q1, q2, q3, rn, rp)

    def emit(p, even, odd):
        out[2 * p] = even
        out[2 * p + 1] = odd

    details = second_details(g1, g2, g3, q1, q2, q3)
    rows = inverse(sz, details, emit, va, ba, i1, i2, i3, ta1, ta, v3, b3, v2, b2, v1, b1, ve)
    step = 8
    copies = []
    for i, x0 in enumerate(range(0, sz.x, step)):
        lax.fori_loop(x0 // 2, (x0 + step) // 2, rows, 0)
        copies.append(pltpu.make_async_copy(out.at[x0 : x0 + step], out_hbm.at[x0 : x0 + step], sems.at[i]))
        copies[-1].start()
    for copy in copies:
        copy.wait()


VMEM = pltpu.MemorySpace.VMEM
HBM = pltpu.MemorySpace.HBM


def call(kernel, sz, outs, scratch, aliases, *args, ins_hbm=(), outs_hbm=(), flops=0):
    def specs(n, in_hbm):
        return [pl.BlockSpec(memory_space=HBM if k in in_hbm else VMEM) for k in range(n)]

    return pl.pallas_call(
        functools.partial(kernel, sz),
        out_shape=[jax.ShapeDtypeStruct(s, jnp.float32) for s in outs],
        in_specs=specs(len(args), ins_hbm),
        out_specs=specs(len(outs), outs_hbm),
        scratch_shapes=scratch,
        input_output_aliases=aliases,
        cost_estimate=pl.CostEstimate(flops=flops, bytes_accessed=flops // 100, transcendentals=0) if flops else None,
        compiler_params=pltpu.CompilerParams(vmem_limit_bytes=36 * 2**20),
    )(*args)


def on_device(counts):
    sz = Sizes(*counts.shape)
    x, y, t = counts.shape
    l1, l2, l3 = sz.lx
    p1, p2, p3 = sz.py
    matrices = [time_matrix(t, t), time_matrix(t // 2, LANES), time_matrix(t // 4, LANES)]
    f = jnp.asarray(pack_matrices(*matrices))
    i = jnp.asarray(pack_matrices(*[m.T for m in matrices]))

    def f32(*shapes):
        return [pltpu.VMEM(s, jnp.float32) for s in shapes]

    parts = [pltpu.VMEM((2, n, n), jnp.bfloat16) for n in (t, LANES, LANES)]
    u = f32((x + 4, y, t))
    sems = [pltpu.SemaphoreType.DMA((x // 8 + 1,))]
    fw = f32((l1, 2, y, t), (l1, 2, 2, sz.zrows[0], LANES), (l2, 2, p1, LANES), (l2, 2, sz.zrows[1], LANES),
             (l3, 2, p2, LANES), (l3, 2, sz.zrows[2], LANES))
    ta1 = f32((l1, 4, p1 + 8, LANES))
    bw = ta1 + f32((2, l2, 2, p2 + 8, LANES), (l3, 2, p2, LANES), (l3, 2, p2, LANES), (l2, 2, p1 + 8, LANES),
                   (l2, 2, p1, LANES), (l1, y, LANES), (l1, y, t), (2, 2, y, LANES))
    to_prev, to_next = (sz.xp, LANES), (sz.xn, LANES)
    y_prev, y_next = (sz.yp, LANES), (sz.yn, LANES)
    halves = [(l1, y, LANES), (l1, y, t)]
    inner = parts + ta1 + f32((l1, 2, y, LANES))
    work = 6 * l1 * y * t * t

    def exchange(g, mp, mn):
        rn, rp = shifted(mp, "gy", -1), shifted(mn, "gy", 1)
        *g, mp, mn = call(edge_kernel, sz, sz.g + [to_prev, to_next], [], {0: 0, 1: 1, 2: 2}, *g, rn, rp)
        return g, shifted(mp, "gx", -1), shifted(mn, "gx", 1)

    weight, *g, mp, mn = call(first_kernel, sz, [(x, y, t)] + sz.g + [y_prev, y_next],
                              [pltpu.VMEM((x, y, t), jnp.int32)] + f32(f.shape) + parts + u + sems + fw,
                              {}, counts, f, ins_hbm=(0, 1))
    g, rn, rp = exchange(g, mp, mn)
    kept = call(inner_first_kernel, sz, halves, inner, {}, g[0], i, flops=work)
    same = {k: k for k in range(5)}
    *rest, mp, mn = call(middle_kernel, sz, sz.g + halves + sz.g + [y_prev, y_next], u + parts + parts + bw + fw, same,
                         *g, *kept, rn, rp, weight, f, i)
    g, q = rest[:3], rest[5:]
    q, rn, rp = exchange(q, mp, mn)
    kept = call(inner_last_kernel, sz, halves, inner, {}, g[0], q[0], i, flops=work)
    return call(last_kernel, sz, sz.g + halves + [(x, y, t)], f32((x, y, t)) + sems + parts + bw, same,
                *q, *kept, rn, rp, *g, i, outs_hbm=(5,))[5]


def solution(mesh):
    spec = P(("grp", "gx"), "gy", None)
    return jax.shard_map(on_device, mesh=mesh, in_specs=(spec,), out_specs=spec, check_vma=False)
```

```python
import functools
import math

import jax
import jax.numpy as jnp
from jax import lax
from jax.experimental import pallas as pl
from jax.experimental.pallas import tpu as pltpu
from jax.sharding import PartitionSpec as P

R3 = math.sqrt(3.0)
H0 = (1.0 + R3) / (4.0 * math.sqrt(2.0))
RHO = (1.0 - R3) / (1.0 + R3)
LOW_TAPS = [H0 * t for t in (1.0, R3, -R3 * RHO, RHO)]
HIGH_TAPS = [LOW_TAPS[3], -LOW_TAPS[2], LOW_TAPS[1], -LOW_TAPS[0]]
KAPPA = -R3 * (1.0 + RHO * RHO)
THRESHOLD = 0.1
LANES = 128


def shifted(x, axis, by):
    count = lax.axis_size(axis)
    return lax.ppermute(x, axis, [(i, (i + by) % count) for i in range(count)])


def time_matrix(length, width, transposed):
    half = length // 2
    row = lax.broadcasted_iota(jnp.int32, (width, width), 1 if transposed else 0)
    col = lax.broadcasted_iota(jnp.int32, (width, width), 0 if transposed else 1)
    is_low = col < half
    offset = lax.rem(row - 2 * jnp.where(is_low, col, col - half) + 2 * length, jnp.int32(length))
    value = jnp.zeros((width, width), jnp.float32)
    for j in range(4):
        tap = jnp.where(is_low, jnp.float32(LOW_TAPS[j] * H0 * H0), jnp.float32(HIGH_TAPS[j] * H0 * H0))
        value = jnp.where(offset == j, tap, value)
    return value if length == width else jnp.where((row < length) & (col < length), value, 0.0)


def split(x):
    high = x.astype(jnp.bfloat16)
    return high, (x - high.astype(jnp.float32)).astype(jnp.bfloat16)


def dot_parts(x, m_ref):
    high, low = split(x)
    dot = functools.partial(jnp.dot, preferred_element_type=jnp.float32)
    return dot(high, m_ref[0]) + (dot(low, m_ref[0]) + dot(high, m_ref[1]))


def ceil8(n):
    return (n + 7) // 8 * 8


class Sizes:
    def __init__(self, x, y, t):
        self.x, self.y, self.t = x, y, t
        self.lx = [x // 2 + 1, x // 4 + 2, x // 8 + 2]
        self.ly = [y // 2 + 1, y // 4 + 2, y // 8 + 2]
        self.py = [ceil8(n) for n in self.ly]
        p1, p2, p3 = self.py
        self.g = [(self.lx[0], 2, p1, LANES), (self.lx[0], 3, 2, p1, LANES), (self.lx[1], 2, 2, p2, LANES),
                  (self.lx[2], 2, 2, p3, LANES)]
        self.zin = [y, p1, p2]
        self.zbase = [6, 5, 6]
        self.zrows = [ceil8(2 * (p - 1) + 4 + b) for p, b in zip(self.py, self.zbase)]
        self.main = [y // 2, y // 4, y // 8]
        self.xp_pieces = [4, 4, 3]
        self.xn_pieces = [4, 6, 3]
        self.xp = self.x_rows(self.xp_pieces)
        self.xn = self.x_rows(self.xn_pieces)
        n1, n2, n3 = self.lx[0] * 4, self.lx[1] * 2, self.lx[2] * 2
        self.yp = ceil8(n1 + 2 * n2 + 3 * n3)
        self.yn = ceil8(n1 + 3 * n2 + 3 * n3)


    def x_rows(self, pieces):
        return ceil8(sum(n * w for n, w in zip(pieces, self.ly)))

    def x_offsets(self, pieces):
        at = 0
        mains, extras = [], []
        for n, m in zip(pieces, self.main):
            mains.append([at + i * m for i in range(n)])
            at += n * m
        for n, m, w in zip(pieces, self.main, self.ly):
            extras.append([at + i * (w - m) for i in range(n)])
            at += n * (w - m)
        return [list(zip(a, b)) for a, b in zip(mains, extras)]


def lattice(v0, v1, v2, v3):
    a = v0 + R3 * v1
    b = v3 - R3 * v2
    return a + RHO * b, RHO * a - b


def lattice_t(low_next, high_next, low_here, high_here):
    a = low_next + RHO * high_next
    b = RHO * low_here - high_here
    return a - R3 * b, R3 * a + b


def x_lattice_static(rows, shape):
    v = [jnp.zeros(shape, jnp.float32) if r is None else r for r in rows]
    return lattice(*v)


class Bands:
    def __init__(self, ga, gb, g2, g3):
        self.ga, self.gb, self.g2, self.g3 = ga, gb, g2, g3

    def at(self, level, s, xb, q):
        if level == 1:
            return self.g2.at[s, xb, q]
        if level == 2:
            return self.g3.at[s, xb, q]
        pair, yb = 2 * xb + q % 2, q // 2
        return self.ga.at[s, yb] if pair == 0 else self.gb.at[s, pair - 1, yb]


def y_analysis(z_ref, base, count, low_ref, high_ref):
    v = [z_ref[pl.ds(base + j, count, stride=2), :] for j in range(4)]
    low, high = lattice(*v)
    low_ref[...] = low
    high_ref[...] = high


def u_rows(u, x, y):
    return pl.ds(pl.multiple_of(x * y, 8), y)


def x_lattice_rows(u, h, s, y):
    return lattice(*[u[h, u_rows(u, 2 * s + j, y), :] for j in range(4)])


def pad_z(z, index, lo, hi, total):
    z[index + (slice(0, lo), slice(None))] = jnp.zeros((lo, LANES), jnp.float32)
    if hi < total:
        z[index + (slice(hi, total), slice(None))] = jnp.zeros((total - hi, LANES), jnp.float32)


def forward_coarse(sz, u, f1, f2, f3, g, zh, mp, mn, a1, z1, a2, z2, a3, z3):
    x, y, t = sz.x, sz.y, sz.t
    l1 = sz.lx[0]

    def rows_x(s, carry):
        for h in range(2):
            a1[h, s] = x_lattice_rows(u, h, s, y)[0]
        return carry

    lax.fori_loop(0, l1, rows_x, 0)

    step = 9
    for s0 in range(0, l1, step):
        n = min(step, l1 - s0)
        out = dot_parts(jnp.concatenate([a1[0, s0 : s0 + n], a1[1, s0 : s0 + n]], axis=-1).reshape(n * y, t), f1)
        out = out.reshape(n, y, t)
        z1[s0 : s0 + n, 8 : 8 + y, :] = out[..., :LANES]
        zh[s0 : s0 + n, 8 : 8 + y, :] = out[..., LANES:]

    def cols_1(s, carry):
        pad_z(z1, (s,), 8, 8 + y, sz.zrows[0])
        y_analysis(z1.at[s], sz.zbase[0], sz.py[0], g.at(0, s, 0, 0), g.at(0, s, 0, 2))
        return carry

    lax.fori_loop(0, l1, cols_1, 0)

    def column(h, j, col):
        return u[h, pl.ds(j * y + col, l1, stride=2 * y), :]

    edges = []
    for c0, c1, w0, w1 in ((0, 1, R3, -1.0), (y - 2, y - 1, 1.0, R3)):
        halves = [lattice(*[w0 * column(h, j, c0) + w1 * column(h, j, c1) for j in range(4)]) for h in range(2)]
        pad = jnp.zeros((ceil8(l1) - l1, t), jnp.float32)
        for xb in range(2):
            edges += [jnp.concatenate([halves[0][xb], halves[1][xb]], axis=-1), pad]
    out = dot_parts(jnp.concatenate(edges, axis=0), f1)
    for m, at in ((mp, 0), (mn, 2)):
        for tb in range(2):
            for xb in range(2):
                row = (at + xb) * ceil8(l1)
                to = (2 * tb + xb) * l1
                m[to : to + l1] = out[row : row + l1, tb * LANES : (tb + 1) * LANES]

    for level, (offset, a, z, f) in enumerate(((3, a2, z2, f2), (2, a3, z3, f3)), 1):
        rows_in, count = sz.lx[level - 1], sz.lx[level]
        p_in, p_out = sz.py[level - 1], sz.py[level]
        for s in range(count):
            picks = [2 * s + j - offset for j in range(4)]
            rows = [g.at(level - 1, i, 0, 0)[...] if 0 <= i < rows_in else None for i in picks]
            low, high = x_lattice_static(rows, (p_in, LANES))
            a[s, 0] = low
            a[s, 1] = high
        out = dot_parts(a[...].reshape(count * 2 * p_in, LANES), f)
        z[:, :, 8 : 8 + p_in, :] = out.reshape(count, 2, p_in, LANES)
        for s in range(count):
            for xb in range(2):
                pad_z(z, (s, xb), 8, 8 + p_in, sz.zrows[level])
                y_analysis(z.at[s, xb], sz.zbase[level], p_out, g.at(level, s, xb, 0), g.at(level, s, xb, 1))
    pack_y(sz, g, mp, mn)


def forward_fine_kernel(sz, u, zh, f1, gb, zl, a1, z1):
    x, y, t = sz.x, sz.y, sz.t
    l1 = sz.lx[0]

    def rows_x(s, carry):
        for h in range(2):
            a1[h, s] = x_lattice_rows(u, h, s, y)[1]
        return carry

    lax.fori_loop(0, l1, rows_x, 0)

    step = 9
    for s0 in range(0, l1, step):
        n = min(step, l1 - s0)
        out = dot_parts(jnp.concatenate([a1[0, s0 : s0 + n], a1[1, s0 : s0 + n]], axis=-1).reshape(n * y, t), f1)
        out = out.reshape(n, y, t)
        z1[s0 : s0 + n, 0, 8 : 8 + y, :] = out[..., :LANES]
        z1[s0 : s0 + n, 1, 8 : 8 + y, :] = out[..., LANES:]

    def cols_1(s, carry):
        zl[8 : 8 + y] = zh[s, 8 : 8 + y, :]
        y_analysis(zl, sz.zbase[0], sz.py[0], gb.at[s, 0, 0], gb.at[s, 0, 1])
        for tb in range(2):
            pad_z(z1, (s, tb), 8, 8 + y, sz.zrows[0])
            y_analysis(z1.at[s, tb], sz.zbase[0], sz.py[0], gb.at[s, 1 + tb, 0], gb.at[s, 1 + tb, 1])
        return carry

    pad_z(zl, (), 8, 8 + y, sz.zrows[0])
    lax.fori_loop(0, l1, cols_1, 0)


def pack_x(sz, g, mp, mn):
    l1, l2, l3 = sz.lx
    lower = lane_below(LANES // 2, (1, LANES))

    def put(ref, pieces, level, items):
        m, w = sz.main[level], sz.ly[level]
        for (main, extra), item in zip(sz.x_offsets(pieces)[level], items):
            for at, lo, hi in ((main, 0, m), (extra, m, w)):
                value = item[0][lo:hi]
                if level == 2:
                    value = jnp.where(lower, value, pltpu.roll(item[1][lo:hi], LANES // 2, 1))
                ref[at : at + hi - lo] = value

    put(mp, sz.xp_pieces, 0, [[g.at(0, 0, 1, q)] for q in range(4)])
    put(mn, sz.xn_pieces, 0, [[g.at(0, l1 - 1, 0, q)] for q in range(4)])
    put(mp, sz.xp_pieces, 1, [[g.at(1, s, 1, q)] for s in (0, 1) for q in (0, 1)])
    put(mn, sz.xn_pieces, 1, [[g.at(1, s, b, q)] for s, b in ((l2 - 2, 0), (l2 - 2, 1), (l2 - 1, 0)) for q in (0, 1)])
    put(mp, sz.xp_pieces, 2, [[g.at(2, s, b, q) for q in (0, 1)] for s, b in ((0, 1), (1, 0), (1, 1))])
    put(mn, sz.xn_pieces, 2, [[g.at(2, s, b, q) for q in (0, 1)] for s, b in ((l3 - 2, 0), (l3 - 2, 1), (l3 - 1, 0))])


def fix_x(sz, g, rn, rp):
    l1, l2, l3 = sz.lx
    lower = lane_below(LANES // 2, (1, LANES))

    def take(ref, pieces, level, lo, hi):
        part = 0 if lo == 0 else 1
        return [ref[at[part] : at[part] + hi - lo] for at in sz.x_offsets(pieces)[level]]

    def halves(value):
        return [jnp.where(lower, v, 0.0) for v in (value, pltpu.roll(value, LANES // 2, 1))]

    for level in range(3):
        m, w = sz.main[level], sz.ly[level]
        for lo, hi in ((0, m), (m, w)):
            n = take(rn, sz.xp_pieces, level, lo, hi)
            p = take(rp, sz.xn_pieces, level, lo, hi)

            def add(s, xb, q, value):
                g.at(level, s, xb, q)[lo:hi] += value

            if level == 0:
                for q in range(4):
                    add(l1 - 1, 0, q, -RHO * n[q])
                    add(l1 - 1, 1, q, n[q])
                    add(0, 0, q, p[q])
                    add(0, 1, q, RHO * p[q])
            elif level == 1:
                for q in range(2):
                    h0, h1 = n[q], n[2 + q]
                    add(l2 - 2, 0, q, -RHO * h0)
                    add(l2 - 2, 1, q, h0)
                    add(l2 - 1, 0, q, KAPPA * h0 - RHO * h1)
                    add(l2 - 1, 1, q, h1)
                    add(0, 0, q, p[q])
                    add(0, 1, q, p[2 + q])
                    add(1, 0, q, p[4 + q])
                    add(1, 1, q, RHO * p[4 + q])
            else:
                n, p = [halves(v) for v in n], [halves(v) for v in p]
                for q in range(2):
                    add(l3 - 2, 0, q, -RHO * n[0][q])
                    add(l3 - 2, 1, q, n[0][q])
                    add(l3 - 1, 0, q, n[1][q])
                    add(l3 - 1, 1, q, n[2][q])
                    add(0, 0, q, p[0][q])
                    add(0, 1, q, p[1][q])
                    add(1, 0, q, p[2][q])
                    add(1, 1, q, RHO * p[2][q])


def pack_y(sz, g, mp, mn):
    k1, k2, k3 = sz.ly
    at_p = at_n = 4 * sz.lx[0]
    for s in range(sz.lx[1]):
        for xb in range(2):
            mp[at_p : at_p + 2] = g.at(1, s, xb, 1)[0:2]
            mn[at_n : at_n + 2] = g.at(1, s, xb, 0)[k2 - 2 : k2]
            mn[at_n + 2 : at_n + 3] = g.at(1, s, xb, 1)[k2 - 2 : k2 - 1]
            at_p += 2
            at_n += 3
    for s in range(sz.lx[2]):
        for xb in range(2):
            mp[at_p : at_p + 2] = g.at(2, s, xb, 1)[0:2]
            mp[at_p + 2 : at_p + 3] = g.at(2, s, xb, 0)[1:2]
            mn[at_n : at_n + 2] = g.at(2, s, xb, 0)[k3 - 2 : k3]
            mn[at_n + 2 : at_n + 3] = g.at(2, s, xb, 1)[k3 - 2 : k3 - 1]
            at_p += 3
            at_n += 3
    if at_p < sz.yp:
        mp[at_p:] = jnp.zeros((sz.yp - at_p, LANES), jnp.float32)
    if at_n < sz.yn:
        mn[at_n:] = jnp.zeros((sz.yn - at_n, LANES), jnp.float32)


def fix_y_fine(sz, g, rn, rp, rows):
    last = sz.ly[0] - 1
    for s in rows:
        for xb in range(2):
            for tb in range(2):
                at = (2 * tb + xb) * sz.lx[0] + s
                high, low = rn[at : at + 1], rp[at : at + 1]
                g.at(0, s, xb, tb)[last : last + 1] += -RHO * high
                g.at(0, s, xb, 2 + tb)[last : last + 1] += high
                g.at(0, s, xb, tb)[0:1] += low
                g.at(0, s, xb, 2 + tb)[0:1] += RHO * low


def fix_y_coarse(sz, g, rn, rp):
    k1, k2, k3 = sz.ly
    at_p = at_n = 4 * sz.lx[0]

    for level in (1, 2):
        k = sz.ly[level]
        for s in range(sz.lx[level]):
            for xb in range(2):

                def add(q, row, value):
                    g.at(level, s, xb, q)[row : row + 1] += value

                h0, h1 = rn[at_n : at_n + 1], rn[at_n + 1 : at_n + 2]
                if level == 1:
                    l1 = KAPPA * h0 - RHO * h1
                    at_n += 2
                else:
                    l1 = rn[at_n + 2 : at_n + 3]
                    at_n += 3
                add(0, k - 2, -RHO * h0)
                add(1, k - 2, h0)
                add(0, k - 1, l1)
                add(1, k - 1, h1)
                w0, w2, w1 = (rp[at_p + i : at_p + i + 1] for i in range(3))
                add(0, 0, w0)
                add(1, 0, w1)
                add(0, 1, w2)
                add(1, 1, RHO * w2)
                at_p += 3


def shrink(v):
    return v - jnp.clip(v, -THRESHOLD, THRESHOLD)


def y_synthesis(low, high, count, t_ref, v_ref, index, start):
    a = low + RHO * high
    b = RHO * low - high
    t_ref[...] = a
    a = t_ref[1 : 1 + count]
    b = b[:count]
    v_ref[index + (pl.ds(start, count, stride=2), slice(None))] = a - R3 * b
    v_ref[index + (pl.ds(start + 1, count, stride=2), slice(None))] = R3 * a + b


def lane_below(limit, shape):
    return lax.broadcasted_iota(jnp.int32, shape, 1) < limit


def level_1_columns(sz, details, s, xb, tb, coarse, ta, v1, index):
    low = coarse if coarse is not None else details(0, s, xb, tb, None)
    high = details(0, s, xb, 2 + tb, None)
    y_synthesis(low, high, sz.y // 2, ta.at[s, xb * 2 + tb, 0 : sz.py[0]], v1, index, 0)


def times_back(sz, v_low, v_high, i1):
    v = jnp.concatenate([v_low, v_high], axis=-1)
    return dot_parts(v.reshape(-1, sz.t), i1).reshape(v.shape)


def inner_inverse(sz, details, i1, va, ba, ta, v1):
    l1 = sz.lx[0]

    def rows(s, carry):
        level_1_columns(sz, details, s, 0, 1, None, ta, va, (s,))
        level_1_columns(sz, details, s, 1, 0, None, ta, v1, (s, 0))
        level_1_columns(sz, details, s, 1, 1, None, ta, v1, (s, 1))
        return carry

    lax.fori_loop(1, l1 - 1, rows, 0)
    step = 8
    for s0 in range(1, l1 - 1, step):
        n = min(step, l1 - 1 - s0)
        ba[s0 : s0 + n] = times_back(sz, v1[s0 : s0 + n, 0], v1[s0 : s0 + n, 1], i1)


def inverse(sz, details, emit, va, ba, i1, i2, i3, ta1, ta, v3, b3, v2, b2, v1, b1, ve):
    y, t = sz.y, sz.t
    p1, p2, p3 = sz.py
    l1, l2, l3 = sz.lx
    third = lane_below(t // 8, (p3, LANES))

    for e, s in enumerate((0, l1 - 1)):
        level_1_columns(sz, details, s, 0, 1, None, ta1, va, (s,))
        level_1_columns(sz, details, s, 1, 0, None, ta1, ve, (e, 0))
        level_1_columns(sz, details, s, 1, 1, None, ta1, ve, (e, 1))

    for s in range(l3):
        for xb in range(2):
            low = details(2, s, xb, 0, third if xb == 0 else None)
            high = details(2, s, xb, 1, None)
            y_synthesis(low, high, sz.ly[1] // 2, ta.at[1, s, xb, 0:p3], v3, (s, xb), 0)
    b3[...] = dot_parts(v3[...].reshape(l3 * 2 * p2, LANES), i3).reshape(l3, 2, p2, LANES)

    second = lane_below(t // 4, (p2, LANES))
    for p in range(l2 // 2):
        even, odd = lattice_t(b3[p + 1, 0], b3[p + 1, 1], b3[p, 0], b3[p, 1])
        for s, coarse in ((2 * p, even), (2 * p + 1, odd)):
            for xb in range(2):
                low = details(1, s, xb, 0, None)
                if xb == 0:
                    low = jnp.where(second, coarse, low)
                high = details(1, s, xb, 1, None)
                y_synthesis(low, high, (sz.ly[0] + 1) // 2, ta.at[0, s, xb, 0:p2], v2, (s, xb), 7)
    b2[...] = dot_parts(v2[:, :, 8 : 8 + p1, :].reshape(l2 * 2 * p1, LANES), i2).reshape(l2, 2, p1, LANES)

    edge = times_back(sz, ve[:, 0], ve[:, 1], i1)
    ba[0] = edge[0]
    ba[l1 - 1] = edge[1]

    def coarse_rows(p):
        return lattice_t(b2[p + 1, 0], b2[p + 1, 1], b2[p, 0], b2[p, 1])

    level_1_columns(sz, details, 0, 0, 0, coarse_rows(0)[1], ta1, v1, (0,))

    def pair_1(p, carry):
        even, odd = coarse_rows(p)
        level_1_columns(sz, details, 2 * p - 1, 0, 0, even, ta1, v1, (2 * p - 1,))
        level_1_columns(sz, details, 2 * p, 0, 0, odd, ta1, v1, (2 * p,))
        return carry

    lax.fori_loop(1, l2 - 1, pair_1, 0)

    step = 9
    for s0 in range(0, l1, step):
        n = min(step, l1 - s0)
        b1[s0 : s0 + n] = times_back(sz, v1[s0 : s0 + n], va[s0 : s0 + n], i1)

    def rows_x(p, carry):
        even, odd = lattice_t(b1[p + 1], ba[p + 1], b1[p], ba[p])
        emit(p, even, odd)
        return carry

    return rows_x


def border(sz, u):
    zeros = jnp.zeros((2 * sz.y, LANES), jnp.float32)
    for h in range(2):
        u[h, 0 : 2 * sz.y, :] = zeros
        u[h, (sz.x + 2) * sz.y :, :] = zeros


def store_u(sz, u, x, value):
    for h in range(2):
        u[h, u_rows(u, x + 2, sz.y), :] = value[:, h * LANES : (h + 1) * LANES]


def first_kernel(sz, c, w_ref, ga, g2, g3, mp, mn, u, zh, f1, f2, f3, i1, i2, i3, *scratch):
    border(sz, u)
    for level, (f, i) in enumerate(((f1, i1), (f2, i2), (f3, i3))):
        for m, transposed in ((f, False), (i, True)):
            m[0], m[1] = split(time_matrix(sz.t >> level, m.shape[1], transposed))

    def rows(x, carry):
        value = c[x].astype(jnp.float32) * (1.0 / 64.0)
        weight = 1.0 / (1.0 + jnp.abs(value))
        w_ref[x] = weight
        store_u(sz, u, x, weight * value)
        return carry

    lax.fori_loop(0, sz.x, rows, 0)
    forward_coarse(sz, u, f1, f2, f3, Bands(ga, None, g2, g3), zh, mp, mn, *scratch)


def edge_kernel(sz, gai, gbi, g2i, g3i, rn, rp, ga, gb, g2, g3, mp, mn):
    g = Bands(ga, gb, g2, g3)
    fix_y_coarse(sz, g, rn, rp)
    fix_y_fine(sz, g, rn, rp, (0, sz.lx[0] - 1))
    pack_x(sz, g, mp, mn)


def first_details(g):
    def details(level, s, xb, q, approx_lanes):
        value = g.at(level, s, xb, q)[...]
        small = shrink(value)
        return small if approx_lanes is None else jnp.where(approx_lanes, value, small)

    return details


def second_details(g, q_bands):
    def details(level, s, xb, q, approx_lanes):
        first = g.at(level, s, xb, q)[...]
        second = q_bands.at(level, s, xb, q)[...]
        small = shrink(shrink(first) + (first - second))
        if approx_lanes is None:
            return small
        return jnp.where(approx_lanes, first + (first - second), small)

    return details


def inner_first_kernel(sz, gai, gbi, rn, rp, i1, ga, gb, va, ba, ta, v1):
    g = Bands(ga, gb, None, None)
    fix_y_fine(sz, g, rn, rp, range(1, sz.lx[0] - 1))
    inner_inverse(sz, first_details(g), i1, va, ba, ta, v1)


def inner_last_kernel(sz, qai, qbi, rn, rp, i1, ga, gb, qa, qb, va, ba, ta, v1):
    q = Bands(qa, qb, None, None)
    fix_y_fine(sz, q, rn, rp, range(1, sz.lx[0] - 1))
    inner_inverse(sz, second_details(Bands(ga, gb, None, None), q), i1, va, ba, ta, v1)


def middle_kernel(sz, gai, gbi, g2i, g3i, vai, bai, rn, rp, w_ref, f1, f2, f3, i1, i2, i3,
                  ga, gb, g2, g3, va, ba, qa, q2, q3, mp, mn, u, zh, ta1, ta, v3, b3, v2, b2, v1, b1, ve, *scratch):
    g = Bands(ga, gb, g2, g3)
    fix_x(sz, g, rn, rp)
    border(sz, u)

    def emit(p, even, odd):
        store_u(sz, u, 2 * p, w_ref[2 * p] * even)
        store_u(sz, u, 2 * p + 1, w_ref[2 * p + 1] * odd)

    rows = inverse(sz, first_details(g), emit, va, ba, i1, i2, i3, ta1, ta, v3, b3, v2, b2, v1, b1, ve)
    lax.fori_loop(0, sz.x // 2, rows, 0)
    forward_coarse(sz, u, f1, f2, f3, Bands(qa, None, q2, q3), zh, mp, mn, *scratch)


def last_kernel(sz, qai, qbi, q2i, q3i, vai, bai, rn, rp, ga, gb, g2, g3, i1, i2, i3,
                qa, qb, q2, q3, va, ba, out_hbm, out, sems, ta1, ta, v3, b3, v2, b2, v1, b1, ve):
    q = Bands(qa, qb, q2, q3)
    fix_x(sz, q, rn, rp)

    def emit(p, even, odd):
        out[2 * p] = even
        out[2 * p + 1] = odd

    details = second_details(Bands(ga, gb, g2, g3), q)
    rows = inverse(sz, details, emit, va, ba, i1, i2, i3, ta1, ta, v3, b3, v2, b2, v1, b1, ve)
    step = 8
    copies = []
    for i, x0 in enumerate(range(0, sz.x, step)):
        lax.fori_loop(x0 // 2, (x0 + step) // 2, rows, 0)
        copies.append(pltpu.make_async_copy(out.at[x0 : x0 + step], out_hbm.at[x0 : x0 + step], sems.at[i]))
        copies[-1].start()
    for copy in copies:
        copy.wait()


VMEM = pltpu.MemorySpace.VMEM
HBM = pltpu.MemorySpace.HBM


def call(kernel, sz, outs, scratch, aliases, *args, outs_hbm=(), flops=0):
    def specs(n, in_hbm):
        return [pl.BlockSpec(memory_space=HBM if k in in_hbm else VMEM) for k in range(n)]

    outs = [s if isinstance(s, jax.ShapeDtypeStruct) else jax.ShapeDtypeStruct(s, jnp.float32) for s in outs]
    return pl.pallas_call(
        functools.partial(kernel, sz),
        out_shape=outs,
        in_specs=specs(len(args), ()),
        out_specs=specs(len(outs), outs_hbm),
        scratch_shapes=scratch,
        input_output_aliases=aliases,
        cost_estimate=pl.CostEstimate(flops=flops, bytes_accessed=flops // 100, transcendentals=0) if flops else None,
        compiler_params=pltpu.CompilerParams(vmem_limit_bytes=36 * 2**20),
    )(*args)


def on_device(counts):
    sz = Sizes(*counts.shape)
    x, y, t = counts.shape
    l1, l2, l3 = sz.lx
    p1, p2, p3 = sz.py

    def f32(*shapes):
        return [pltpu.VMEM(s, jnp.float32) for s in shapes]

    parts = [jax.ShapeDtypeStruct((2, n, n), jnp.bfloat16) for n in (t, LANES, LANES)]
    u, zh = (2, (x + 4) * y, LANES), (l1, sz.zrows[0], LANES)
    sems = [pltpu.SemaphoreType.DMA((x // 8,))]
    fw = f32((2, l1, y, LANES), (l1, sz.zrows[0], LANES), (l2, 2, p1, LANES), (l2, 2, sz.zrows[1], LANES),
             (l3, 2, p2, LANES), (l3, 2, sz.zrows[2], LANES))
    fine = f32((sz.zrows[0], LANES), (2, l1, y, LANES), (l1, 2, sz.zrows[0], LANES))
    ta1 = f32((l1, 4, p1 + 8, LANES))
    bw = ta1 + f32((2, l2, 2, p2 + 8, LANES), (l3, 2, p2, LANES), (l3, 2, p2, LANES), (l2, 2, p1 + 8, LANES),
                   (l2, 2, p1, LANES), (l1, y, LANES), (l1, y, t), (2, 2, y, LANES))
    to_prev, to_next = (sz.xp, LANES), (sz.xn, LANES)
    messages = [(sz.yp, LANES), (sz.yn, LANES)]
    halves = [(l1, y, LANES), (l1, y, t)]
    inner = ta1 + f32((l1, 2, y, LANES))
    work = 6 * l1 * y * t * t
    ga, gb, g2, g3 = sz.g

    def exchange(ga, g2, g3, mp, mn, u, zh, f1):
        rn, rp = shifted(mp, "gy", -1), shifted(mn, "gy", 1)
        (gb,) = call(forward_fine_kernel, sz, [sz.g[1]], fine, {}, u, zh, f1, flops=work)
        *g, mp, mn = call(edge_kernel, sz, sz.g + [to_prev, to_next], [], {k: k for k in range(4)},
                          ga, gb, g2, g3, rn, rp)
        return g, (rn, rp), shifted(mp, "gx", -1), shifted(mn, "gx", 1)

    weight, *rest = call(first_kernel, sz, [(x, y, t), ga, g2, g3] + messages + [u, zh] + parts + parts,
                         fw, {}, counts)
    g_a, g_2, g_3, mp, mn, *rest = rest
    f, i = rest[2:5], rest[5:8]
    g, ry, rn, rp = exchange(g_a, g_2, g_3, mp, mn, *rest[:3])
    *kept, va, ba = call(inner_first_kernel, sz, [ga, gb] + halves, inner, {0: 0, 1: 1}, g[0], g[1], *ry, i[0], flops=work)
    same = {k: k for k in range(6)}
    *rest, q_a, q_2, q_3, mp, mn, u_, zh_ = call(
        middle_kernel, sz, sz.g + halves + [ga, g2, g3] + messages + [u, zh], bw + fw, same,
        *kept, g[2], g[3], va, ba, rn, rp, weight, *f, *i)
    g = rest[:4]
    q, ry, rn, rp = exchange(q_a, q_2, q_3, mp, mn, u_, zh_, f[0])
    *kept, va, ba = call(inner_last_kernel, sz, [ga, gb] + halves, inner, {0: 0, 1: 1}, q[0], q[1], *ry, i[0], g[0], g[1],
                         flops=work)
    return call(last_kernel, sz, sz.g + halves + [(x, y, t)], f32((x, y, t)) + sems + bw, same,
                *kept, q[2], q[3], va, ba, rn, rp, *g, *i, outs_hbm=(6,))[6]


def solution(mesh):
    spec = P(("grp", "gx"), "gy", None)
    return jax.shard_map(on_device, mesh=mesh, in_specs=(spec,), out_specs=spec, check_vma=False)
```

```python
import functools
import math

import jax
import jax.numpy as jnp
from jax import lax
from jax.experimental import pallas as pl
from jax.experimental.pallas import tpu as pltpu
from jax.sharding import PartitionSpec as P

R3 = math.sqrt(3.0)
H0 = (1.0 + R3) / (4.0 * math.sqrt(2.0))
RHO = (1.0 - R3) / (1.0 + R3)
LOW_TAPS = [H0 * t for t in (1.0, R3, -R3 * RHO, RHO)]
HIGH_TAPS = [LOW_TAPS[3], -LOW_TAPS[2], LOW_TAPS[1], -LOW_TAPS[0]]
KAPPA = -R3 * (1.0 + RHO * RHO)
THRESHOLD = 0.1
LANES = 128


def shifted(x, axis, by):
    count = lax.axis_size(axis)
    return lax.ppermute(x, axis, [(i, (i + by) % count) for i in range(count)])


def time_matrix(length, width, transposed):
    half = length // 2
    row = lax.broadcasted_iota(jnp.int32, (width, width), 1 if transposed else 0)
    col = lax.broadcasted_iota(jnp.int32, (width, width), 0 if transposed else 1)
    is_low = col < half
    offset = lax.rem(row - 2 * jnp.where(is_low, col, col - half) + 2 * length, jnp.int32(length))
    value = jnp.zeros((width, width), jnp.float32)
    for j in range(4):
        tap = jnp.where(is_low, jnp.float32(LOW_TAPS[j] * H0 * H0), jnp.float32(HIGH_TAPS[j] * H0 * H0))
        value = jnp.where(offset == j, tap, value)
    return value if length == width else jnp.where((row < length) & (col < length), value, 0.0)


def split(x):
    high = x.astype(jnp.bfloat16)
    return high, (x - high.astype(jnp.float32)).astype(jnp.bfloat16)


def dot_parts(x, m_ref):
    high, low = split(x)
    return jnp.dot(jnp.concatenate([high, low, high], axis=-1), m_ref[...], preferred_element_type=jnp.float32)


def each(first, end, body):
    for i in range(first, end):
        body(i)


def ceil8(n):
    return (n + 7) // 8 * 8


class Sizes:
    def __init__(self, x, y, t):
        self.x, self.y, self.t = x, y, t
        self.lx = [x // 2 + 1, x // 4 + 2, x // 8 + 2]
        self.ly = [y // 2 + 1, y // 4 + 2, y // 8 + 2]
        self.py = [ceil8(n) for n in self.ly]
        p1, p2, p3 = self.py
        self.g = [(self.lx[0], 2, p1, LANES), (self.lx[0], 3, 2, p1, LANES), (self.lx[1], 2, 2, p2, LANES),
                  (self.lx[2], 2, 2, p3, LANES)]
        self.zin = [y, p1, p2]
        self.zbase = [6, 5, 6]
        self.zrows = [ceil8(2 * (p - 1) + 4 + b) for p, b in zip(self.py, self.zbase)]
        self.main = [y // 2, y // 4, y // 8]
        self.xp_pieces = [4, 4, 3]
        self.xn_pieces = [4, 6, 3]
        self.xp = self.x_rows(self.xp_pieces)
        self.xn = self.x_rows(self.xn_pieces)
        n1, n2, n3 = self.lx[0] * 4, self.lx[1] * 2, self.lx[2] * 2
        self.yp = ceil8(n1 + 2 * n2 + 3 * n3)
        self.yn = ceil8(n1 + 3 * n2 + 3 * n3)


    def x_rows(self, pieces):
        return ceil8(sum(n * w for n, w in zip(pieces, self.ly)))

    def x_offsets(self, pieces):
        at = 0
        mains, extras = [], []
        for n, m in zip(pieces, self.main):
            mains.append([at + i * m for i in range(n)])
            at += n * m
        for n, m, w in zip(pieces, self.main, self.ly):
            extras.append([at + i * (w - m) for i in range(n)])
            at += n * (w - m)
        return [list(zip(a, b)) for a, b in zip(mains, extras)]


def lattice(v0, v1, v2, v3):
    a = v0 + R3 * v1
    b = v3 - R3 * v2
    return a + RHO * b, RHO * a - b


def lattice_t(low_next, high_next, low_here, high_here):
    a = low_next + RHO * high_next
    b = RHO * low_here - high_here
    return a - R3 * b, R3 * a + b


def x_lattice_static(rows, shape):
    v = [jnp.zeros(shape, jnp.float32) if r is None else r for r in rows]
    return lattice(*v)


class Bands:
    def __init__(self, ga, gb, g2, g3):
        self.ga, self.gb, self.g2, self.g3 = ga, gb, g2, g3

    def at(self, level, s, xb, q):
        if level == 1:
            return self.g2.at[s, xb, q]
        if level == 2:
            return self.g3.at[s, xb, q]
        pair, yb = 2 * xb + q % 2, q // 2
        return self.ga.at[s, yb] if pair == 0 else self.gb.at[s, pair - 1, yb]


def y_analysis(z_ref, base, count, low_ref, high_ref):
    v = [z_ref[pl.ds(base + j, count, stride=2), :] for j in range(4)]
    low, high = lattice(*v)
    low_ref[...] = low
    high_ref[...] = high


def u_rows(u, x, y):
    return pl.ds(x * y, y)


def x_lattice_rows(u, h, s, y):
    return lattice(*[u[h, u_rows(u, 2 * s + j, y), :] for j in range(4)])


def pad_z(z, index, lo, hi, total):
    z[index + (slice(0, lo), slice(None))] = jnp.zeros((lo, LANES), jnp.float32)
    if hi < total:
        z[index + (slice(hi, total), slice(None))] = jnp.zeros((total - hi, LANES), jnp.float32)


def forward_coarse(sz, u, f1, f2, f3, g, zh, mp, mn, a1, z1, a2, z2, a3, z3):
    x, y, t = sz.x, sz.y, sz.t
    l1 = sz.lx[0]

    def rows_x(s):
        for h in range(2):
            a1[h, s] = x_lattice_rows(u, h, s, y)[0]

    each(0, l1, rows_x)

    step = 9
    for s0 in range(0, l1, step):
        n = min(step, l1 - s0)
        out = dot_parts(jnp.concatenate([a1[0, s0 : s0 + n], a1[1, s0 : s0 + n]], axis=-1).reshape(n * y, t), f1)
        out = out.reshape(n, y, t)
        z1[s0 : s0 + n, 8 : 8 + y, :] = out[..., :LANES]
        zh[s0 : s0 + n, 8 : 8 + y, :] = out[..., LANES:]

    def cols_1(s):
        pad_z(z1, (s,), 8, 8 + y, sz.zrows[0])
        y_analysis(z1.at[s], sz.zbase[0], sz.py[0], g.at(0, s, 0, 0), g.at(0, s, 0, 2))

    each(0, l1, cols_1)

    def column(h, j, col):
        return u[h, pl.ds(j * y + col, l1, stride=2 * y), :]

    edges = []
    for c0, c1, w0, w1 in ((0, 1, R3, -1.0), (y - 2, y - 1, 1.0, R3)):
        halves = [lattice(*[w0 * column(h, j, c0) + w1 * column(h, j, c1) for j in range(4)]) for h in range(2)]
        pad = jnp.zeros((ceil8(l1) - l1, t), jnp.float32)
        for xb in range(2):
            edges += [jnp.concatenate([halves[0][xb], halves[1][xb]], axis=-1), pad]
    out = dot_parts(jnp.concatenate(edges, axis=0), f1)
    for m, at in ((mp, 0), (mn, 2)):
        for tb in range(2):
            for xb in range(2):
                row = (at + xb) * ceil8(l1)
                to = (2 * tb + xb) * l1
                m[to : to + l1] = out[row : row + l1, tb * LANES : (tb + 1) * LANES]

    for level, (offset, a, z, f) in enumerate(((3, a2, z2, f2), (2, a3, z3, f3)), 1):
        rows_in, count = sz.lx[level - 1], sz.lx[level]
        p_in, p_out = sz.py[level - 1], sz.py[level]
        for s in range(count):
            picks = [2 * s + j - offset for j in range(4)]
            rows = [g.at(level - 1, i, 0, 0)[...] if 0 <= i < rows_in else None for i in picks]
            low, high = x_lattice_static(rows, (p_in, LANES))
            a[s, 0] = low
            a[s, 1] = high
        out = dot_parts(a[...].reshape(count * 2 * p_in, LANES), f)
        z[:, :, 8 : 8 + p_in, :] = out.reshape(count, 2, p_in, LANES)
        for s in range(count):
            for xb in range(2):
                pad_z(z, (s, xb), 8, 8 + p_in, sz.zrows[level])
                y_analysis(z.at[s, xb], sz.zbase[level], p_out, g.at(level, s, xb, 0), g.at(level, s, xb, 1))
    pack_y(sz, g, mp, mn)


def forward_fine_kernel(sz, u, zh, f1, gb, zl, a1, z1):
    x, y, t = sz.x, sz.y, sz.t
    l1 = sz.lx[0]

    def rows_x(s):
        for h in range(2):
            a1[h, s] = x_lattice_rows(u, h, s, y)[1]

    each(0, l1, rows_x)

    step = 9
    for s0 in range(0, l1, step):
        n = min(step, l1 - s0)
        out = dot_parts(jnp.concatenate([a1[0, s0 : s0 + n], a1[1, s0 : s0 + n]], axis=-1).reshape(n * y, t), f1)
        out = out.reshape(n, y, t)
        z1[s0 : s0 + n, 0, 8 : 8 + y, :] = out[..., :LANES]
        z1[s0 : s0 + n, 1, 8 : 8 + y, :] = out[..., LANES:]

    def cols_1(s):
        zl[8 : 8 + y] = zh[s, 8 : 8 + y, :]
        y_analysis(zl, sz.zbase[0], sz.py[0], gb.at[s, 0, 0], gb.at[s, 0, 1])
        for tb in range(2):
            pad_z(z1, (s, tb), 8, 8 + y, sz.zrows[0])
            y_analysis(z1.at[s, tb], sz.zbase[0], sz.py[0], gb.at[s, 1 + tb, 0], gb.at[s, 1 + tb, 1])

    pad_z(zl, (), 8, 8 + y, sz.zrows[0])
    each(0, l1, cols_1)


def pack_x(sz, g, mp, mn):
    l1, l2, l3 = sz.lx
    lower = lane_below(LANES // 2, (1, LANES))

    def put(ref, pieces, level, items):
        m, w = sz.main[level], sz.ly[level]
        for (main, extra), item in zip(sz.x_offsets(pieces)[level], items):
            for at, lo, hi in ((main, 0, m), (extra, m, w)):
                value = item[0][lo:hi]
                if level == 2:
                    value = jnp.where(lower, value, pltpu.roll(item[1][lo:hi], LANES // 2, 1))
                ref[at : at + hi - lo] = value

    put(mp, sz.xp_pieces, 0, [[g.at(0, 0, 1, q)] for q in range(4)])
    put(mn, sz.xn_pieces, 0, [[g.at(0, l1 - 1, 0, q)] for q in range(4)])
    put(mp, sz.xp_pieces, 1, [[g.at(1, s, 1, q)] for s in (0, 1) for q in (0, 1)])
    put(mn, sz.xn_pieces, 1, [[g.at(1, s, b, q)] for s, b in ((l2 - 2, 0), (l2 - 2, 1), (l2 - 1, 0)) for q in (0, 1)])
    put(mp, sz.xp_pieces, 2, [[g.at(2, s, b, q) for q in (0, 1)] for s, b in ((0, 1), (1, 0), (1, 1))])
    put(mn, sz.xn_pieces, 2, [[g.at(2, s, b, q) for q in (0, 1)] for s, b in ((l3 - 2, 0), (l3 - 2, 1), (l3 - 1, 0))])


def fix_x(sz, g, rn, rp):
    l1, l2, l3 = sz.lx
    lower = lane_below(LANES // 2, (1, LANES))

    def take(ref, pieces, level, lo, hi):
        part = 0 if lo == 0 else 1
        return [ref[at[part] : at[part] + hi - lo] for at in sz.x_offsets(pieces)[level]]

    def halves(value):
        return [jnp.where(lower, v, 0.0) for v in (value, pltpu.roll(value, LANES // 2, 1))]

    for level in range(3):
        m, w = sz.main[level], sz.ly[level]
        for lo, hi in ((0, m), (m, w)):
            n = take(rn, sz.xp_pieces, level, lo, hi)
            p = take(rp, sz.xn_pieces, level, lo, hi)

            def add(s, xb, q, value):
                g.at(level, s, xb, q)[lo:hi] += value

            if level == 0:
                for q in range(4):
                    add(l1 - 1, 0, q, -RHO * n[q])
                    add(l1 - 1, 1, q, n[q])
                    add(0, 0, q, p[q])
                    add(0, 1, q, RHO * p[q])
            elif level == 1:
                for q in range(2):
                    h0, h1 = n[q], n[2 + q]
                    add(l2 - 2, 0, q, -RHO * h0)
                    add(l2 - 2, 1, q, h0)
                    add(l2 - 1, 0, q, KAPPA * h0 - RHO * h1)
                    add(l2 - 1, 1, q, h1)
                    add(0, 0, q, p[q])
                    add(0, 1, q, p[2 + q])
                    add(1, 0, q, p[4 + q])
                    add(1, 1, q, RHO * p[4 + q])
            else:
                n, p = [halves(v) for v in n], [halves(v) for v in p]
                for q in range(2):
                    add(l3 - 2, 0, q, -RHO * n[0][q])
                    add(l3 - 2, 1, q, n[0][q])
                    add(l3 - 1, 0, q, n[1][q])
                    add(l3 - 1, 1, q, n[2][q])
                    add(0, 0, q, p[0][q])
                    add(0, 1, q, p[1][q])
                    add(1, 0, q, p[2][q])
                    add(1, 1, q, RHO * p[2][q])


def pack_y(sz, g, mp, mn):
    k1, k2, k3 = sz.ly
    at_p = at_n = 4 * sz.lx[0]
    for s in range(sz.lx[1]):
        for xb in range(2):
            mp[at_p : at_p + 2] = g.at(1, s, xb, 1)[0:2]
            mn[at_n : at_n + 2] = g.at(1, s, xb, 0)[k2 - 2 : k2]
            mn[at_n + 2 : at_n + 3] = g.at(1, s, xb, 1)[k2 - 2 : k2 - 1]
            at_p += 2
            at_n += 3
    for s in range(sz.lx[2]):
        for xb in range(2):
            mp[at_p : at_p + 2] = g.at(2, s, xb, 1)[0:2]
            mp[at_p + 2 : at_p + 3] = g.at(2, s, xb, 0)[1:2]
            mn[at_n : at_n + 2] = g.at(2, s, xb, 0)[k3 - 2 : k3]
            mn[at_n + 2 : at_n + 3] = g.at(2, s, xb, 1)[k3 - 2 : k3 - 1]
            at_p += 3
            at_n += 3
    if at_p < sz.yp:
        mp[at_p:] = jnp.zeros((sz.yp - at_p, LANES), jnp.float32)
    if at_n < sz.yn:
        mn[at_n:] = jnp.zeros((sz.yn - at_n, LANES), jnp.float32)


def fix_y_fine(sz, g, rn, rp, rows):
    last = sz.ly[0] - 1
    for s in rows:
        for xb in range(2):
            for tb in range(2):
                at = (2 * tb + xb) * sz.lx[0] + s
                high, low = rn[at : at + 1], rp[at : at + 1]
                g.at(0, s, xb, tb)[last : last + 1] += -RHO * high
                g.at(0, s, xb, 2 + tb)[last : last + 1] += high
                g.at(0, s, xb, tb)[0:1] += low
                g.at(0, s, xb, 2 + tb)[0:1] += RHO * low


def fix_y_coarse(sz, g, rn, rp):
    k1, k2, k3 = sz.ly
    at_p = at_n = 4 * sz.lx[0]

    for level in (1, 2):
        k = sz.ly[level]
        for s in range(sz.lx[level]):
            for xb in range(2):

                def add(q, row, value):
                    g.at(level, s, xb, q)[row : row + 1] += value

                h0, h1 = rn[at_n : at_n + 1], rn[at_n + 1 : at_n + 2]
                if level == 1:
                    l1 = KAPPA * h0 - RHO * h1
                    at_n += 2
                else:
                    l1 = rn[at_n + 2 : at_n + 3]
                    at_n += 3
                add(0, k - 2, -RHO * h0)
                add(1, k - 2, h0)
                add(0, k - 1, l1)
                add(1, k - 1, h1)
                w0, w2, w1 = (rp[at_p + i : at_p + i + 1] for i in range(3))
                add(0, 0, w0)
                add(1, 0, w1)
                add(0, 1, w2)
                add(1, 1, RHO * w2)
                at_p += 3


def shrink(v):
    return v - jnp.clip(v, -THRESHOLD, THRESHOLD)


def y_synthesis(low, high, count, t_ref, v_ref, index, start):
    a = low + RHO * high
    b = RHO * low - high
    t_ref[...] = a
    a = t_ref[1 : 1 + count]
    b = b[:count]
    v_ref[index + (pl.ds(start, count, stride=2), slice(None))] = a - R3 * b
    v_ref[index + (pl.ds(start + 1, count, stride=2), slice(None))] = R3 * a + b


def lane_below(limit, shape):
    return lax.broadcasted_iota(jnp.int32, shape, 1) < limit


def level_1_columns(sz, details, s, xb, tb, coarse, ta, v1, index):
    low = coarse if coarse is not None else details(0, s, xb, tb, None)
    high = details(0, s, xb, 2 + tb, None)
    y_synthesis(low, high, sz.y // 2, ta.at[s, xb * 2 + tb, 0 : sz.py[0]], v1, index, 0)


def times_back(sz, v_low, v_high, i1):
    v = jnp.concatenate([v_low, v_high], axis=-1)
    return dot_parts(v.reshape(-1, sz.t), i1).reshape(v.shape)


def inner_inverse(sz, details, i1, va, ba, ta, v1):
    l1 = sz.lx[0]

    def rows(s):
        level_1_columns(sz, details, s, 0, 1, None, ta, va, (s,))
        level_1_columns(sz, details, s, 1, 0, None, ta, v1, (s, 0))
        level_1_columns(sz, details, s, 1, 1, None, ta, v1, (s, 1))

    each(1, l1 - 1, rows)
    step = 15
    for s0 in range(1, l1 - 1, step):
        n = min(step, l1 - 1 - s0)
        ba[s0 : s0 + n] = times_back(sz, v1[s0 : s0 + n, 0], v1[s0 : s0 + n, 1], i1)


def inverse(sz, details, emit, done, groups, va, ba, i1, i2, i3, ta1, ta, v3, b3, v2, b2, v1, b1, ve):
    y, t = sz.y, sz.t
    p1, p2, p3 = sz.py
    l1, l2, l3 = sz.lx
    third = lane_below(t // 8, (p3, LANES))

    for e, s in enumerate((0, l1 - 1)):
        level_1_columns(sz, details, s, 0, 1, None, ta1, va, (s,))
        level_1_columns(sz, details, s, 1, 0, None, ta1, ve, (e, 0))
        level_1_columns(sz, details, s, 1, 1, None, ta1, ve, (e, 1))

    for s in range(l3):
        for xb in range(2):
            low = details(2, s, xb, 0, third if xb == 0 else None)
            high = details(2, s, xb, 1, None)
            y_synthesis(low, high, sz.ly[1] // 2, ta.at[1, s, xb, 0:p3], v3, (s, xb), 0)
    b3[...] = dot_parts(v3[...].reshape(l3 * 2 * p2, LANES), i3).reshape(l3, 2, p2, LANES)

    second = lane_below(t // 4, (p2, LANES))
    for p in range(l2 // 2):
        even, odd = lattice_t(b3[p + 1, 0], b3[p + 1, 1], b3[p, 0], b3[p, 1])
        for s, coarse in ((2 * p, even), (2 * p + 1, odd)):
            for xb in range(2):
                low = details(1, s, xb, 0, None)
                if xb == 0:
                    low = jnp.where(second, coarse, low)
                high = details(1, s, xb, 1, None)
                y_synthesis(low, high, (sz.ly[0] + 1) // 2, ta.at[0, s, xb, 0:p2], v2, (s, xb), 7)
    b2[...] = dot_parts(v2[:, :, 8 : 8 + p1, :].reshape(l2 * 2 * p1, LANES), i2).reshape(l2, 2, p1, LANES)

    edge = times_back(sz, ve[:, 0], ve[:, 1], i1)
    ba[0] = edge[0]
    ba[l1 - 1] = edge[1]

    def coarse_rows(p):
        return lattice_t(b2[p + 1, 0], b2[p + 1, 1], b2[p, 0], b2[p, 1])

    def pair_1(p):
        even, odd = coarse_rows(p)
        level_1_columns(sz, details, 2 * p - 1, 0, 0, even, ta1, v1, (2 * p - 1,))
        level_1_columns(sz, details, 2 * p, 0, 0, odd, ta1, v1, (2 * p,))

    def rows_x(p):
        even, odd = lattice_t(b1[p + 1], ba[p + 1], b1[p], ba[p])
        emit(p, even, odd)

    level_1_columns(sz, details, 0, 0, 0, coarse_rows(0)[1], ta1, v1, (0,))
    step = sz.x // groups
    for x0 in range(0, sz.x, step):
        each(x0 // 4 + 1, (x0 + step) // 4 + 1, pair_1)
        s0, s1 = (x0 // 2 + 1 if x0 else 0), (x0 + step) // 2 + 1
        b1[s0:s1] = times_back(sz, v1[s0:s1], va[s0:s1], i1)
        each(x0 // 2, (x0 + step) // 2, rows_x)
        done(x0, step)


def border(sz, u):
    zeros = jnp.zeros((2 * sz.y, LANES), jnp.float32)
    for h in range(2):
        u[h, 0 : 2 * sz.y, :] = zeros
        u[h, (sz.x + 2) * sz.y :, :] = zeros


def store_u(sz, u, x, value):
    for h in range(2):
        u[h, u_rows(u, x + 2, sz.y), :] = value[:, h * LANES : (h + 1) * LANES]


def matrix_kernel(sz, f1, f2, f3, i1, i2, i3):
    for level, (f, i) in enumerate(((f1, i1), (f2, i2), (f3, i3))):
        for m, transposed in ((f, False), (i, True)):
            n = m.shape[1]
            high, low = split(time_matrix(sz.t >> level, n, transposed))
            m[0:n] = high
            m[n : 2 * n] = high
            m[2 * n :] = low


def first_kernel(sz, c, f1, f2, f3, w_ref, ga, g2, g3, mp, mn, u, zh, *scratch):
    border(sz, u)

    def rows(x):
        value = c[x].astype(jnp.float32) * (1.0 / 64.0)
        weight = 1.0 / (1.0 + jnp.abs(value))
        w_ref[x] = weight
        store_u(sz, u, x, weight * value)

    each(0, sz.x, rows)
    forward_coarse(sz, u, f1, f2, f3, Bands(ga, None, g2, g3), zh, mp, mn, *scratch)


def edge_kernel(sz, gai, gbi, g2i, g3i, rn, rp, ga, gb, g2, g3, mp, mn):
    g = Bands(ga, gb, g2, g3)
    fix_y_coarse(sz, g, rn, rp)
    fix_y_fine(sz, g, rn, rp, (0, sz.lx[0] - 1))
    pack_x(sz, g, mp, mn)


def first_details(g):
    def details(level, s, xb, q, approx_lanes):
        value = g.at(level, s, xb, q)[...]
        small = shrink(value)
        return small if approx_lanes is None else jnp.where(approx_lanes, value, small)

    return details


def second_details(g, q_bands):
    def details(level, s, xb, q, approx_lanes):
        first = g.at(level, s, xb, q)[...]
        second = q_bands.at(level, s, xb, q)[...]
        small = shrink(shrink(first) + (first - second))
        if approx_lanes is None:
            return small
        return jnp.where(approx_lanes, first + (first - second), small)

    return details


def inner_first_kernel(sz, gai, gbi, rn, rp, i1, ga, gb, va, ba, ta, v1):
    g = Bands(ga, gb, None, None)
    fix_y_fine(sz, g, rn, rp, range(1, sz.lx[0] - 1))
    inner_inverse(sz, first_details(g), i1, va, ba, ta, v1)


def inner_last_kernel(sz, qai, qbi, rn, rp, i1, ga, gb, qa, qb, va, ba, ta, v1):
    q = Bands(qa, qb, None, None)
    fix_y_fine(sz, q, rn, rp, range(1, sz.lx[0] - 1))
    inner_inverse(sz, second_details(Bands(ga, gb, None, None), q), i1, va, ba, ta, v1)


def middle_kernel(sz, gai, gbi, g2i, g3i, vai, bai, rn, rp, w_ref, f1, f2, f3, i1, i2, i3,
                  ga, gb, g2, g3, va, ba, qa, q2, q3, mp, mn, u, zh, ta1, ta, v3, b3, v2, b2, v1, b1, ve, *scratch):
    g = Bands(ga, gb, g2, g3)
    fix_x(sz, g, rn, rp)
    border(sz, u)

    def emit(p, even, odd):
        store_u(sz, u, 2 * p, w_ref[2 * p] * even)
        store_u(sz, u, 2 * p + 1, w_ref[2 * p + 1] * odd)

    inverse(sz, first_details(g), emit, lambda x0, n: None, 2, va, ba, i1, i2, i3, ta1, ta, v3, b3, v2, b2, v1, b1, ve)
    forward_coarse(sz, u, f1, f2, f3, Bands(qa, None, q2, q3), zh, mp, mn, *scratch)


def last_kernel(sz, qai, qbi, q2i, q3i, vai, bai, rn, rp, ga, gb, g2, g3, i1, i2, i3,
                qa, qb, q2, q3, va, ba, out_hbm, out, sems, ta1, ta, v3, b3, v2, b2, v1, b1, ve):
    q = Bands(qa, qb, q2, q3)
    fix_x(sz, q, rn, rp)

    def emit(p, even, odd):
        out[2 * p] = even
        out[2 * p + 1] = odd

    details = second_details(Bands(ga, gb, g2, g3), q)
    copies = []

    def done(x0, n):
        copies.append(pltpu.make_async_copy(out.at[x0 : x0 + n], out_hbm.at[x0 : x0 + n], sems.at[len(copies)]))
        copies[-1].start()

    inverse(sz, details, emit, done, sz.x // 4, va, ba, i1, i2, i3, ta1, ta, v3, b3, v2, b2, v1, b1, ve)
    for copy in copies:
        copy.wait()


VMEM = pltpu.MemorySpace.VMEM
HBM = pltpu.MemorySpace.HBM


def call(kernel, sz, outs, scratch, aliases, *args, outs_hbm=(), flops=0):
    def specs(n, in_hbm):
        return [pl.BlockSpec(memory_space=HBM if k in in_hbm else VMEM) for k in range(n)]

    outs = [s if isinstance(s, jax.ShapeDtypeStruct) else jax.ShapeDtypeStruct(s, jnp.float32) for s in outs]
    return pl.pallas_call(
        functools.partial(kernel, sz),
        out_shape=outs,
        in_specs=specs(len(args), ()),
        out_specs=specs(len(outs), outs_hbm),
        scratch_shapes=scratch,
        input_output_aliases=aliases,
        cost_estimate=pl.CostEstimate(flops=flops, bytes_accessed=flops // 100, transcendentals=0) if flops else None,
        compiler_params=pltpu.CompilerParams(vmem_limit_bytes=36 * 2**20),
    )(*args)


def on_device(counts):
    sz = Sizes(*counts.shape)
    x, y, t = counts.shape
    l1, l2, l3 = sz.lx
    p1, p2, p3 = sz.py

    def f32(*shapes):
        return [pltpu.VMEM(s, jnp.float32) for s in shapes]

    parts = [jax.ShapeDtypeStruct((3 * n, n), jnp.bfloat16) for n in (t, LANES, LANES)]
    u, zh = (2, (x + 4) * y, LANES), (l1, sz.zrows[0], LANES)
    sems = [pltpu.SemaphoreType.DMA((x // 4,))]
    fw = f32((2, l1, y, LANES), (l1, sz.zrows[0], LANES), (l2, 2, p1, LANES), (l2, 2, sz.zrows[1], LANES),
             (l3, 2, p2, LANES), (l3, 2, sz.zrows[2], LANES))
    fine = f32((sz.zrows[0], LANES), (2, l1, y, LANES), (l1, 2, sz.zrows[0], LANES))
    ta1 = f32((l1, 4, p1 + 8, LANES))
    bw = ta1 + f32((2, l2, 2, p2 + 8, LANES), (l3, 2, p2, LANES), (l3, 2, p2, LANES), (l2, 2, p1 + 8, LANES),
                   (l2, 2, p1, LANES), (l1, y, LANES), (l1, y, t), (2, 2, y, LANES))
    to_prev, to_next = (sz.xp, LANES), (sz.xn, LANES)
    messages = [(sz.yp, LANES), (sz.yn, LANES)]
    halves = [(l1, y, LANES), (l1, y, t)]
    inner = ta1 + f32((l1, 2, y, LANES))
    work = 6 * l1 * y * t * t
    ga, gb, g2, g3 = sz.g

    def exchange(ga, g2, g3, mp, mn, u, zh, f1):
        rn, rp = shifted(mp, "gy", -1), shifted(mn, "gy", 1)
        (gb,) = call(forward_fine_kernel, sz, [sz.g[1]], fine, {}, u, zh, f1, flops=work)
        *g, mp, mn = call(edge_kernel, sz, sz.g + [to_prev, to_next], [], {k: k for k in range(4)},
                          ga, gb, g2, g3, rn, rp)
        return g, (rn, rp), shifted(mp, "gx", -1), shifted(mn, "gx", 1)

    matrices = call(matrix_kernel, sz, parts + parts, [], {}, flops=x * y * t)
    f, i = matrices[:3], matrices[3:]
    weight, *rest = call(first_kernel, sz, [(x, y, t), ga, g2, g3] + messages + [u, zh], fw, {}, counts, *f)
    g, ry, rn, rp = exchange(*rest, f[0])
    *kept, va, ba = call(inner_first_kernel, sz, [ga, gb] + halves, inner, {0: 0, 1: 1}, g[0], g[1], *ry, i[0], flops=work)
    same = {k: k for k in range(6)}
    *rest, q_a, q_2, q_3, mp, mn, u_, zh_ = call(
        middle_kernel, sz, sz.g + halves + [ga, g2, g3] + messages + [u, zh], bw + fw, same,
        *kept, g[2], g[3], va, ba, rn, rp, weight, *f, *i)
    g = rest[:4]
    q, ry, rn, rp = exchange(q_a, q_2, q_3, mp, mn, u_, zh_, f[0])
    *kept, va, ba = call(inner_last_kernel, sz, [ga, gb] + halves, inner, {0: 0, 1: 1}, q[0], q[1], *ry, i[0], g[0], g[1],
                         flops=work)
    return call(last_kernel, sz, sz.g + halves + [(x, y, t)], f32((x, y, t)) + sems + bw, same,
                *kept, q[2], q[3], va, ba, rn, rp, *g, *i, outs_hbm=(6,))[6]


def solution(mesh):
    spec = P(("grp", "gx"), "gy", None)
    return jax.shard_map(on_device, mesh=mesh, in_specs=(spec,), out_specs=spec, check_vma=False)
```

```python
import functools
import math

import jax
import jax.numpy as jnp
from jax import lax
from jax.experimental import pallas as pl
from jax.experimental.pallas import tpu as pltpu
from jax.sharding import PartitionSpec as P

R3 = math.sqrt(3.0)
H0 = (1.0 + R3) / (4.0 * math.sqrt(2.0))
RHO = (1.0 - R3) / (1.0 + R3)
LOW_TAPS = [H0 * t for t in (1.0, R3, -R3 * RHO, RHO)]
HIGH_TAPS = [LOW_TAPS[3], -LOW_TAPS[2], LOW_TAPS[1], -LOW_TAPS[0]]
KAPPA = -R3 * (1.0 + RHO * RHO)
THRESHOLD = 0.1
LANES = 128


def shifted(x, axis, by):
    count = lax.axis_size(axis)
    return lax.ppermute(x, axis, [(i, (i + by) % count) for i in range(count)])


def time_matrix(length, width, transposed):
    half = length // 2
    row = lax.broadcasted_iota(jnp.int32, (width, width), 1 if transposed else 0)
    col = lax.broadcasted_iota(jnp.int32, (width, width), 0 if transposed else 1)
    is_low = col < half
    offset = lax.rem(row - 2 * jnp.where(is_low, col, col - half) + 2 * length, jnp.int32(length))
    value = jnp.zeros((width, width), jnp.float32)
    for j in range(4):
        tap = jnp.where(is_low, jnp.float32(LOW_TAPS[j] * H0 * H0), jnp.float32(HIGH_TAPS[j] * H0 * H0))
        value = jnp.where(offset == j, tap, value)
    return value if length == width else jnp.where((row < length) & (col < length), value, 0.0)


def split(x):
    high = x.astype(jnp.bfloat16)
    return high, (x - high.astype(jnp.float32)).astype(jnp.bfloat16)


def dot_parts(x, m_ref):
    high, low = split(x)
    return jnp.dot(jnp.concatenate([high, low, high], axis=-1), m_ref[...], preferred_element_type=jnp.float32)


def each(first, end, body):
    for i in range(first, end):
        body(i)


def ceil8(n):
    return (n + 7) // 8 * 8


class Sizes:
    def __init__(self, x, y, t):
        self.x, self.y, self.t = x, y, t
        self.lx = [x // 2 + 1, x // 4 + 2, x // 8 + 2]
        self.ly = [y // 2 + 1, y // 4 + 2, y // 8 + 2]
        self.py = [ceil8(n) for n in self.ly]
        p1, p2, p3 = self.py
        self.g = [(self.lx[0], 2, p1, LANES), (self.lx[0], 3, 2, p1, LANES), (self.lx[1], 2, 2, p2, LANES),
                  (self.lx[2], 2, 2, p3, LANES)]
        self.zin = [y, p1, p2]
        self.zbase = [6, 5, 6]
        self.zrows = [ceil8(2 * (p - 1) + 4 + b) for p, b in zip(self.py, self.zbase)]
        self.main = [y // 2, y // 4, y // 8]
        self.xp_pieces = [4, 4, 3]
        self.xn_pieces = [4, 6, 3]
        self.xp = self.x_rows(self.xp_pieces)
        self.xn = self.x_rows(self.xn_pieces)
        n1, n2, n3 = self.lx[0] * 4, self.lx[1] * 2, self.lx[2] * 2
        self.yp = ceil8(n1 + 2 * n2 + 3 * n3)
        self.yn = ceil8(n1 + 3 * n2 + 3 * n3)


    def x_rows(self, pieces):
        return ceil8(sum(n * w for n, w in zip(pieces, self.ly)))

    def x_offsets(self, pieces):
        at = 0
        mains, extras = [], []
        for n, m in zip(pieces, self.main):
            mains.append([at + i * m for i in range(n)])
            at += n * m
        for n, m, w in zip(pieces, self.main, self.ly):
            extras.append([at + i * (w - m) for i in range(n)])
            at += n * (w - m)
        return [list(zip(a, b)) for a, b in zip(mains, extras)]


def lattice(v0, v1, v2, v3):
    a = v0 + R3 * v1
    b = v3 - R3 * v2
    return a + RHO * b, RHO * a - b


def lattice_t(low_next, high_next, low_here, high_here):
    a = low_next + RHO * high_next
    b = RHO * low_here - high_here
    return a - R3 * b, R3 * a + b


def x_lattice_static(rows, shape):
    v = [jnp.zeros(shape, jnp.float32) if r is None else r for r in rows]
    return lattice(*v)


class Bands:
    def __init__(self, ga, gb, g2, g3):
        self.ga, self.gb, self.g2, self.g3 = ga, gb, g2, g3

    def at(self, level, s, xb, q):
        if level == 1:
            return self.g2.at[s, xb, q]
        if level == 2:
            return self.g3.at[s, xb, q]
        pair, yb = 2 * xb + q % 2, q // 2
        return self.ga.at[s, yb] if pair == 0 else self.gb.at[s, pair - 1, yb]


def y_analysis(z_ref, base, count, low_ref, high_ref):
    v = [z_ref[pl.ds(base + j, count, stride=2), :] for j in range(4)]
    low, high = lattice(*v)
    low_ref[...] = low
    high_ref[...] = high


def u_rows(u, x, y):
    return pl.ds(x * y, y)


def x_lattice_rows(u, h, s, y):
    return lattice(*[u[h, u_rows(u, 2 * s + j, y), :] for j in range(4)])


def pad_z(z, index, lo, hi, total):
    z[index + (slice(0, lo), slice(None))] = jnp.zeros((lo, LANES), jnp.float32)
    if hi < total:
        z[index + (slice(hi, total), slice(None))] = jnp.zeros((total - hi, LANES), jnp.float32)


def forward_coarse(sz, u, f1, f2, f3, g, zh, mp, mn, a1, z1, a2, z2, a3, z3):
    x, y, t = sz.x, sz.y, sz.t
    l1 = sz.lx[0]

    def rows_x(s):
        for h in range(2):
            a1[h, s] = x_lattice_rows(u, h, s, y)[0]

    each(0, l1, rows_x)

    step = 9
    for s0 in range(0, l1, step):
        n = min(step, l1 - s0)
        out = dot_parts(jnp.concatenate([a1[0, s0 : s0 + n], a1[1, s0 : s0 + n]], axis=-1).reshape(n * y, t), f1)
        out = out.reshape(n, y, t)
        z1[s0 : s0 + n, 8 : 8 + y, :] = out[..., :LANES]
        zh[s0 : s0 + n, 8 : 8 + y, :] = out[..., LANES:]

    def cols_1(s):
        pad_z(z1, (s,), 8, 8 + y, sz.zrows[0])
        y_analysis(z1.at[s], sz.zbase[0], sz.py[0], g.at(0, s, 0, 0), g.at(0, s, 0, 2))

    each(0, l1, cols_1)

    def column(h, j, col):
        return u[h, pl.ds(j * y + col, l1, stride=2 * y), :]

    edges = []
    for c0, c1, w0, w1 in ((0, 1, R3, -1.0), (y - 2, y - 1, 1.0, R3)):
        halves = [lattice(*[w0 * column(h, j, c0) + w1 * column(h, j, c1) for j in range(4)]) for h in range(2)]
        pad = jnp.zeros((ceil8(l1) - l1, t), jnp.float32)
        for xb in range(2):
            edges += [jnp.concatenate([halves[0][xb], halves[1][xb]], axis=-1), pad]
    out = dot_parts(jnp.concatenate(edges, axis=0), f1)
    for m, at in ((mp, 0), (mn, 2)):
        for tb in range(2):
            for xb in range(2):
                row = (at + xb) * ceil8(l1)
                to = (2 * tb + xb) * l1
                m[to : to + l1] = out[row : row + l1, tb * LANES : (tb + 1) * LANES]

    for level, (offset, a, z, f) in enumerate(((3, a2, z2, f2), (2, a3, z3, f3)), 1):
        rows_in, count = sz.lx[level - 1], sz.lx[level]
        p_in, p_out = sz.py[level - 1], sz.py[level]
        for s in range(count):
            picks = [2 * s + j - offset for j in range(4)]
            rows = [g.at(level - 1, i, 0, 0)[...] if 0 <= i < rows_in else None for i in picks]
            low, high = x_lattice_static(rows, (p_in, LANES))
            a[s, 0] = low
            a[s, 1] = high
        out = dot_parts(a[...].reshape(count * 2 * p_in, LANES), f)
        z[:, :, 8 : 8 + p_in, :] = out.reshape(count, 2, p_in, LANES)
        for s in range(count):
            for xb in range(2):
                pad_z(z, (s, xb), 8, 8 + p_in, sz.zrows[level])
                y_analysis(z.at[s, xb], sz.zbase[level], p_out, g.at(level, s, xb, 0), g.at(level, s, xb, 1))
    pack_y(sz, g, mp, mn)


def forward_fine_kernel(sz, u, zh, f1, gb, zl, a1, z1):
    x, y, t = sz.x, sz.y, sz.t
    l1 = sz.lx[0]

    def rows_x(s):
        for h in range(2):
            a1[h, s] = x_lattice_rows(u, h, s, y)[1]

    each(0, l1, rows_x)

    step = 9
    for s0 in range(0, l1, step):
        n = min(step, l1 - s0)
        out = dot_parts(jnp.concatenate([a1[0, s0 : s0 + n], a1[1, s0 : s0 + n]], axis=-1).reshape(n * y, t), f1)
        out = out.reshape(n, y, t)
        z1[s0 : s0 + n, 0, 8 : 8 + y, :] = out[..., :LANES]
        z1[s0 : s0 + n, 1, 8 : 8 + y, :] = out[..., LANES:]

    def cols_1(s):
        zl[8 : 8 + y] = zh[s, 8 : 8 + y, :]
        y_analysis(zl, sz.zbase[0], sz.py[0], gb.at[s, 0, 0], gb.at[s, 0, 1])
        for tb in range(2):
            pad_z(z1, (s, tb), 8, 8 + y, sz.zrows[0])
            y_analysis(z1.at[s, tb], sz.zbase[0], sz.py[0], gb.at[s, 1 + tb, 0], gb.at[s, 1 + tb, 1])

    pad_z(zl, (), 8, 8 + y, sz.zrows[0])
    each(0, l1, cols_1)


def pack_x(sz, g, mp, mn):
    l1, l2, l3 = sz.lx
    lower = lane_below(LANES // 2, (1, LANES))

    def put(ref, pieces, level, items):
        m, w = sz.main[level], sz.ly[level]
        for (main, extra), item in zip(sz.x_offsets(pieces)[level], items):
            for at, lo, hi in ((main, 0, m), (extra, m, w)):
                value = item[0][lo:hi]
                if level == 2:
                    value = jnp.where(lower, value, pltpu.roll(item[1][lo:hi], LANES // 2, 1))
                ref[at : at + hi - lo] = value

    put(mp, sz.xp_pieces, 0, [[g.at(0, 0, 1, q)] for q in range(4)])
    put(mn, sz.xn_pieces, 0, [[g.at(0, l1 - 1, 0, q)] for q in range(4)])
    put(mp, sz.xp_pieces, 1, [[g.at(1, s, 1, q)] for s in (0, 1) for q in (0, 1)])
    put(mn, sz.xn_pieces, 1, [[g.at(1, s, b, q)] for s, b in ((l2 - 2, 0), (l2 - 2, 1), (l2 - 1, 0)) for q in (0, 1)])
    put(mp, sz.xp_pieces, 2, [[g.at(2, s, b, q) for q in (0, 1)] for s, b in ((0, 1), (1, 0), (1, 1))])
    put(mn, sz.xn_pieces, 2, [[g.at(2, s, b, q) for q in (0, 1)] for s, b in ((l3 - 2, 0), (l3 - 2, 1), (l3 - 1, 0))])


def fix_x(sz, g, rn, rp):
    l1, l2, l3 = sz.lx
    lower = lane_below(LANES // 2, (1, LANES))

    def take(ref, pieces, level, lo, hi):
        part = 0 if lo == 0 else 1
        return [ref[at[part] : at[part] + hi - lo] for at in sz.x_offsets(pieces)[level]]

    def halves(value):
        return [jnp.where(lower, v, 0.0) for v in (value, pltpu.roll(value, LANES // 2, 1))]

    for level in range(3):
        m, w = sz.main[level], sz.ly[level]
        for lo, hi in ((0, m), (m, w)):
            n = take(rn, sz.xp_pieces, level, lo, hi)
            p = take(rp, sz.xn_pieces, level, lo, hi)

            def add(s, xb, q, value):
                g.at(level, s, xb, q)[lo:hi] += value

            if level == 0:
                for q in range(4):
                    add(l1 - 1, 0, q, -RHO * n[q])
                    add(l1 - 1, 1, q, n[q])
                    add(0, 0, q, p[q])
                    add(0, 1, q, RHO * p[q])
            elif level == 1:
                for q in range(2):
                    h0, h1 = n[q], n[2 + q]
                    add(l2 - 2, 0, q, -RHO * h0)
                    add(l2 - 2, 1, q, h0)
                    add(l2 - 1, 0, q, KAPPA * h0 - RHO * h1)
                    add(l2 - 1, 1, q, h1)
                    add(0, 0, q, p[q])
                    add(0, 1, q, p[2 + q])
                    add(1, 0, q, p[4 + q])
                    add(1, 1, q, RHO * p[4 + q])
            else:
                n, p = [halves(v) for v in n], [halves(v) for v in p]
                for q in range(2):
                    add(l3 - 2, 0, q, -RHO * n[0][q])
                    add(l3 - 2, 1, q, n[0][q])
                    add(l3 - 1, 0, q, n[1][q])
                    add(l3 - 1, 1, q, n[2][q])
                    add(0, 0, q, p[0][q])
                    add(0, 1, q, p[1][q])
                    add(1, 0, q, p[2][q])
                    add(1, 1, q, RHO * p[2][q])


def pack_y(sz, g, mp, mn):
    k1, k2, k3 = sz.ly
    at_p = at_n = 4 * sz.lx[0]
    for s in range(sz.lx[1]):
        for xb in range(2):
            mp[at_p : at_p + 2] = g.at(1, s, xb, 1)[0:2]
            mn[at_n : at_n + 2] = g.at(1, s, xb, 0)[k2 - 2 : k2]
            mn[at_n + 2 : at_n + 3] = g.at(1, s, xb, 1)[k2 - 2 : k2 - 1]
            at_p += 2
            at_n += 3
    for s in range(sz.lx[2]):
        for xb in range(2):
            mp[at_p : at_p + 2] = g.at(2, s, xb, 1)[0:2]
            mp[at_p + 2 : at_p + 3] = g.at(2, s, xb, 0)[1:2]
            mn[at_n : at_n + 2] = g.at(2, s, xb, 0)[k3 - 2 : k3]
            mn[at_n + 2 : at_n + 3] = g.at(2, s, xb, 1)[k3 - 2 : k3 - 1]
            at_p += 3
            at_n += 3
    if at_p < sz.yp:
        mp[at_p:] = jnp.zeros((sz.yp - at_p, LANES), jnp.float32)
    if at_n < sz.yn:
        mn[at_n:] = jnp.zeros((sz.yn - at_n, LANES), jnp.float32)


def fix_y_fine(sz, g, rn, rp, rows):
    last = sz.ly[0] - 1
    for s in rows:
        for xb in range(2):
            for tb in range(2):
                at = (2 * tb + xb) * sz.lx[0] + s
                high, low = rn[at : at + 1], rp[at : at + 1]
                g.at(0, s, xb, tb)[last : last + 1] += -RHO * high
                g.at(0, s, xb, 2 + tb)[last : last + 1] += high
                g.at(0, s, xb, tb)[0:1] += low
                g.at(0, s, xb, 2 + tb)[0:1] += RHO * low


def fix_y_coarse(sz, g, rn, rp):
    k1, k2, k3 = sz.ly
    at_p = at_n = 4 * sz.lx[0]

    for level in (1, 2):
        k = sz.ly[level]
        for s in range(sz.lx[level]):
            for xb in range(2):

                def add(q, row, value):
                    g.at(level, s, xb, q)[row : row + 1] += value

                h0, h1 = rn[at_n : at_n + 1], rn[at_n + 1 : at_n + 2]
                if level == 1:
                    l1 = KAPPA * h0 - RHO * h1
                    at_n += 2
                else:
                    l1 = rn[at_n + 2 : at_n + 3]
                    at_n += 3
                add(0, k - 2, -RHO * h0)
                add(1, k - 2, h0)
                add(0, k - 1, l1)
                add(1, k - 1, h1)
                w0, w2, w1 = (rp[at_p + i : at_p + i + 1] for i in range(3))
                add(0, 0, w0)
                add(1, 0, w1)
                add(0, 1, w2)
                add(1, 1, RHO * w2)
                at_p += 3


def shrink(v):
    return v - jnp.clip(v, -THRESHOLD, THRESHOLD)


def y_synthesis(low, high, count, t_ref, v_ref, index, start):
    a = low + RHO * high
    b = RHO * low - high
    t_ref[...] = a
    a = t_ref[1 : 1 + count]
    b = b[:count]
    v_ref[index + (pl.ds(start, count, stride=2), slice(None))] = a - R3 * b
    v_ref[index + (pl.ds(start + 1, count, stride=2), slice(None))] = R3 * a + b


def lane_below(limit, shape):
    return lax.broadcasted_iota(jnp.int32, shape, 1) < limit


def level_1_columns(sz, details, s, xb, tb, coarse, ta, v1, index):
    low = coarse if coarse is not None else details(0, s, xb, tb, None)
    high = details(0, s, xb, 2 + tb, None)
    y_synthesis(low, high, sz.y // 2, ta.at[s, xb * 2 + tb, 0 : sz.py[0]], v1, index, 0)


def times_back(sz, v_low, v_high, i1):
    v = jnp.concatenate([v_low, v_high], axis=-1)
    return dot_parts(v.reshape(-1, sz.t), i1).reshape(v.shape)


def inner_inverse(sz, details, i1, va, ba, ta, v1):
    l1 = sz.lx[0]

    def rows(s):
        level_1_columns(sz, details, s, 0, 1, None, ta, va, (s,))
        level_1_columns(sz, details, s, 1, 0, None, ta, v1, (s, 0))
        level_1_columns(sz, details, s, 1, 1, None, ta, v1, (s, 1))

    each(1, l1 - 1, rows)
    step = 15
    for s0 in range(1, l1 - 1, step):
        n = min(step, l1 - 1 - s0)
        ba[s0 : s0 + n] = times_back(sz, v1[s0 : s0 + n, 0], v1[s0 : s0 + n, 1], i1)


def inverse(sz, details, emit, done, groups, va, ba, i1, i2, i3, ta1, ta, v3, b3, v2, b2, v1, b1, ve):
    y, t = sz.y, sz.t
    p1, p2, p3 = sz.py
    l1, l2, l3 = sz.lx
    third = lane_below(t // 8, (p3, LANES))

    for e, s in enumerate((0, l1 - 1)):
        level_1_columns(sz, details, s, 0, 1, None, ta1, va, (s,))
        level_1_columns(sz, details, s, 1, 0, None, ta1, ve, (e, 0))
        level_1_columns(sz, details, s, 1, 1, None, ta1, ve, (e, 1))

    for s in range(l3):
        for xb in range(2):
            low = details(2, s, xb, 0, third if xb == 0 else None)
            high = details(2, s, xb, 1, None)
            y_synthesis(low, high, sz.ly[1] // 2, ta.at[1, s, xb, 0:p3], v3, (s, xb), 0)
    b3[...] = dot_parts(v3[...].reshape(l3 * 2 * p2, LANES), i3).reshape(l3, 2, p2, LANES)

    second = lane_below(t // 4, (p2, LANES))
    for p in range(l2 // 2):
        even, odd = lattice_t(b3[p + 1, 0], b3[p + 1, 1], b3[p, 0], b3[p, 1])
        for s, coarse in ((2 * p, even), (2 * p + 1, odd)):
            for xb in range(2):
                low = details(1, s, xb, 0, None)
                if xb == 0:
                    low = jnp.where(second, coarse, low)
                high = details(1, s, xb, 1, None)
                y_synthesis(low, high, (sz.ly[0] + 1) // 2, ta.at[0, s, xb, 0:p2], v2, (s, xb), 7)
    b2[...] = dot_parts(v2[:, :, 8 : 8 + p1, :].reshape(l2 * 2 * p1, LANES), i2).reshape(l2, 2, p1, LANES)

    edge = times_back(sz, ve[:, 0], ve[:, 1], i1)
    ba[0] = edge[0]
    ba[l1 - 1] = edge[1]

    def coarse_rows(p):
        return lattice_t(b2[p + 1, 0], b2[p + 1, 1], b2[p, 0], b2[p, 1])

    def pair_1(p):
        even, odd = coarse_rows(p)
        level_1_columns(sz, details, 2 * p - 1, 0, 0, even, ta1, v1, (2 * p - 1,))
        level_1_columns(sz, details, 2 * p, 0, 0, odd, ta1, v1, (2 * p,))

    def rows_x(p):
        even, odd = lattice_t(b1[p + 1], ba[p + 1], b1[p], ba[p])
        emit(p, even, odd)

    level_1_columns(sz, details, 0, 0, 0, coarse_rows(0)[1], ta1, v1, (0,))
    step = sz.x // groups
    for x0 in range(0, sz.x, step):
        each(x0 // 4 + 1, (x0 + step) // 4 + 1, pair_1)
        s0, s1 = (x0 // 2 + 1 if x0 else 0), (x0 + step) // 2 + 1
        b1[s0:s1] = times_back(sz, v1[s0:s1], va[s0:s1], i1)
        each(x0 // 2, (x0 + step) // 2, rows_x)
        done(x0, step)


def border(sz, u):
    zeros = jnp.zeros((2 * sz.y, LANES), jnp.float32)
    for h in range(2):
        u[h, 0 : 2 * sz.y, :] = zeros
        u[h, (sz.x + 2) * sz.y :, :] = zeros


def store_u(sz, u, x, value):
    for h in range(2):
        u[h, u_rows(u, x + 2, sz.y), :] = value[:, h * LANES : (h + 1) * LANES]


def scaled_and_weight(c):
    value = c.astype(jnp.float32) * (1.0 / 64.0)
    return value, 1.0 / (1.0 + jnp.abs(value))


def first_kernel(sz, c_hbm, ga, g2, g3, mp, mn, zh, f1, f2, f3, i1, i2, i3, c, sems, u, *scratch):
    step = 4
    copies = [pltpu.make_async_copy(c_hbm.at[x0 : x0 + step], c.at[x0 : x0 + step], sems.at[x0 // step])
              for x0 in range(0, sz.x, step)]
    for copy in copies:
        copy.start()
    border(sz, u)
    for level, (f, i) in enumerate(((f1, i1), (f2, i2), (f3, i3))):
        for m, transposed in ((f, False), (i, True)):
            n = m.shape[1]
            high, low = split(time_matrix(sz.t >> level, n, transposed))
            m[0:n] = high
            m[n : 2 * n] = high
            m[2 * n :] = low
    for x in range(sz.x):
        if x % step == 0:
            copies[x // step].wait()
        value, weight = scaled_and_weight(c[x])
        store_u(sz, u, x, weight * value)
    forward_coarse(sz, u, f1, f2, f3, Bands(ga, None, g2, g3), zh, mp, mn, *scratch)


def forward_fine_first_kernel(sz, c, zh, f1, gb, u, zl, a1, z1):
    border(sz, u)
    for x in range(sz.x):
        value, weight = scaled_and_weight(c[x])
        store_u(sz, u, x, weight * value)
    forward_fine_kernel(sz, u, zh, f1, gb, zl, a1, z1)


def edge_kernel(sz, gai, gbi, g2i, g3i, rn, rp, ga, gb, g2, g3, mp, mn):
    g = Bands(ga, gb, g2, g3)
    fix_y_coarse(sz, g, rn, rp)
    fix_y_fine(sz, g, rn, rp, (0, sz.lx[0] - 1))
    pack_x(sz, g, mp, mn)


def first_details(g):
    def details(level, s, xb, q, approx_lanes):
        value = g.at(level, s, xb, q)[...]
        small = shrink(value)
        return small if approx_lanes is None else jnp.where(approx_lanes, value, small)

    return details


def second_details(g, q_bands):
    def details(level, s, xb, q, approx_lanes):
        first = g.at(level, s, xb, q)[...]
        second = q_bands.at(level, s, xb, q)[...]
        small = shrink(shrink(first) + (first - second))
        if approx_lanes is None:
            return small
        return jnp.where(approx_lanes, first + (first - second), small)

    return details


def inner_first_kernel(sz, gai, gbi, rn, rp, i1, c, ga, gb, va, ba, w_ref, ta, v1):
    for x in range(sz.x):
        w_ref[x] = scaled_and_weight(c[x])[1]
    g = Bands(ga, gb, None, None)
    fix_y_fine(sz, g, rn, rp, range(1, sz.lx[0] - 1))
    inner_inverse(sz, first_details(g), i1, va, ba, ta, v1)


def inner_last_kernel(sz, qai, qbi, rn, rp, i1, ga, gb, qa, qb, va, ba, ta, v1):
    q = Bands(qa, qb, None, None)
    fix_y_fine(sz, q, rn, rp, range(1, sz.lx[0] - 1))
    inner_inverse(sz, second_details(Bands(ga, gb, None, None), q), i1, va, ba, ta, v1)


def middle_kernel(sz, gai, gbi, g2i, g3i, vai, bai, rn, rp, w_ref, f1, f2, f3, i1, i2, i3,
                  ga, gb, g2, g3, va, ba, qa, q2, q3, mp, mn, u, zh, ta1, ta, v3, b3, v2, b2, v1, b1, ve, *scratch):
    g = Bands(ga, gb, g2, g3)
    fix_x(sz, g, rn, rp)
    border(sz, u)

    def emit(p, even, odd):
        store_u(sz, u, 2 * p, w_ref[2 * p] * even)
        store_u(sz, u, 2 * p + 1, w_ref[2 * p + 1] * odd)

    inverse(sz, first_details(g), emit, lambda x0, n: None, 2, va, ba, i1, i2, i3, ta1, ta, v3, b3, v2, b2, v1, b1, ve)
    forward_coarse(sz, u, f1, f2, f3, Bands(qa, None, q2, q3), zh, mp, mn, *scratch)


def last_kernel(sz, qai, qbi, q2i, q3i, vai, bai, rn, rp, ga, gb, g2, g3, i1, i2, i3,
                qa, qb, q2, q3, va, ba, out_hbm, out, sems, ta1, ta, v3, b3, v2, b2, v1, b1, ve):
    q = Bands(qa, qb, q2, q3)
    fix_x(sz, q, rn, rp)

    def emit(p, even, odd):
        out[2 * p] = even
        out[2 * p + 1] = odd

    details = second_details(Bands(ga, gb, g2, g3), q)
    copies = []

    def done(x0, n):
        copies.append(pltpu.make_async_copy(out.at[x0 : x0 + n], out_hbm.at[x0 : x0 + n], sems.at[len(copies)]))
        copies[-1].start()

    inverse(sz, details, emit, done, sz.x // 4, va, ba, i1, i2, i3, ta1, ta, v3, b3, v2, b2, v1, b1, ve)
    for copy in copies:
        copy.wait()


VMEM = pltpu.MemorySpace.VMEM
HBM = pltpu.MemorySpace.HBM


def call(kernel, sz, outs, scratch, aliases, *args, ins_hbm=(), outs_hbm=(), flops=0, limit=36):
    def specs(n, in_hbm):
        return [pl.BlockSpec(memory_space=HBM if k in in_hbm else VMEM) for k in range(n)]

    outs = [s if isinstance(s, jax.ShapeDtypeStruct) else jax.ShapeDtypeStruct(s, jnp.float32) for s in outs]
    return pl.pallas_call(
        functools.partial(kernel, sz),
        out_shape=outs,
        in_specs=specs(len(args), ins_hbm),
        out_specs=specs(len(outs), outs_hbm),
        scratch_shapes=scratch,
        input_output_aliases=aliases,
        cost_estimate=pl.CostEstimate(flops=flops, bytes_accessed=flops // 100, transcendentals=0) if flops else None,
        compiler_params=pltpu.CompilerParams(vmem_limit_bytes=limit * 2**20),
    )(*args)


def on_device(counts):
    sz = Sizes(*counts.shape)
    x, y, t = counts.shape
    l1, l2, l3 = sz.lx
    p1, p2, p3 = sz.py

    def f32(*shapes):
        return [pltpu.VMEM(s, jnp.float32) for s in shapes]

    parts = [jax.ShapeDtypeStruct((3 * n, n), jnp.bfloat16) for n in (t, LANES, LANES)]
    u, zh = (2, (x + 4) * y, LANES), (l1, sz.zrows[0], LANES)
    sems = [pltpu.SemaphoreType.DMA((x // 4,))]
    fw = f32((2, l1, y, LANES), (l1, sz.zrows[0], LANES), (l2, 2, p1, LANES), (l2, 2, sz.zrows[1], LANES),
             (l3, 2, p2, LANES), (l3, 2, sz.zrows[2], LANES))
    fine = f32((sz.zrows[0], LANES), (2, l1, y, LANES), (l1, 2, sz.zrows[0], LANES))
    ta1 = f32((l1, 4, p1 + 8, LANES))
    bw = ta1 + f32((2, l2, 2, p2 + 8, LANES), (l3, 2, p2, LANES), (l3, 2, p2, LANES), (l2, 2, p1 + 8, LANES),
                   (l2, 2, p1, LANES), (l1, y, LANES), (l1, y, t), (2, 2, y, LANES))
    to_prev, to_next = (sz.xp, LANES), (sz.xn, LANES)
    messages = [(sz.yp, LANES), (sz.yn, LANES)]
    halves = [(l1, y, LANES), (l1, y, t)]
    inner = ta1 + f32((l1, 2, y, LANES))
    work = 6 * l1 * y * t * t
    ga, gb, g2, g3 = sz.g

    def exchange(ga, g2, g3, mp, mn, fine_kernel, fine_scratch, source, zh, f1):
        rn, rp = shifted(mp, "gy", -1), shifted(mn, "gy", 1)
        (gb,) = call(fine_kernel, sz, [sz.g[1]], fine_scratch, {}, source, zh, f1, flops=work)
        *g, mp, mn = call(edge_kernel, sz, sz.g + [to_prev, to_next], [], {k: k for k in range(4)},
                          ga, gb, g2, g3, rn, rp)
        return g, (rn, rp), shifted(mp, "gx", -1), shifted(mn, "gx", 1)

    *rest, z_, f1, f2, f3, i1, i2, i3 = call(
        first_kernel, sz, [ga, g2, g3] + messages + [zh] + parts + parts,
        [pltpu.VMEM((x, y, t), jnp.int32)] + sems + f32(u) + fw, {}, counts, ins_hbm=(0,), limit=50)
    f, i = [f1, f2, f3], [i1, i2, i3]
    g, ry, rn, rp = exchange(*rest, forward_fine_first_kernel, f32(u) + fine, counts, z_, f1)
    *kept, va, ba, weight = call(inner_first_kernel, sz, [ga, gb] + halves + [(x, y, t)], inner, {0: 0, 1: 1},
                                 g[0], g[1], *ry, i1, counts, flops=work)
    same = {k: k for k in range(6)}
    *rest, q_a, q_2, q_3, mp, mn, u_, zh_ = call(
        middle_kernel, sz, sz.g + halves + [ga, g2, g3] + messages + [u, zh], bw + fw, same,
        *kept, g[2], g[3], va, ba, rn, rp, weight, *f, *i)
    g = rest[:4]
    q, ry, rn, rp = exchange(q_a, q_2, q_3, mp, mn, forward_fine_kernel, fine, u_, zh_, f1)
    *kept, va, ba = call(inner_last_kernel, sz, [ga, gb] + halves, inner, {0: 0, 1: 1}, q[0], q[1], *ry, i[0], g[0], g[1],
                         flops=work)
    return call(last_kernel, sz, sz.g + halves + [(x, y, t)], f32((x, y, t)) + sems + bw, same,
                *kept, q[2], q[3], va, ba, rn, rp, *g, *i, outs_hbm=(6,))[6]


def solution(mesh):
    spec = P(("grp", "gx"), "gy", None)
    return jax.shard_map(on_device, mesh=mesh, in_specs=(spec,), out_specs=spec, check_vma=False)
```

```python
import functools
import math

import jax
import jax.numpy as jnp
from jax import lax
from jax.experimental import pallas as pl
from jax.experimental.pallas import tpu as pltpu
from jax.sharding import PartitionSpec as P

R3 = math.sqrt(3.0)
H0 = (1.0 + R3) / (4.0 * math.sqrt(2.0))
RHO = (1.0 - R3) / (1.0 + R3)
LOW_TAPS = [H0 * t for t in (1.0, R3, -R3 * RHO, RHO)]
HIGH_TAPS = [LOW_TAPS[3], -LOW_TAPS[2], LOW_TAPS[1], -LOW_TAPS[0]]
KAPPA = -R3 * (1.0 + RHO * RHO)
THRESHOLD = 0.1
LANES = 128


def shifted(x, axis, by):
    count = lax.axis_size(axis)
    return lax.ppermute(x, axis, [(i, (i + by) % count) for i in range(count)])


def time_matrix(length, width, transposed):
    half = length // 2
    row = lax.broadcasted_iota(jnp.int32, (width, width), 1 if transposed else 0)
    col = lax.broadcasted_iota(jnp.int32, (width, width), 0 if transposed else 1)
    is_low = col < half
    offset = lax.rem(row - 2 * jnp.where(is_low, col, col - half) + 2 * length, jnp.int32(length))
    value = jnp.zeros((width, width), jnp.float32)
    for j in range(4):
        tap = jnp.where(is_low, jnp.float32(LOW_TAPS[j] * H0 * H0), jnp.float32(HIGH_TAPS[j] * H0 * H0))
        value = jnp.where(offset == j, tap, value)
    return value if length == width else jnp.where((row < length) & (col < length), value, 0.0)


def split(x):
    high = x.astype(jnp.bfloat16)
    return high, (x - high.astype(jnp.float32)).astype(jnp.bfloat16)


def dot_parts(x, m_ref):
    high, low = split(x)
    return jnp.dot(jnp.concatenate([high, low, high], axis=-1), m_ref[...], preferred_element_type=jnp.float32)


def each(first, end, body):
    for i in range(first, end):
        body(i)


def dot_parts_narrow(x, m_ref):
    out = jnp.dot(jnp.concatenate(split(x), axis=-1), m_ref[...], preferred_element_type=jnp.float32)
    return out[:, :LANES] + out[:, LANES:]


def ceil8(n):
    return (n + 7) // 8 * 8


class Sizes:
    def __init__(self, x, y, t):
        self.x, self.y, self.t = x, y, t
        self.lx = [x // 2 + 1, x // 4 + 2, x // 8 + 2]
        self.ly = [y // 2 + 1, y // 4 + 2, y // 8 + 2]
        self.py = [ceil8(n) for n in self.ly]
        p1, p2, p3 = self.py
        self.g = [(self.lx[0], 2, p1, LANES), (self.lx[0], 3, 2, p1, LANES), (self.lx[1], 2, 2, p2, LANES),
                  (self.lx[2], 2, 2, p3, LANES)]
        self.zin = [y, p1, p2]
        self.zbase = [6, 5, 6]
        self.zrows = [ceil8(2 * (p - 1) + 4 + b) for p, b in zip(self.py, self.zbase)]
        self.main = [y // 2, y // 4, y // 8]
        self.xp_pieces = [4, 4, 3]
        self.xn_pieces = [4, 6, 3]
        self.xp = self.x_rows(self.xp_pieces)
        self.xn = self.x_rows(self.xn_pieces)
        n1, n2, n3 = self.lx[0] * 4, self.lx[1] * 2, self.lx[2] * 2
        self.yp = ceil8(n1 + 2 * n2 + 3 * n3)
        self.yn = ceil8(n1 + 3 * n2 + 3 * n3)


    def x_rows(self, pieces):
        return ceil8(sum(n * w for n, w in zip(pieces, self.ly)))

    def x_offsets(self, pieces):
        at = 0
        mains, extras = [], []
        for n, m in zip(pieces, self.main):
            mains.append([at + i * m for i in range(n)])
            at += n * m
        for n, m, w in zip(pieces, self.main, self.ly):
            extras.append([at + i * (w - m) for i in range(n)])
            at += n * (w - m)
        return [list(zip(a, b)) for a, b in zip(mains, extras)]


def lattice(v0, v1, v2, v3):
    a = v0 + R3 * v1
    b = v3 - R3 * v2
    return a + RHO * b, RHO * a - b


def lattice_t(low_next, high_next, low_here, high_here):
    a = low_next + RHO * high_next
    b = RHO * low_here - high_here
    return a - R3 * b, R3 * a + b


def x_lattice_static(rows, shape):
    v = [jnp.zeros(shape, jnp.float32) if r is None else r for r in rows]
    return lattice(*v)


class Bands:
    def __init__(self, ga, gb, g2, g3):
        self.ga, self.gb, self.g2, self.g3 = ga, gb, g2, g3

    def at(self, level, s, xb, q):
        if level == 1:
            return self.g2.at[s, xb, q]
        if level == 2:
            return self.g3.at[s, xb, q]
        pair, yb = 2 * xb + q % 2, q // 2
        return self.ga.at[s, yb] if pair == 0 else self.gb.at[s, pair - 1, yb]


def y_analysis(z_ref, base, count, low_ref, high_ref):
    v = [z_ref[pl.ds(base + j, count, stride=2), :] for j in range(4)]
    low, high = lattice(*v)
    low_ref[...] = low
    high_ref[...] = high


def u_rows(u, x, y):
    return pl.ds(x * y, y)


def x_lattice_rows(u, h, s, y):
    return lattice(*[u[h, u_rows(u, 2 * s + j, y), :] for j in range(4)])


def pad_z(z, index, lo, hi, total):
    z[index + (slice(0, lo), slice(None))] = jnp.zeros((lo, LANES), jnp.float32)
    if hi < total:
        z[index + (slice(hi, total), slice(None))] = jnp.zeros((total - hi, LANES), jnp.float32)


def forward_coarse(sz, u, f1, f2, f3, g, zh, mp, mn, a1, z1, a2, z2, a3, z3):
    x, y, t = sz.x, sz.y, sz.t
    l1 = sz.lx[0]

    def rows_x(s):
        for h in range(2):
            a1[h, s] = x_lattice_rows(u, h, s, y)[0]

    each(0, l1, rows_x)

    step = 9
    for s0 in range(0, l1, step):
        n = min(step, l1 - s0)
        out = dot_parts(jnp.concatenate([a1[0, s0 : s0 + n], a1[1, s0 : s0 + n]], axis=-1).reshape(n * y, t), f1)
        out = out.reshape(n, y, t)
        z1[s0 : s0 + n, 8 : 8 + y, :] = out[..., :LANES]
        zh[s0 : s0 + n, 8 : 8 + y, :] = out[..., LANES:]

    def cols_1(s):
        pad_z(z1, (s,), 8, 8 + y, sz.zrows[0])
        y_analysis(z1.at[s], sz.zbase[0], sz.py[0], g.at(0, s, 0, 0), g.at(0, s, 0, 2))

    each(0, l1, cols_1)

    def column(h, j, col):
        return u[h, pl.ds(j * y + col, l1, stride=2 * y), :]

    edges = []
    for c0, c1, w0, w1 in ((0, 1, R3, -1.0), (y - 2, y - 1, 1.0, R3)):
        halves = [lattice(*[w0 * column(h, j, c0) + w1 * column(h, j, c1) for j in range(4)]) for h in range(2)]
        pad = jnp.zeros((ceil8(l1) - l1, t), jnp.float32)
        for xb in range(2):
            edges += [jnp.concatenate([halves[0][xb], halves[1][xb]], axis=-1), pad]
    out = dot_parts(jnp.concatenate(edges, axis=0), f1)
    for m, at in ((mp, 0), (mn, 2)):
        for tb in range(2):
            for xb in range(2):
                row = (at + xb) * ceil8(l1)
                to = (2 * tb + xb) * l1
                m[to : to + l1] = out[row : row + l1, tb * LANES : (tb + 1) * LANES]

    for level, (offset, a, z, f) in enumerate(((3, a2, z2, f2), (2, a3, z3, f3)), 1):
        rows_in, count = sz.lx[level - 1], sz.lx[level]
        p_in, p_out = sz.py[level - 1], sz.py[level]
        for s in range(count):
            picks = [2 * s + j - offset for j in range(4)]
            rows = [g.at(level - 1, i, 0, 0)[...] if 0 <= i < rows_in else None for i in picks]
            low, high = x_lattice_static(rows, (p_in, LANES))
            a[s, 0] = low
            a[s, 1] = high
        out = dot_parts_narrow(a[...].reshape(count * 2 * p_in, LANES), f)
        z[:, :, 8 : 8 + p_in, :] = out.reshape(count, 2, p_in, LANES)
        for s in range(count):
            for xb in range(2):
                pad_z(z, (s, xb), 8, 8 + p_in, sz.zrows[level])
                y_analysis(z.at[s, xb], sz.zbase[level], p_out, g.at(level, s, xb, 0), g.at(level, s, xb, 1))
    pack_y(sz, g, mp, mn)


def forward_fine_kernel(sz, u, zh, f1, gb, zl, a1, z1):
    x, y, t = sz.x, sz.y, sz.t
    l1 = sz.lx[0]

    def rows_x(s):
        for h in range(2):
            a1[h, s] = x_lattice_rows(u, h, s, y)[1]

    each(0, l1, rows_x)

    step = 9
    for s0 in range(0, l1, step):
        n = min(step, l1 - s0)
        out = dot_parts(jnp.concatenate([a1[0, s0 : s0 + n], a1[1, s0 : s0 + n]], axis=-1).reshape(n * y, t), f1)
        out = out.reshape(n, y, t)
        z1[s0 : s0 + n, 0, 8 : 8 + y, :] = out[..., :LANES]
        z1[s0 : s0 + n, 1, 8 : 8 + y, :] = out[..., LANES:]

    def cols_1(s):
        zl[8 : 8 + y] = zh[s, 8 : 8 + y, :]
        y_analysis(zl, sz.zbase[0], sz.py[0], gb.at[s, 0, 0], gb.at[s, 0, 1])
        for tb in range(2):
            pad_z(z1, (s, tb), 8, 8 + y, sz.zrows[0])
            y_analysis(z1.at[s, tb], sz.zbase[0], sz.py[0], gb.at[s, 1 + tb, 0], gb.at[s, 1 + tb, 1])

    pad_z(zl, (), 8, 8 + y, sz.zrows[0])
    each(0, l1, cols_1)


def pack_x(sz, g, mp, mn):
    l1, l2, l3 = sz.lx
    lower = lane_below(LANES // 2, (1, LANES))

    def put(ref, pieces, level, items):
        m, w = sz.main[level], sz.ly[level]
        for (main, extra), item in zip(sz.x_offsets(pieces)[level], items):
            for at, lo, hi in ((main, 0, m), (extra, m, w)):
                value = item[0][lo:hi]
                if level == 2:
                    value = jnp.where(lower, value, pltpu.roll(item[1][lo:hi], LANES // 2, 1))
                ref[at : at + hi - lo] = value

    put(mp, sz.xp_pieces, 0, [[g.at(0, 0, 1, q)] for q in range(4)])
    put(mn, sz.xn_pieces, 0, [[g.at(0, l1 - 1, 0, q)] for q in range(4)])
    put(mp, sz.xp_pieces, 1, [[g.at(1, s, 1, q)] for s in (0, 1) for q in (0, 1)])
    put(mn, sz.xn_pieces, 1, [[g.at(1, s, b, q)] for s, b in ((l2 - 2, 0), (l2 - 2, 1), (l2 - 1, 0)) for q in (0, 1)])
    put(mp, sz.xp_pieces, 2, [[g.at(2, s, b, q) for q in (0, 1)] for s, b in ((0, 1), (1, 0), (1, 1))])
    put(mn, sz.xn_pieces, 2, [[g.at(2, s, b, q) for q in (0, 1)] for s, b in ((l3 - 2, 0), (l3 - 2, 1), (l3 - 1, 0))])


def fix_x(sz, g, rn, rp):
    l1, l2, l3 = sz.lx
    lower = lane_below(LANES // 2, (1, LANES))

    def take(ref, pieces, level, lo, hi):
        part = 0 if lo == 0 else 1
        return [ref[at[part] : at[part] + hi - lo] for at in sz.x_offsets(pieces)[level]]

    def halves(value):
        return [jnp.where(lower, v, 0.0) for v in (value, pltpu.roll(value, LANES // 2, 1))]

    for level in range(3):
        m, w = sz.main[level], sz.ly[level]
        for lo, hi in ((0, m), (m, w)):
            n = take(rn, sz.xp_pieces, level, lo, hi)
            p = take(rp, sz.xn_pieces, level, lo, hi)

            def add(s, xb, q, value):
                g.at(level, s, xb, q)[lo:hi] += value

            if level == 0:
                for q in range(4):
                    add(l1 - 1, 0, q, -RHO * n[q])
                    add(l1 - 1, 1, q, n[q])
                    add(0, 0, q, p[q])
                    add(0, 1, q, RHO * p[q])
            elif level == 1:
                for q in range(2):
                    h0, h1 = n[q], n[2 + q]
                    add(l2 - 2, 0, q, -RHO * h0)
                    add(l2 - 2, 1, q, h0)
                    add(l2 - 1, 0, q, KAPPA * h0 - RHO * h1)
                    add(l2 - 1, 1, q, h1)
                    add(0, 0, q, p[q])
                    add(0, 1, q, p[2 + q])
                    add(1, 0, q, p[4 + q])
                    add(1, 1, q, RHO * p[4 + q])
            else:
                n, p = [halves(v) for v in n], [halves(v) for v in p]
                for q in range(2):
                    add(l3 - 2, 0, q, -RHO * n[0][q])
                    add(l3 - 2, 1, q, n[0][q])
                    add(l3 - 1, 0, q, n[1][q])
                    add(l3 - 1, 1, q, n[2][q])
                    add(0, 0, q, p[0][q])
                    add(0, 1, q, p[1][q])
                    add(1, 0, q, p[2][q])
                    add(1, 1, q, RHO * p[2][q])


def pack_y(sz, g, mp, mn):
    k1, k2, k3 = sz.ly
    at_p = at_n = 4 * sz.lx[0]
    for s in range(sz.lx[1]):
        for xb in range(2):
            mp[at_p : at_p + 2] = g.at(1, s, xb, 1)[0:2]
            mn[at_n : at_n + 2] = g.at(1, s, xb, 0)[k2 - 2 : k2]
            mn[at_n + 2 : at_n + 3] = g.at(1, s, xb, 1)[k2 - 2 : k2 - 1]
            at_p += 2
            at_n += 3
    for s in range(sz.lx[2]):
        for xb in range(2):
            mp[at_p : at_p + 2] = g.at(2, s, xb, 1)[0:2]
            mp[at_p + 2 : at_p + 3] = g.at(2, s, xb, 0)[1:2]
            mn[at_n : at_n + 2] = g.at(2, s, xb, 0)[k3 - 2 : k3]
            mn[at_n + 2 : at_n + 3] = g.at(2, s, xb, 1)[k3 - 2 : k3 - 1]
            at_p += 3
            at_n += 3
    if at_p < sz.yp:
        mp[at_p:] = jnp.zeros((sz.yp - at_p, LANES), jnp.float32)
    if at_n < sz.yn:
        mn[at_n:] = jnp.zeros((sz.yn - at_n, LANES), jnp.float32)


def fix_y_fine(sz, g, rn, rp, rows):
    last = sz.ly[0] - 1
    for s in rows:
        for xb in range(2):
            for tb in range(2):
                at = (2 * tb + xb) * sz.lx[0] + s
                high, low = rn[at : at + 1], rp[at : at + 1]
                g.at(0, s, xb, tb)[last : last + 1] += -RHO * high
                g.at(0, s, xb, 2 + tb)[last : last + 1] += high
                g.at(0, s, xb, tb)[0:1] += low
                g.at(0, s, xb, 2 + tb)[0:1] += RHO * low


def fix_y_coarse(sz, g, rn, rp):
    k1, k2, k3 = sz.ly
    at_p = at_n = 4 * sz.lx[0]

    for level in (1, 2):
        k = sz.ly[level]
        for s in range(sz.lx[level]):
            for xb in range(2):

                def add(q, row, value):
                    g.at(level, s, xb, q)[row : row + 1] += value

                h0, h1 = rn[at_n : at_n + 1], rn[at_n + 1 : at_n + 2]
                if level == 1:
                    l1 = KAPPA * h0 - RHO * h1
                    at_n += 2
                else:
                    l1 = rn[at_n + 2 : at_n + 3]
                    at_n += 3
                add(0, k - 2, -RHO * h0)
                add(1, k - 2, h0)
                add(0, k - 1, l1)
                add(1, k - 1, h1)
                w0, w2, w1 = (rp[at_p + i : at_p + i + 1] for i in range(3))
                add(0, 0, w0)
                add(1, 0, w1)
                add(0, 1, w2)
                add(1, 1, RHO * w2)
                at_p += 3


def shrink(v):
    return v - jnp.clip(v, -THRESHOLD, THRESHOLD)


def y_synthesis(low, high, count, t_ref, v_ref, index, start):
    a = low + RHO * high
    b = RHO * low - high
    t_ref[...] = a
    a = t_ref[1 : 1 + count]
    b = b[:count]
    v_ref[index + (pl.ds(start, count, stride=2), slice(None))] = a - R3 * b
    v_ref[index + (pl.ds(start + 1, count, stride=2), slice(None))] = R3 * a + b


def lane_below(limit, shape):
    return lax.broadcasted_iota(jnp.int32, shape, 1) < limit


def level_1_columns(sz, details, s, xb, tb, coarse, ta, v1, index):
    low = details(0, s, xb, tb, None) if coarse is None else coarse
    high = details(0, s, xb, 2 + tb, None)
    y_synthesis(low, high, sz.y // 2, ta.at[s, xb * 2 + tb, 0 : sz.py[0]], v1, index, 0)


def times_back(sz, v_low, v_high, i1):
    v = jnp.concatenate([v_low, v_high], axis=-1)
    return dot_parts(v.reshape(-1, sz.t), i1).reshape(v.shape)


def inner_inverse(sz, details, i1, ba, ta, v1):
    l1 = sz.lx[0]

    def rows(s):
        for xb in range(2):
            for tb in range(2):
                coarse = 0.0 if xb == 0 and tb == 0 else None
                level_1_columns(sz, details, s, xb, tb, coarse, ta, v1, (tb, s, xb))

    each(1, l1 - 1, rows)
    for s0 in range(1, l1 - 1, 15):
        n = min(15, l1 - 1 - s0)
        ba[s0 : s0 + n] = times_back(sz, v1[0, s0 : s0 + n], v1[1, s0 : s0 + n], i1)


def inverse(sz, details, emit, done, groups, ba, i1, i2, i3, ta1, ta, v3, b3, v2, b2, v1, b1, ve):
    y, t = sz.y, sz.t
    p1, p2, p3 = sz.py
    l1, l2, l3 = sz.lx
    third = lane_below(t // 8, (p3, LANES))

    for s in range(l3):
        for xb in range(2):
            low = details(2, s, xb, 0, third if xb == 0 else None)
            high = details(2, s, xb, 1, None)
            y_synthesis(low, high, sz.ly[1] // 2, ta.at[1, s, xb, 0:p3], v3, (s, xb), 0)
    b3[...] = dot_parts_narrow(v3[...].reshape(l3 * 2 * p2, LANES), i3).reshape(l3, 2, p2, LANES)

    second = lane_below(t // 4, (p2, LANES))
    for p in range(l2 // 2):
        even, odd = lattice_t(b3[p + 1, 0], b3[p + 1, 1], b3[p, 0], b3[p, 1])
        for s, coarse in ((2 * p, even), (2 * p + 1, odd)):
            for xb in range(2):
                low = details(1, s, xb, 0, None)
                if xb == 0:
                    low = jnp.where(second, coarse, low)
                high = details(1, s, xb, 1, None)
                y_synthesis(low, high, (sz.ly[0] + 1) // 2, ta.at[0, s, xb, 0:p2], v2, (s, xb), 7)
    b2[...] = dot_parts_narrow(v2[:, :, 8 : 8 + p1, :].reshape(l2 * 2 * p1, LANES), i2).reshape(l2, 2, p1, LANES)

    def coarse_rows(p):
        return lattice_t(b2[p + 1, 0], b2[p + 1, 1], b2[p, 0], b2[p, 1])

    n = t // 2
    half = jnp.concatenate([i1[0:n], i1[t : t + n], i1[2 * t : 2 * t + n]], axis=0)

    def coarse_columns(s, low):
        y_synthesis(low, 0.0, y // 2, ta1.at[s, 0, 0:p1], v1, (s,), 0)

    def pair_1(p):
        even, odd = coarse_rows(p)
        coarse_columns(2 * p - 1, even)
        if p < l2 - 2:
            coarse_columns(2 * p, odd)
        else:
            ends.append(odd)

    def rows_x(p):
        even, odd = lattice_t(b1[p + 1] + ba[p + 1, 0], ba[p + 1, 1], b1[p] + ba[p, 0], ba[p, 1])
        emit(p, even, odd)

    ends = [coarse_rows(0)[1]]
    step = sz.x // groups
    for x0 in range(0, sz.x, step):
        each(x0 // 4 + 1, (x0 + step) // 4 + 1, pair_1)
        s0, s1 = x0 // 2 + 1, min((x0 + step) // 2 + 1, l1 - 1)
        b1[s0:s1] = dot_parts(v1[s0:s1].reshape(-1, LANES), half).reshape(s1 - s0, y, t)
        if x0 == 0 or x0 + step == sz.x:
            e, s = (0, 0) if x0 == 0 else (1, l1 - 1)
            for xb in range(2):
                for tb in range(2):
                    coarse = ends[e] if xb == 0 and tb == 0 else None
                    level_1_columns(sz, details, s, xb, tb, coarse, ta1, ve, (tb, e, xb))
            ba[s] = times_back(sz, ve[0, e], ve[1, e], i1)
            b1[s] = jnp.zeros((y, t), jnp.float32)
        each(x0 // 2, (x0 + step) // 2, rows_x)
        done(x0, step)


def border(sz, u):
    zeros = jnp.zeros((2 * sz.y, LANES), jnp.float32)
    for h in range(2):
        u[h, 0 : 2 * sz.y, :] = zeros
        u[h, (sz.x + 2) * sz.y :, :] = zeros


def store_u(sz, u, x, value):
    for h in range(2):
        u[h, u_rows(u, x + 2, sz.y), :] = value[:, h * LANES : (h + 1) * LANES]


def scaled_and_weight(c):
    value = c.astype(jnp.float32) * (1.0 / 64.0)
    return value, 1.0 / (1.0 + jnp.abs(value))


def first_kernel(sz, c_hbm, ga, g2, g3, mp, mn, zh, f1, f2, f3, i1, i2, i3, c, sems, u, *scratch):
    step = 4
    copies = [pltpu.make_async_copy(c_hbm.at[x0 : x0 + step], c.at[x0 : x0 + step], sems.at[x0 // step])
              for x0 in range(0, sz.x, step)]
    for copy in copies:
        copy.start()
    border(sz, u)
    for level, (f, i) in enumerate(((f1, i1), (f2, i2), (f3, i3))):
        for m, transposed in ((f, False), (i, True)):
            n = LANES if level else sz.t
            high, low = split(time_matrix(sz.t >> level, n, transposed))
            m[0:n, 0:n] = high
            m[n : 2 * n, 0:n] = high
            if level:
                m[0:n, n:] = low
                m[n:, n:] = jnp.zeros_like(low)
            else:
                m[2 * n :] = low
    for x in range(sz.x):
        if x % step == 0:
            copies[x // step].wait()
        value, weight = scaled_and_weight(c[x])
        store_u(sz, u, x, weight * value)
    forward_coarse(sz, u, f1, f2, f3, Bands(ga, None, g2, g3), zh, mp, mn, *scratch)


def forward_fine_first_kernel(sz, c, zh, f1, gb, u, zl, a1, z1):
    border(sz, u)
    for x in range(sz.x):
        value, weight = scaled_and_weight(c[x])
        store_u(sz, u, x, weight * value)
    forward_fine_kernel(sz, u, zh, f1, gb, zl, a1, z1)


def edge_kernel(sz, gai, gbi, g2i, g3i, rn, rp, ga, gb, g2, g3, mp, mn):
    g = Bands(ga, gb, g2, g3)
    fix_y_coarse(sz, g, rn, rp)
    fix_y_fine(sz, g, rn, rp, (0, sz.lx[0] - 1))
    pack_x(sz, g, mp, mn)


def first_details(g):
    def details(level, s, xb, q, approx_lanes):
        value = g.at(level, s, xb, q)[...]
        small = shrink(value)
        return small if approx_lanes is None else jnp.where(approx_lanes, value, small)

    return details


def second_details(g, q_bands):
    def details(level, s, xb, q, approx_lanes):
        first = g.at(level, s, xb, q)[...]
        second = q_bands.at(level, s, xb, q)[...]
        small = shrink(shrink(first) + (first - second))
        if approx_lanes is None:
            return small
        return jnp.where(approx_lanes, first + (first - second), small)

    return details


def inner_first_kernel(sz, gai, gbi, rn, rp, i1, c, ga, gb, ba, w_ref, ta, v1):
    for x in range(sz.x):
        w_ref[x] = scaled_and_weight(c[x])[1]
    g = Bands(ga, gb, None, None)
    fix_y_fine(sz, g, rn, rp, range(1, sz.lx[0] - 1))
    inner_inverse(sz, first_details(g), i1, ba, ta, v1)


def inner_last_kernel(sz, qai, qbi, rn, rp, i1, ga, gb, qa, qb, ba, ta, v1):
    q = Bands(qa, qb, None, None)
    fix_y_fine(sz, q, rn, rp, range(1, sz.lx[0] - 1))
    inner_inverse(sz, second_details(Bands(ga, gb, None, None), q), i1, ba, ta, v1)


def middle_kernel(sz, gai, gbi, g2i, g3i, bai, rn, rp, w_ref, f1, f2, f3, i1, i2, i3,
                  ga, gb, g2, g3, ba, qa, q2, q3, mp, mn, u, zh, ta1, ta, v3, b3, v2, b2, v1, b1, ve, *scratch):
    g = Bands(ga, gb, g2, g3)
    fix_x(sz, g, rn, rp)
    border(sz, u)

    def emit(p, even, odd):
        store_u(sz, u, 2 * p, w_ref[2 * p] * even)
        store_u(sz, u, 2 * p + 1, w_ref[2 * p + 1] * odd)

    inverse(sz, first_details(g), emit, lambda x0, n: None, 2, ba, i1, i2, i3, ta1, ta, v3, b3, v2, b2, v1, b1, ve)
    forward_coarse(sz, u, f1, f2, f3, Bands(qa, None, q2, q3), zh, mp, mn, *scratch)


def last_kernel(sz, qai, qbi, q2i, q3i, bai, rn, rp, ga, gb, g2, g3, i1, i2, i3,
                qa, qb, q2, q3, ba, out_hbm, out, sems, ta1, ta, v3, b3, v2, b2, v1, b1, ve):
    q = Bands(qa, qb, q2, q3)
    fix_x(sz, q, rn, rp)

    def emit(p, even, odd):
        out[2 * p] = even
        out[2 * p + 1] = odd

    details = second_details(Bands(ga, gb, g2, g3), q)
    copies = []

    def done(x0, n):
        copies.append(pltpu.make_async_copy(out.at[x0 : x0 + n], out_hbm.at[x0 : x0 + n], sems.at[len(copies)]))
        copies[-1].start()

    inverse(sz, details, emit, done, sz.x // 4, ba, i1, i2, i3, ta1, ta, v3, b3, v2, b2, v1, b1, ve)
    for copy in copies:
        copy.wait()


VMEM = pltpu.MemorySpace.VMEM
HBM = pltpu.MemorySpace.HBM


def call(kernel, sz, outs, scratch, aliases, *args, ins_hbm=(), outs_hbm=(), flops=0, limit=36):
    def specs(n, in_hbm):
        return [pl.BlockSpec(memory_space=HBM if k in in_hbm else VMEM) for k in range(n)]

    outs = [s if isinstance(s, jax.ShapeDtypeStruct) else jax.ShapeDtypeStruct(s, jnp.float32) for s in outs]
    return pl.pallas_call(
        functools.partial(kernel, sz),
        out_shape=outs,
        in_specs=specs(len(args), ins_hbm),
        out_specs=specs(len(outs), outs_hbm),
        scratch_shapes=scratch,
        input_output_aliases=aliases,
        cost_estimate=pl.CostEstimate(flops=flops, bytes_accessed=flops // 100, transcendentals=0) if flops else None,
        compiler_params=pltpu.CompilerParams(vmem_limit_bytes=limit * 2**20),
    )(*args)


def on_device(counts):
    sz = Sizes(*counts.shape)
    x, y, t = counts.shape
    l1, l2, l3 = sz.lx
    p1, p2, p3 = sz.py

    def f32(*shapes):
        return [pltpu.VMEM(s, jnp.float32) for s in shapes]

    parts = [jax.ShapeDtypeStruct(s, jnp.bfloat16) for s in ((3 * t, t), (2 * LANES,) * 2, (2 * LANES,) * 2)]
    u, zh = (2, (x + 4) * y, LANES), (l1, sz.zrows[0], LANES)
    sems = [pltpu.SemaphoreType.DMA((x // 4,))]
    fw = f32((2, l1, y, LANES), (l1, sz.zrows[0], LANES), (l2, 2, p1, LANES), (l2, 2, sz.zrows[1], LANES),
             (l3, 2, p2, LANES), (l3, 2, sz.zrows[2], LANES))
    fine = f32((sz.zrows[0], LANES), (2, l1, y, LANES), (l1, 2, sz.zrows[0], LANES))
    ta1 = f32((l1, 4, p1 + 8, LANES))
    bw = ta1 + f32((2, l2, 2, p2 + 8, LANES), (l3, 2, p2, LANES), (l3, 2, p2, LANES), (l2, 2, p1 + 8, LANES),
                   (l2, 2, p1, LANES), (l1, y, LANES), (l1, y, t), (2, 2, 2, y, LANES))
    to_prev, to_next = (sz.xp, LANES), (sz.xn, LANES)
    messages = [(sz.yp, LANES), (sz.yn, LANES)]
    halves = [(l1, 2, y, t)]
    inner = ta1 + f32((2, l1, 2, y, LANES))
    work = 6 * l1 * y * t * t
    ga, gb, g2, g3 = sz.g

    def exchange(ga, g2, g3, mp, mn, fine_kernel, fine_scratch, source, zh, f1):
        rn, rp = shifted(mp, "gy", -1), shifted(mn, "gy", 1)
        (gb,) = call(fine_kernel, sz, [sz.g[1]], fine_scratch, {}, source, zh, f1, flops=work)
        *g, mp, mn = call(edge_kernel, sz, sz.g + [to_prev, to_next], [], {k: k for k in range(4)},
                          ga, gb, g2, g3, rn, rp)
        return g, (rn, rp), shifted(mp, "gx", -1), shifted(mn, "gx", 1)

    *rest, z_, f1, f2, f3, i1, i2, i3 = call(
        first_kernel, sz, [ga, g2, g3] + messages + [zh] + parts + parts,
        [pltpu.VMEM((x, y, t), jnp.int32)] + sems + f32(u) + fw, {}, counts, ins_hbm=(0,), limit=50)
    f, i = [f1, f2, f3], [i1, i2, i3]
    g, ry, rn, rp = exchange(*rest, forward_fine_first_kernel, f32(u) + fine, counts, z_, f1)
    *kept, ba, weight = call(inner_first_kernel, sz, [ga, gb] + halves + [(x, y, t)], inner, {0: 0, 1: 1},
                                 g[0], g[1], *ry, i1, counts, flops=work)
    same = {k: k for k in range(5)}
    *rest, q_a, q_2, q_3, mp, mn, u_, zh_ = call(
        middle_kernel, sz, sz.g + halves + [ga, g2, g3] + messages + [u, zh], bw + fw, same,
        *kept, g[2], g[3], ba, rn, rp, weight, *f, *i)
    g = rest[:4]
    q, ry, rn, rp = exchange(q_a, q_2, q_3, mp, mn, forward_fine_kernel, fine, u_, zh_, f1)
    *kept, ba = call(inner_last_kernel, sz, [ga, gb] + halves, inner, {0: 0, 1: 1}, q[0], q[1], *ry, i[0], g[0], g[1],
                         flops=work)
    return call(last_kernel, sz, sz.g + halves + [(x, y, t)], f32((x, y, t)) + sems + bw, same,
                *kept, q[2], q[3], ba, rn, rp, *g, *i, outs_hbm=(5,))[5]


def solution(mesh):
    spec = P(("grp", "gx"), "gy", None)
    return jax.shard_map(on_device, mesh=mesh, in_specs=(spec,), out_specs=spec, check_vma=False)
```

```python
import functools
import math

import jax
import jax.numpy as jnp
from jax import lax
from jax.experimental import pallas as pl
from jax.experimental.pallas import tpu as pltpu
from jax.sharding import PartitionSpec as P

R3 = math.sqrt(3.0)
H0 = (1.0 + R3) / (4.0 * math.sqrt(2.0))
RHO = (1.0 - R3) / (1.0 + R3)
LOW_TAPS = [H0 * t for t in (1.0, R3, -R3 * RHO, RHO)]
HIGH_TAPS = [LOW_TAPS[3], -LOW_TAPS[2], LOW_TAPS[1], -LOW_TAPS[0]]
KAPPA = -R3 * (1.0 + RHO * RHO)
THRESHOLD = 0.1
LANES = 128


def shifted(x, axis, by):
    count = lax.axis_size(axis)
    return lax.ppermute(x, axis, [(i, (i + by) % count) for i in range(count)])


def time_matrix(length, width, transposed):
    half = length // 2
    row = lax.broadcasted_iota(jnp.int32, (width, width), 1 if transposed else 0)
    col = lax.broadcasted_iota(jnp.int32, (width, width), 0 if transposed else 1)
    is_low = col < half
    offset = lax.rem(row - 2 * jnp.where(is_low, col, col - half) + 2 * length, jnp.int32(length))
    value = jnp.zeros((width, width), jnp.float32)
    for j in range(4):
        tap = jnp.where(is_low, jnp.float32(LOW_TAPS[j] * H0 * H0), jnp.float32(HIGH_TAPS[j] * H0 * H0))
        value = jnp.where(offset == j, tap, value)
    return value if length == width else jnp.where((row < length) & (col < length), value, 0.0)


def split(x):
    high = x.astype(jnp.bfloat16)
    return high, (x - high.astype(jnp.float32)).astype(jnp.bfloat16)


def dot_parts(x, m_ref):
    high, low = split(x)
    return jnp.dot(jnp.concatenate([high, low, high], axis=-1), m_ref[...], preferred_element_type=jnp.float32)


def each(first, end, body):
    for i in range(first, end):
        body(i)


def dot_parts_narrow(x, m_ref):
    out = jnp.dot(jnp.concatenate(split(x), axis=-1), m_ref[...], preferred_element_type=jnp.float32)
    return out[:, :LANES] + out[:, LANES:]


def ceil8(n):
    return (n + 7) // 8 * 8


class Sizes:
    def __init__(self, x, y, t):
        self.x, self.y, self.t = x, y, t
        self.lx = [x // 2 + 1, x // 4 + 2, x // 8 + 2]
        self.ly = [y // 2 + 1, y // 4 + 2, y // 8 + 2]
        self.py = [ceil8(n) for n in self.ly]
        p1, p2, p3 = self.py
        self.g = [(self.lx[0], 2, p1, LANES), (self.lx[0], 3, 2, p1, LANES), (self.lx[1], 2, 2, p2, LANES),
                  (self.lx[2], 2, 2, p3, LANES)]
        self.zin = [y, p1, p2]
        self.zbase = [6, 5, 6]
        self.zfill = [ceil8(2 * (p - 1) + 4 + b) for p, b in zip(self.py, self.zbase)]
        self.zrows = [n + 8 for n in self.zfill]
        self.vrows = [2 * ceil8(self.ly[1] // 2), 8 + 2 * ceil8((self.ly[0] + 1) // 2)]
        self.main = [y // 2, y // 4, y // 8]
        self.xp_pieces = [4, 4, 3]
        self.xn_pieces = [4, 6, 3]
        self.xp = self.x_rows(self.xp_pieces)
        self.xn = self.x_rows(self.xn_pieces)
        n1, n2, n3 = self.lx[0] * 4, self.lx[1] * 2, self.lx[2] * 2
        self.yp = ceil8(n1 + 2 * n2 + 3 * n3) + 8
        self.yn = ceil8(n1 + 3 * n2 + 3 * n3) + 8


    def x_rows(self, pieces):
        return ceil8(sum(n * w for n, w in zip(pieces, self.ly)))

    def x_offsets(self, pieces):
        at = 0
        mains, extras = [], []
        for n, m in zip(pieces, self.main):
            mains.append([at + i * m for i in range(n)])
            at += n * m
        for n, m, w in zip(pieces, self.main, self.ly):
            extras.append([at + i * (w - m) for i in range(n)])
            at += n * (w - m)
        return [list(zip(a, b)) for a, b in zip(mains, extras)]


def lattice(v0, v1, v2, v3):
    a = v0 + R3 * v1
    b = v3 - R3 * v2
    return a + RHO * b, RHO * a - b


def lattice_t(low_next, high_next, low_here, high_here):
    a = low_next + RHO * high_next
    b = RHO * low_here - high_here
    return a - R3 * b, R3 * a + b


def x_lattice_static(rows, shape):
    v = [jnp.zeros(shape, jnp.float32) if r is None else r for r in rows]
    return lattice(*v)


class Bands:
    def __init__(self, ga, gb, g2, g3):
        self.ga, self.gb, self.g2, self.g3 = ga, gb, g2, g3

    def at(self, level, s, xb, q):
        if level == 1:
            return self.g2.at[s, xb, q]
        if level == 2:
            return self.g3.at[s, xb, q]
        pair, yb = 2 * xb + q % 2, q // 2
        return self.ga.at[s, yb] if pair == 0 else self.gb.at[s, pair - 1, yb]


def y_analysis(z_ref, base, count, low_ref, high_ref):
    v = [z_ref[pl.ds(base + j, count, stride=2), :] for j in range(4)]
    low, high = lattice(*v)
    low_ref[...] = low
    high_ref[...] = high


def u_rows(u, x, y):
    return pl.ds(x * y, y)


def x_lattice_rows(u, h, s, y):
    return lattice(*[u[h, u_rows(u, 2 * s + j, y), :] for j in range(4)])


def pad_z(z, index, lo, hi, total):
    z[index + (slice(0, lo), slice(None))] = jnp.zeros((lo, LANES), jnp.float32)
    if hi < total:
        z[index + (slice(hi, total), slice(None))] = jnp.zeros((total - hi, LANES), jnp.float32)


def forward_coarse(sz, u, f1, f2, f3, g, zh, mp, mn, a1, z1, a2, z2, a3, z3):
    x, y, t = sz.x, sz.y, sz.t
    l1 = sz.lx[0]

    def rows_x(s):
        for h in range(2):
            a1[h, s] = x_lattice_rows(u, h, s, y)[0]

    each(0, l1, rows_x)

    step = 9
    for s0 in range(0, l1, step):
        n = min(step, l1 - s0)
        out = dot_parts(jnp.concatenate([a1[0, s0 : s0 + n], a1[1, s0 : s0 + n]], axis=-1).reshape(n * y, t), f1)
        out = out.reshape(n, y, t)
        z1[s0 : s0 + n, 8 : 8 + y, :] = out[..., :LANES]
        zh[s0 : s0 + n, 8 : 8 + y, :] = out[..., LANES:]

    def cols_1(s):
        pad_z(z1, (s,), 8, 8 + y, sz.zfill[0])
        y_analysis(z1.at[s], sz.zbase[0], sz.py[0], g.at(0, s, 0, 0), g.at(0, s, 0, 2))

    each(0, l1, cols_1)

    def column(h, j, col):
        last = (2 * (l1 - 1) + j) * y + col
        return jnp.concatenate(
            [u[h, pl.ds(j * y + col, l1 - 1, stride=2 * y), :], u[h, last : last + 1, :]], axis=0)

    edges = []
    for c0, c1, w0, w1 in ((0, 1, R3, -1.0), (y - 2, y - 1, 1.0, R3)):
        halves = [lattice(*[w0 * column(h, j, c0) + w1 * column(h, j, c1) for j in range(4)]) for h in range(2)]
        pad = jnp.zeros((ceil8(l1) - l1, t), jnp.float32)
        for xb in range(2):
            edges += [jnp.concatenate([halves[0][xb], halves[1][xb]], axis=-1), pad]
    out = dot_parts(jnp.concatenate(edges, axis=0), f1)
    for m, at in ((mp, 0), (mn, 2)):
        for tb in range(2):
            for xb in range(2):
                row = (at + xb) * ceil8(l1)
                to = (2 * tb + xb) * l1
                m[to : to + l1] = out[row : row + l1, tb * LANES : (tb + 1) * LANES]

    for level, (offset, a, z, f) in enumerate(((3, a2, z2, f2), (2, a3, z3, f3)), 1):
        rows_in, count = sz.lx[level - 1], sz.lx[level]
        p_in, p_out = sz.py[level - 1], sz.py[level]
        for s in range(count):
            picks = [2 * s + j - offset for j in range(4)]
            rows = [g.at(level - 1, i, 0, 0)[...] if 0 <= i < rows_in else None for i in picks]
            low, high = x_lattice_static(rows, (p_in, LANES))
            a[s, 0] = low
            a[s, 1] = high
        out = dot_parts_narrow(a[...].reshape(count * 2 * p_in, LANES), f)
        z[:, :, 8 : 8 + p_in, :] = out.reshape(count, 2, p_in, LANES)
        for s in range(count):
            for xb in range(2):
                pad_z(z, (s, xb), 8, 8 + p_in, sz.zfill[level])
                y_analysis(z.at[s, xb], sz.zbase[level], p_out, g.at(level, s, xb, 0), g.at(level, s, xb, 1))
    pack_y(sz, g, mp, mn)


def forward_fine_kernel(sz, u, zh, f1, gb, zl, a1, z1):
    x, y, t = sz.x, sz.y, sz.t
    l1 = sz.lx[0]

    def rows_x(s):
        for h in range(2):
            a1[h, s] = x_lattice_rows(u, h, s, y)[1]

    each(0, l1, rows_x)

    step = 9
    for s0 in range(0, l1, step):
        n = min(step, l1 - s0)
        out = dot_parts(jnp.concatenate([a1[0, s0 : s0 + n], a1[1, s0 : s0 + n]], axis=-1).reshape(n * y, t), f1)
        out = out.reshape(n, y, t)
        z1[s0 : s0 + n, 0, 8 : 8 + y, :] = out[..., :LANES]
        z1[s0 : s0 + n, 1, 8 : 8 + y, :] = out[..., LANES:]

    def cols_1(s):
        zl[8 : 8 + y] = zh[s, 8 : 8 + y, :]
        y_analysis(zl, sz.zbase[0], sz.py[0], gb.at[s, 0, 0], gb.at[s, 0, 1])
        for tb in range(2):
            pad_z(z1, (s, tb), 8, 8 + y, sz.zfill[0])
            y_analysis(z1.at[s, tb], sz.zbase[0], sz.py[0], gb.at[s, 1 + tb, 0], gb.at[s, 1 + tb, 1])

    pad_z(zl, (), 8, 8 + y, sz.zfill[0])
    each(0, l1, cols_1)


def pack_x(sz, g, mp, mn):
    l1, l2, l3 = sz.lx
    lower = lane_below(LANES // 2, (1, LANES))

    def put(ref, pieces, level, items):
        m, w = sz.main[level], sz.ly[level]
        for (main, extra), item in zip(sz.x_offsets(pieces)[level], items):
            for at, lo, hi in ((main, 0, m), (extra, m, w)):
                value = item[0][lo:hi]
                if level == 2:
                    value = jnp.where(lower, value, pltpu.roll(item[1][lo:hi], LANES // 2, 1))
                if lo == 0:
                    ref[at : at + hi] = value
                else:
                    tails[ref is mn].append(value)

    tails = [], []
    put(mp, sz.xp_pieces, 0, [[g.at(0, 0, 1, q)] for q in range(4)])
    put(mn, sz.xn_pieces, 0, [[g.at(0, l1 - 1, 0, q)] for q in range(4)])
    put(mp, sz.xp_pieces, 1, [[g.at(1, s, 1, q)] for s in (0, 1) for q in (0, 1)])
    put(mn, sz.xn_pieces, 1, [[g.at(1, s, b, q)] for s, b in ((l2 - 2, 0), (l2 - 2, 1), (l2 - 1, 0)) for q in (0, 1)])
    put(mp, sz.xp_pieces, 2, [[g.at(2, s, b, q) for q in (0, 1)] for s, b in ((0, 1), (1, 0), (1, 1))])
    put(mn, sz.xn_pieces, 2, [[g.at(2, s, b, q) for q in (0, 1)] for s, b in ((l3 - 2, 0), (l3 - 2, 1), (l3 - 1, 0))])
    for ref, tail, pieces in ((mp, tails[0], sz.xp_pieces), (mn, tails[1], sz.xn_pieces)):
        at = sz.x_offsets(pieces)[0][0][1]
        rest = ref.shape[0] - at - sum(v.shape[0] for v in tail)
        ref[at:] = jnp.concatenate(tail + ([jnp.zeros((rest, LANES), jnp.float32)] if rest else []), axis=0)


def fix_x(sz, g, rn, rp):
    l1, l2, l3 = sz.lx
    lower = lane_below(LANES // 2, (1, LANES))

    def take(ref, pieces, level, lo, hi):
        offsets = sz.x_offsets(pieces)
        if lo == 0:
            return [ref[at : at + hi] for at, _ in offsets[level]]
        first = offsets[0][0][1]
        tail = ref[first:]
        return [tail[at - first : at - first + hi - lo] for _, at in offsets[level]]

    def halves(value):
        return [jnp.where(lower, v, 0.0) for v in (value, pltpu.roll(value, LANES // 2, 1))]

    for level in range(3):
        m, w = sz.main[level], sz.ly[level]
        for lo, hi in ((0, m), (m, w)):
            n = take(rn, sz.xp_pieces, level, lo, hi)
            p = take(rp, sz.xn_pieces, level, lo, hi)

            def add(s, xb, q, value):
                g.at(level, s, xb, q)[lo:hi] += value

            if level == 0:
                for q in range(4):
                    add(l1 - 1, 0, q, -RHO * n[q])
                    add(l1 - 1, 1, q, n[q])
                    add(0, 0, q, p[q])
                    add(0, 1, q, RHO * p[q])
            elif level == 1:
                for q in range(2):
                    h0, h1 = n[q], n[2 + q]
                    add(l2 - 2, 0, q, -RHO * h0)
                    add(l2 - 2, 1, q, h0)
                    add(l2 - 1, 0, q, KAPPA * h0 - RHO * h1)
                    add(l2 - 1, 1, q, h1)
                    add(0, 0, q, p[q])
                    add(0, 1, q, p[2 + q])
                    add(1, 0, q, p[4 + q])
                    add(1, 1, q, RHO * p[4 + q])
            else:
                n, p = [halves(v) for v in n], [halves(v) for v in p]
                for q in range(2):
                    add(l3 - 2, 0, q, -RHO * n[0][q])
                    add(l3 - 2, 1, q, n[0][q])
                    add(l3 - 1, 0, q, n[1][q])
                    add(l3 - 1, 1, q, n[2][q])
                    add(0, 0, q, p[0][q])
                    add(0, 1, q, p[1][q])
                    add(1, 0, q, p[2][q])
                    add(1, 1, q, RHO * p[2][q])


def pack_y(sz, g, mp, mn):
    k1, k2, k3 = sz.ly
    at_p = at_n = 4 * sz.lx[0]
    for s in range(sz.lx[1]):
        for xb in range(2):
            mp[at_p : at_p + 2] = g.at(1, s, xb, 1)[0:2]
            mn[at_n : at_n + 2] = g.at(1, s, xb, 0)[k2 - 2 : k2]
            mn[at_n + 2 : at_n + 3] = g.at(1, s, xb, 1)[k2 - 2 : k2 - 1]
            at_p += 2
            at_n += 3
    for s in range(sz.lx[2]):
        for xb in range(2):
            mp[at_p : at_p + 2] = g.at(2, s, xb, 1)[0:2]
            mp[at_p + 2 : at_p + 3] = g.at(2, s, xb, 0)[1:2]
            mn[at_n : at_n + 2] = g.at(2, s, xb, 0)[k3 - 2 : k3]
            mn[at_n + 2 : at_n + 3] = g.at(2, s, xb, 1)[k3 - 2 : k3 - 1]
            at_p += 3
            at_n += 3
    if at_p < sz.yp:
        mp[at_p:] = jnp.zeros((sz.yp - at_p, LANES), jnp.float32)
    if at_n < sz.yn:
        mn[at_n:] = jnp.zeros((sz.yn - at_n, LANES), jnp.float32)


def fix_y_fine(sz, g, rn, rp, rows):
    last = sz.ly[0] - 1
    for s in rows:
        for xb in range(2):
            for tb in range(2):
                at = (2 * tb + xb) * sz.lx[0] + s
                high, low = rn[at : at + 1], rp[at : at + 1]
                g.at(0, s, xb, tb)[last : last + 1] += -RHO * high
                g.at(0, s, xb, 2 + tb)[last : last + 1] += high
                g.at(0, s, xb, tb)[0:1] += low
                g.at(0, s, xb, 2 + tb)[0:1] += RHO * low


def fix_y_coarse(sz, g, rn, rp):
    k1, k2, k3 = sz.ly
    at_p = at_n = 4 * sz.lx[0]

    for level in (1, 2):
        k = sz.ly[level]
        for s in range(sz.lx[level]):
            for xb in range(2):

                def add(q, row, first, second):
                    g.at(level, s, xb, q)[row : row + 2] += jnp.concatenate([first, second], axis=0)

                h0, h1 = rn[at_n : at_n + 1], rn[at_n + 1 : at_n + 2]
                if level == 1:
                    l1 = KAPPA * h0 - RHO * h1
                    at_n += 2
                else:
                    l1 = rn[at_n + 2 : at_n + 3]
                    at_n += 3
                add(0, k - 2, -RHO * h0, l1)
                add(1, k - 2, h0, h1)
                w0, w2, w1 = (rp[at_p + i : at_p + i + 1] for i in range(3))
                add(0, 0, w0, w2)
                add(1, 0, w1, RHO * w2)
                at_p += 3


def shrink(v):
    return v - jnp.clip(v, -THRESHOLD, THRESHOLD)


def y_synthesis(low, high, count, t_ref, v_ref, index, start):
    a = low + RHO * high
    b = RHO * low - high
    t_ref[0 : a.shape[0]] = a
    a = t_ref[1 : 1 + count]
    b = b[:count]
    v_ref[index + (pl.ds(start, count, stride=2), slice(None))] = a - R3 * b
    v_ref[index + (pl.ds(start + 1, count, stride=2), slice(None))] = R3 * a + b


def lane_below(limit, shape):
    return lax.broadcasted_iota(jnp.int32, shape, 1) < limit


def level_1_columns(sz, details, s, xb, tb, coarse, ta, v1, index):
    low = details(0, s, xb, tb, None) if coarse is None else coarse
    high = details(0, s, xb, 2 + tb, None)
    y_synthesis(low, high, sz.y // 2, ta.at[s, xb * 2 + tb], v1, index, 0)


def times_back(sz, v_low, v_high, i1):
    v = jnp.concatenate([v_low, v_high], axis=-1)
    return dot_parts(v.reshape(-1, sz.t), i1).reshape(v.shape)


def inner_inverse(sz, details, i1, ba, ta, v1):
    l1 = sz.lx[0]

    def rows(s):
        for xb in range(2):
            for tb in range(2):
                coarse = 0.0 if xb == 0 and tb == 0 else None
                level_1_columns(sz, details, s, xb, tb, coarse, ta, v1, (tb, s, xb))

    each(1, l1 - 1, rows)
    for s0 in range(1, l1 - 1, 15):
        n = min(15, l1 - 1 - s0)
        ba[s0 : s0 + n] = times_back(sz, v1[0, s0 : s0 + n], v1[1, s0 : s0 + n], i1)


def inverse(sz, details, emit, done, groups, ba, i1, i2, i3, ta1, ta, v3, b3, v2, b2, v1, b1, ve):
    y, t = sz.y, sz.t
    p1, p2, p3 = sz.py
    l1, l2, l3 = sz.lx
    third = lane_below(t // 8, (p3, LANES))

    for s in range(l3):
        for xb in range(2):
            low = details(2, s, xb, 0, third if xb == 0 else None)
            high = details(2, s, xb, 1, None)
            y_synthesis(low, high, sz.ly[1] // 2, ta.at[1, s, xb], v3, (s, xb), 0)
    b3[...] = dot_parts_narrow(v3[:, :, :p2].reshape(l3 * 2 * p2, LANES), i3).reshape(l3, 2, p2, LANES)

    second = lane_below(t // 4, (p2, LANES))
    for p in range(l2 // 2):
        even, odd = lattice_t(b3[p + 1, 0], b3[p + 1, 1], b3[p, 0], b3[p, 1])
        for s, coarse in ((2 * p, even), (2 * p + 1, odd)):
            for xb in range(2):
                low = details(1, s, xb, 0, None)
                if xb == 0:
                    low = jnp.where(second, coarse, low)
                high = details(1, s, xb, 1, None)
                y_synthesis(low, high, (sz.ly[0] + 1) // 2, ta.at[0, s, xb], v2, (s, xb), 7)
    b2[...] = dot_parts_narrow(v2[:, :, 8 : 8 + p1, :].reshape(l2 * 2 * p1, LANES), i2).reshape(l2, 2, p1, LANES)

    def coarse_rows(p):
        return lattice_t(b2[p + 1, 0], b2[p + 1, 1], b2[p, 0], b2[p, 1])

    n = t // 2
    half = jnp.concatenate([i1[0:n], i1[t : t + n], i1[2 * t : 2 * t + n]], axis=0)

    def coarse_columns(s, low):
        y_synthesis(low, 0.0, y // 2, ta1.at[s, 0], v1, (s,), 0)

    def pair_1(p):
        even, odd = coarse_rows(p)
        coarse_columns(2 * p - 1, even)
        if p < l2 - 2:
            coarse_columns(2 * p, odd)
        else:
            ends.append(odd)

    def rows_x(p):
        even, odd = lattice_t(b1[p + 1] + ba[p + 1, 0], ba[p + 1, 1], b1[p] + ba[p, 0], ba[p, 1])
        emit(p, even, odd)

    ends = [coarse_rows(0)[1]]
    step = sz.x // groups
    for x0 in range(0, sz.x, step):
        each(x0 // 4 + 1, (x0 + step) // 4 + 1, pair_1)
        s0, s1 = x0 // 2 + 1, min((x0 + step) // 2 + 1, l1 - 1)
        b1[s0:s1] = dot_parts(v1[s0:s1].reshape(-1, LANES), half).reshape(s1 - s0, y, t)
        if x0 == 0 or x0 + step == sz.x:
            e, s = (0, 0) if x0 == 0 else (1, l1 - 1)
            for xb in range(2):
                for tb in range(2):
                    coarse = ends[e] if xb == 0 and tb == 0 else None
                    level_1_columns(sz, details, s, xb, tb, coarse, ta1, ve, (tb, e, xb))
            ba[s] = times_back(sz, ve[0, e], ve[1, e], i1)
            b1[s] = jnp.zeros((y, t), jnp.float32)
        each(x0 // 2, (x0 + step) // 2, rows_x)
        done(x0, step)


def border(sz, u):
    zeros = jnp.zeros((2 * sz.y, LANES), jnp.float32)
    for h in range(2):
        u[h, 0 : 2 * sz.y, :] = zeros
        u[h, (sz.x + 2) * sz.y :, :] = zeros


def store_u(sz, u, x, value):
    for h in range(2):
        u[h, u_rows(u, x + 2, sz.y), :] = value[:, h * LANES : (h + 1) * LANES]


def scaled_and_weight(c):
    value = c.astype(jnp.float32) * (1.0 / 64.0)
    return value, 1.0 / (1.0 + jnp.abs(value))


def first_kernel(sz, c_hbm, ga, g2, g3, mp, mn, zh, f1, f2, f3, i1, i2, i3, c, sems, u, *scratch):
    step = 4
    copies = [pltpu.make_async_copy(c_hbm.at[x0 : x0 + step], c.at[x0 : x0 + step], sems.at[x0 // step])
              for x0 in range(0, sz.x, step)]
    for copy in copies:
        copy.start()
    border(sz, u)
    for level, (f, i) in enumerate(((f1, i1), (f2, i2), (f3, i3))):
        for m, transposed in ((f, False), (i, True)):
            n = LANES if level else sz.t
            high, low = split(time_matrix(sz.t >> level, n, transposed))
            m[0:n, 0:n] = high
            m[n : 2 * n, 0:n] = high
            if level:
                m[0:n, n:] = low
                m[n:, n:] = jnp.zeros_like(low)
            else:
                m[2 * n :] = low
    for x in range(sz.x):
        if x % step == 0:
            copies[x // step].wait()
        value, weight = scaled_and_weight(c[x])
        store_u(sz, u, x, weight * value)
    forward_coarse(sz, u, f1, f2, f3, Bands(ga, None, g2, g3), zh, mp, mn, *scratch)


def forward_fine_first_kernel(sz, c, zh, f1, gb, u, zl, a1, z1):
    border(sz, u)
    for x in range(sz.x):
        value, weight = scaled_and_weight(c[x])
        store_u(sz, u, x, weight * value)
    forward_fine_kernel(sz, u, zh, f1, gb, zl, a1, z1)


def edge_kernel(sz, gai, gbi, g2i, g3i, rn, rp, ga, gb, g2, g3, mp, mn):
    g = Bands(ga, gb, g2, g3)
    fix_y_coarse(sz, g, rn, rp)
    fix_y_fine(sz, g, rn, rp, (0, sz.lx[0] - 1))
    pack_x(sz, g, mp, mn)


def first_details(g):
    def details(level, s, xb, q, approx_lanes):
        value = g.at(level, s, xb, q)[...]
        small = shrink(value)
        return small if approx_lanes is None else jnp.where(approx_lanes, value, small)

    return details


def second_details(g, q_bands):
    def details(level, s, xb, q, approx_lanes):
        first = g.at(level, s, xb, q)[...]
        second = q_bands.at(level, s, xb, q)[...]
        small = shrink(shrink(first) + (first - second))
        if approx_lanes is None:
            return small
        return jnp.where(approx_lanes, first + (first - second), small)

    return details


def inner_first_kernel(sz, gai, gbi, rn, rp, i1, c, ga, gb, ba, w_ref, ta, v1):
    for x in range(sz.x):
        w_ref[x] = scaled_and_weight(c[x])[1]
    g = Bands(ga, gb, None, None)
    fix_y_fine(sz, g, rn, rp, range(1, sz.lx[0] - 1))
    inner_inverse(sz, first_details(g), i1, ba, ta, v1)


def inner_last_kernel(sz, qai, qbi, rn, rp, i1, ga, gb, qa, qb, ba, ta, v1):
    q = Bands(qa, qb, None, None)
    fix_y_fine(sz, q, rn, rp, range(1, sz.lx[0] - 1))
    inner_inverse(sz, second_details(Bands(ga, gb, None, None), q), i1, ba, ta, v1)


def middle_kernel(sz, gai, gbi, g2i, g3i, bai, rn, rp, w_ref, f1, f2, f3, i1, i2, i3,
                  ga, gb, g2, g3, ba, qa, q2, q3, mp, mn, u, zh, ta1, ta, v3, b3, v2, b2, v1, b1, ve, *scratch):
    g = Bands(ga, gb, g2, g3)
    fix_x(sz, g, rn, rp)
    border(sz, u)

    def emit(p, even, odd):
        store_u(sz, u, 2 * p, w_ref[2 * p] * even)
        store_u(sz, u, 2 * p + 1, w_ref[2 * p + 1] * odd)

    inverse(sz, first_details(g), emit, lambda x0, n: None, 2, ba, i1, i2, i3, ta1, ta, v3, b3, v2, b2, v1, b1, ve)
    forward_coarse(sz, u, f1, f2, f3, Bands(qa, None, q2, q3), zh, mp, mn, *scratch)


def last_kernel(sz, qai, qbi, q2i, q3i, bai, rn, rp, ga, gb, g2, g3, i1, i2, i3,
                qa, qb, q2, q3, ba, out_hbm, out, sems, ta1, ta, v3, b3, v2, b2, v1, b1, ve):
    q = Bands(qa, qb, q2, q3)
    fix_x(sz, q, rn, rp)

    def emit(p, even, odd):
        out[2 * p] = even
        out[2 * p + 1] = odd

    details = second_details(Bands(ga, gb, g2, g3), q)
    copies = []

    def done(x0, n):
        copies.append(pltpu.make_async_copy(out.at[x0 : x0 + n], out_hbm.at[x0 : x0 + n], sems.at[len(copies)]))
        copies[-1].start()

    inverse(sz, details, emit, done, sz.x // 4, ba, i1, i2, i3, ta1, ta, v3, b3, v2, b2, v1, b1, ve)
    for copy in copies:
        copy.wait()


VMEM = pltpu.MemorySpace.VMEM
HBM = pltpu.MemorySpace.HBM


def call(kernel, sz, outs, scratch, aliases, *args, ins_hbm=(), outs_hbm=(), flops=0, limit=36):
    def specs(n, in_hbm):
        return [pl.BlockSpec(memory_space=HBM if k in in_hbm else VMEM) for k in range(n)]

    outs = [s if isinstance(s, jax.ShapeDtypeStruct) else jax.ShapeDtypeStruct(s, jnp.float32) for s in outs]
    return pl.pallas_call(
        functools.partial(kernel, sz),
        out_shape=outs,
        in_specs=specs(len(args), ins_hbm),
        out_specs=specs(len(outs), outs_hbm),
        scratch_shapes=scratch,
        input_output_aliases=aliases,
        cost_estimate=pl.CostEstimate(flops=flops, bytes_accessed=flops // 100, transcendentals=0) if flops else None,
        compiler_params=pltpu.CompilerParams(vmem_limit_bytes=limit * 2**20),
    )(*args)


def on_device(counts):
    sz = Sizes(*counts.shape)
    x, y, t = counts.shape
    l1, l2, l3 = sz.lx
    p1, p2, p3 = sz.py

    def f32(*shapes):
        return [pltpu.VMEM(s, jnp.float32) for s in shapes]

    parts = [jax.ShapeDtypeStruct(s, jnp.bfloat16) for s in ((3 * t, t), (2 * LANES,) * 2, (2 * LANES,) * 2)]
    u, zh = (2, (x + 4) * y, LANES), (l1, sz.zrows[0], LANES)
    sems = [pltpu.SemaphoreType.DMA((x // 4,))]
    fw = f32((2, l1, y, LANES), (l1, sz.zrows[0], LANES), (l2, 2, p1, LANES), (l2, 2, sz.zrows[1], LANES),
             (l3, 2, p2, LANES), (l3, 2, sz.zrows[2], LANES))
    fine = f32((sz.zrows[0], LANES), (2, l1, y, LANES), (l1, 2, sz.zrows[0], LANES))
    ta1 = f32((l1, 4, p1 + 8, LANES))
    bw = ta1 + f32((2, l2, 2, p2 + 8, LANES), (l3, 2, sz.vrows[0], LANES), (l3, 2, p2, LANES), (l2, 2, sz.vrows[1], LANES),
                   (l2, 2, p1, LANES), (l1, y, LANES), (l1, y, t), (2, 2, 2, y, LANES))
    to_prev, to_next = (sz.xp, LANES), (sz.xn, LANES)
    messages = [(sz.yp, LANES), (sz.yn, LANES)]
    halves = [(l1, 2, y, t)]
    inner = ta1 + f32((2, l1, 2, y, LANES))
    work = 6 * l1 * y * t * t
    ga, gb, g2, g3 = sz.g

    def exchange(ga, g2, g3, mp, mn, fine_kernel, fine_scratch, source, zh, f1):
        rn, rp = shifted(mp, "gy", -1), shifted(mn, "gy", 1)
        (gb,) = call(fine_kernel, sz, [sz.g[1]], fine_scratch, {}, source, zh, f1, flops=work)
        *g, mp, mn = call(edge_kernel, sz, sz.g + [to_prev, to_next], [], {k: k for k in range(4)},
                          ga, gb, g2, g3, rn, rp)
        return g, (rn, rp), shifted(mp, "gx", -1), shifted(mn, "gx", 1)

    *rest, z_, f1, f2, f3, i1, i2, i3 = call(
        first_kernel, sz, [ga, g2, g3] + messages + [zh] + parts + parts,
        [pltpu.VMEM((x, y, t), jnp.int32)] + sems + f32(u) + fw, {}, counts, ins_hbm=(0,), limit=50)
    f, i = [f1, f2, f3], [i1, i2, i3]
    g, ry, rn, rp = exchange(*rest, forward_fine_first_kernel, f32(u) + fine, counts, z_, f1)
    *kept, ba, weight = call(inner_first_kernel, sz, [ga, gb] + halves + [(x, y, t)], inner, {0: 0, 1: 1},
                                 g[0], g[1], *ry, i1, counts, flops=work)
    same = {k: k for k in range(5)}
    *rest, q_a, q_2, q_3, mp, mn, u_, zh_ = call(
        middle_kernel, sz, sz.g + halves + [ga, g2, g3] + messages + [u, zh], bw + fw, same,
        *kept, g[2], g[3], ba, rn, rp, weight, *f, *i)
    g = rest[:4]
    q, ry, rn, rp = exchange(q_a, q_2, q_3, mp, mn, forward_fine_kernel, fine, u_, zh_, f1)
    *kept, ba = call(inner_last_kernel, sz, [ga, gb] + halves, inner, {0: 0, 1: 1}, q[0], q[1], *ry, i[0], g[0], g[1],
                         flops=work)
    return call(last_kernel, sz, sz.g + halves + [(x, y, t)], f32((x, y, t)) + sems + bw, same,
                *kept, q[2], q[3], ba, rn, rp, *g, *i, outs_hbm=(5,))[5]


def solution(mesh):
    spec = P(("grp", "gx"), "gy", None)
    return jax.shard_map(on_device, mesh=mesh, in_specs=(spec,), out_specs=spec, check_vma=False)
```

```python
import functools
import math

import jax
import jax.numpy as jnp
from jax import lax
from jax.experimental import pallas as pl
from jax.experimental.pallas import tpu as pltpu
from jax.sharding import PartitionSpec as P

R3 = math.sqrt(3.0)
H0 = (1.0 + R3) / (4.0 * math.sqrt(2.0))
RHO = (1.0 - R3) / (1.0 + R3)
LOW_TAPS = [H0 * t for t in (1.0, R3, -R3 * RHO, RHO)]
HIGH_TAPS = [LOW_TAPS[3], -LOW_TAPS[2], LOW_TAPS[1], -LOW_TAPS[0]]
KAPPA = -R3 * (1.0 + RHO * RHO)
THRESHOLD = 0.1
LANES = 128


def shifted(x, axis, by):
    count = lax.axis_size(axis)
    return lax.ppermute(x, axis, [(i, (i + by) % count) for i in range(count)])


def time_matrix(length, width, transposed):
    half = length // 2
    row = lax.broadcasted_iota(jnp.int32, (width, width), 1 if transposed else 0)
    col = lax.broadcasted_iota(jnp.int32, (width, width), 0 if transposed else 1)
    is_low = col < half
    offset = lax.rem(row - 2 * jnp.where(is_low, col, col - half) + 2 * length, jnp.int32(length))
    value = jnp.zeros((width, width), jnp.float32)
    for j in range(4):
        tap = jnp.where(is_low, jnp.float32(LOW_TAPS[j] * H0 * H0), jnp.float32(HIGH_TAPS[j] * H0 * H0))
        value = jnp.where(offset == j, tap, value)
    return value if length == width else jnp.where((row < length) & (col < length), value, 0.0)


def split(x):
    high = x.astype(jnp.bfloat16)
    return high, (x - high.astype(jnp.float32)).astype(jnp.bfloat16)


def dot_parts(x, m_ref):
    high, low = split(x)
    return jnp.dot(jnp.concatenate([high, low, high], axis=-1), m_ref[...], preferred_element_type=jnp.float32)


def each(first, end, body):
    for i in range(first, end):
        body(i)


def dot_parts_narrow(x, m_ref):
    out = jnp.dot(jnp.concatenate(split(x), axis=-1), m_ref[...], preferred_element_type=jnp.float32)
    return out[:, :LANES] + out[:, LANES:]


def ceil8(n):
    return (n + 7) // 8 * 8


class Sizes:
    def __init__(self, x, y, t):
        self.x, self.y, self.t = x, y, t
        self.lx = [x // 2 + 1, x // 4 + 2, x // 8 + 2]
        self.ly = [y // 2 + 1, y // 4 + 2, y // 8 + 2]
        self.py = [ceil8(n) for n in self.ly]
        p1, p2, p3 = self.py
        self.g = [(self.lx[0], 2, p1, LANES), (self.lx[0], 3, 2, p1, LANES), (self.lx[1], 2, 2, p2, LANES),
                  (self.lx[2], 2, 2, p3, LANES)]
        self.zin = [y, p1, p2]
        self.zbase = [6, 5, 6]
        self.zfill = [ceil8(2 * (p - 1) + 4 + b) for p, b in zip(self.py, self.zbase)]
        self.zrows = [n + 8 for n in self.zfill]
        self.vrows = [2 * ceil8(self.ly[1] // 2), 8 + 2 * ceil8((self.ly[0] + 1) // 2)]
        self.main = [y // 2, y // 4, y // 8]
        self.xp_pieces = [4, 4, 3]
        self.xn_pieces = [4, 6, 3]
        self.xp = self.x_rows(self.xp_pieces)
        self.xn = self.x_rows(self.xn_pieces)
        n1, n2, n3 = self.lx[0] * 4, self.lx[1] * 2, self.lx[2] * 2
        self.yp = ceil8(n1 + 2 * n2 + 3 * n3) + 8
        self.yn = ceil8(n1 + 3 * n2 + 3 * n3) + 8


    def x_rows(self, pieces):
        return ceil8(sum(n * w for n, w in zip(pieces, self.ly)))

    def x_offsets(self, pieces):
        at = 0
        mains, extras = [], []
        for n, m in zip(pieces, self.main):
            mains.append([at + i * m for i in range(n)])
            at += n * m
        for n, m, w in zip(pieces, self.main, self.ly):
            extras.append([at + i * (w - m) for i in range(n)])
            at += n * (w - m)
        return [list(zip(a, b)) for a, b in zip(mains, extras)]


def lattice(v0, v1, v2, v3):
    a = v0 + R3 * v1
    b = v3 - R3 * v2
    return a + RHO * b, RHO * a - b


def lattice_t(low_next, high_next, low_here, high_here):
    a = low_next + RHO * high_next
    b = RHO * low_here - high_here
    return a - R3 * b, R3 * a + b


def x_lattice_static(rows, shape):
    v = [jnp.zeros(shape, jnp.float32) if r is None else r for r in rows]
    return lattice(*v)


class Bands:
    def __init__(self, ga, gb, g2, g3):
        self.ga, self.gb, self.g2, self.g3 = ga, gb, g2, g3

    def at(self, level, s, xb, q):
        if level == 1:
            return self.g2.at[s, xb, q]
        if level == 2:
            return self.g3.at[s, xb, q]
        pair, yb = 2 * xb + q % 2, q // 2
        return self.ga.at[s, yb] if pair == 0 else self.gb.at[s, pair - 1, yb]


def y_analysis(z_ref, base, count, low_ref, high_ref):
    v = [z_ref[pl.ds(base + j, count, stride=2), :] for j in range(4)]
    low, high = lattice(*v)
    low_ref[...] = low
    high_ref[...] = high


def u_rows(u, x, y):
    return pl.ds(x * y, y)


def x_lattice_rows(u, h, s, y):
    return lattice(*[u[h, u_rows(u, 2 * s + j, y), :] for j in range(4)])


def pad_z(z, index, lo, hi, total):
    z[index + (slice(0, lo), slice(None))] = jnp.zeros((lo, LANES), jnp.float32)
    if hi < total:
        z[index + (slice(hi, total), slice(None))] = jnp.zeros((total - hi, LANES), jnp.float32)


def forward_coarse(sz, step, u, f1, f2, f3, g, zh, mp, mn, a1, z1, a2, z2, a3, z3):
    x, y, t = sz.x, sz.y, sz.t
    l1 = sz.lx[0]

    def rows_x(s):
        for h in range(2):
            a1[h, s] = x_lattice_rows(u, h, s, y)[0]

    each(0, l1, rows_x)

    for s0 in range(0, l1, step):
        n = min(step, l1 - s0)
        out = dot_parts(jnp.concatenate([a1[0, s0 : s0 + n], a1[1, s0 : s0 + n]], axis=-1).reshape(n * y, t), f1)
        out = out.reshape(n, y, t)
        z1[s0 : s0 + n, 8 : 8 + y, :] = out[..., :LANES]
        zh[s0 : s0 + n, 8 : 8 + y, :] = out[..., LANES:]

    def cols_1(s):
        pad_z(z1, (s,), 8, 8 + y, sz.zfill[0])
        y_analysis(z1.at[s], sz.zbase[0], sz.py[0], g.at(0, s, 0, 0), g.at(0, s, 0, 2))

    each(0, l1, cols_1)

    def column(h, j, col):
        last = (2 * (l1 - 1) + j) * y + col
        return jnp.concatenate(
            [u[h, pl.ds(j * y + col, l1 - 1, stride=2 * y), :], u[h, last : last + 1, :]], axis=0)

    edges = []
    for c0, c1, w0, w1 in ((0, 1, R3, -1.0), (y - 2, y - 1, 1.0, R3)):
        halves = [lattice(*[w0 * column(h, j, c0) + w1 * column(h, j, c1) for j in range(4)]) for h in range(2)]
        pad = jnp.zeros((ceil8(l1) - l1, t), jnp.float32)
        for xb in range(2):
            edges += [jnp.concatenate([halves[0][xb], halves[1][xb]], axis=-1), pad]
    out = dot_parts(jnp.concatenate(edges, axis=0), f1)
    for m, at in ((mp, 0), (mn, 2)):
        for tb in range(2):
            for xb in range(2):
                row = (at + xb) * ceil8(l1)
                to = (2 * tb + xb) * l1
                m[to : to + l1] = out[row : row + l1, tb * LANES : (tb + 1) * LANES]

    for level, (offset, a, z, f) in enumerate(((3, a2, z2, f2), (2, a3, z3, f3)), 1):
        rows_in, count = sz.lx[level - 1], sz.lx[level]
        p_in, p_out = sz.py[level - 1], sz.py[level]
        for s in range(count):
            picks = [2 * s + j - offset for j in range(4)]
            rows = [g.at(level - 1, i, 0, 0)[...] if 0 <= i < rows_in else None for i in picks]
            low, high = x_lattice_static(rows, (p_in, LANES))
            a[s, 0] = low
            a[s, 1] = high
        out = dot_parts_narrow(a[...].reshape(count * 2 * p_in, LANES), f)
        z[:, :, 8 : 8 + p_in, :] = out.reshape(count, 2, p_in, LANES)
        for s in range(count):
            for xb in range(2):
                pad_z(z, (s, xb), 8, 8 + p_in, sz.zfill[level])
                y_analysis(z.at[s, xb], sz.zbase[level], p_out, g.at(level, s, xb, 0), g.at(level, s, xb, 1))
    pack_y(sz, g, mp, mn)


def forward_fine_kernel(sz, u, zh, f1, gb, zl, a1, z1):
    x, y, t = sz.x, sz.y, sz.t
    l1 = sz.lx[0]

    def rows_x(s):
        for h in range(2):
            a1[h, s] = x_lattice_rows(u, h, s, y)[1]

    each(0, l1, rows_x)

    step = 9
    for s0 in range(0, l1, step):
        n = min(step, l1 - s0)
        out = dot_parts(jnp.concatenate([a1[0, s0 : s0 + n], a1[1, s0 : s0 + n]], axis=-1).reshape(n * y, t), f1)
        out = out.reshape(n, y, t)
        z1[s0 : s0 + n, 0, 8 : 8 + y, :] = out[..., :LANES]
        z1[s0 : s0 + n, 1, 8 : 8 + y, :] = out[..., LANES:]

    def cols_1(s):
        zl[8 : 8 + y] = zh[s, 8 : 8 + y, :]
        y_analysis(zl, sz.zbase[0], sz.py[0], gb.at[s, 0, 0], gb.at[s, 0, 1])
        for tb in range(2):
            pad_z(z1, (s, tb), 8, 8 + y, sz.zfill[0])
            y_analysis(z1.at[s, tb], sz.zbase[0], sz.py[0], gb.at[s, 1 + tb, 0], gb.at[s, 1 + tb, 1])

    pad_z(zl, (), 8, 8 + y, sz.zfill[0])
    each(0, l1, cols_1)


def pack_x(sz, g, mp, mn):
    l1, l2, l3 = sz.lx
    lower = lane_below(LANES // 2, (1, LANES))

    def put(ref, pieces, level, items):
        m, w = sz.main[level], sz.ly[level]
        for (main, extra), item in zip(sz.x_offsets(pieces)[level], items):
            for at, lo, hi in ((main, 0, m), (extra, m, w)):
                value = item[0][lo:hi]
                if level == 2:
                    value = jnp.where(lower, value, pltpu.roll(item[1][lo:hi], LANES // 2, 1))
                if lo == 0:
                    ref[at : at + hi] = value
                else:
                    tails[ref is mn].append(value)

    tails = [], []
    put(mp, sz.xp_pieces, 0, [[g.at(0, 0, 1, q)] for q in range(4)])
    put(mn, sz.xn_pieces, 0, [[g.at(0, l1 - 1, 0, q)] for q in range(4)])
    put(mp, sz.xp_pieces, 1, [[g.at(1, s, 1, q)] for s in (0, 1) for q in (0, 1)])
    put(mn, sz.xn_pieces, 1, [[g.at(1, s, b, q)] for s, b in ((l2 - 2, 0), (l2 - 2, 1), (l2 - 1, 0)) for q in (0, 1)])
    put(mp, sz.xp_pieces, 2, [[g.at(2, s, b, q) for q in (0, 1)] for s, b in ((0, 1), (1, 0), (1, 1))])
    put(mn, sz.xn_pieces, 2, [[g.at(2, s, b, q) for q in (0, 1)] for s, b in ((l3 - 2, 0), (l3 - 2, 1), (l3 - 1, 0))])
    for ref, tail, pieces in ((mp, tails[0], sz.xp_pieces), (mn, tails[1], sz.xn_pieces)):
        at = sz.x_offsets(pieces)[0][0][1]
        rest = ref.shape[0] - at - sum(v.shape[0] for v in tail)
        ref[at:] = jnp.concatenate(tail + ([jnp.zeros((rest, LANES), jnp.float32)] if rest else []), axis=0)


def fix_x(sz, g, rn, rp):
    l1, l2, l3 = sz.lx
    lower = lane_below(LANES // 2, (1, LANES))

    def take(ref, pieces, level, lo, hi):
        offsets = sz.x_offsets(pieces)
        if lo == 0:
            return [ref[at : at + hi] for at, _ in offsets[level]]
        first = offsets[0][0][1]
        tail = ref[first:]
        return [tail[at - first : at - first + hi - lo] for _, at in offsets[level]]

    def halves(value):
        return [jnp.where(lower, v, 0.0) for v in (value, pltpu.roll(value, LANES // 2, 1))]

    for level in range(3):
        m, w = sz.main[level], sz.ly[level]
        for lo, hi in ((0, m), (m, w)):
            n = take(rn, sz.xp_pieces, level, lo, hi)
            p = take(rp, sz.xn_pieces, level, lo, hi)

            def add(s, xb, q, value):
                g.at(level, s, xb, q)[lo:hi] += value

            if level == 0:
                for q in range(4):
                    add(l1 - 1, 0, q, -RHO * n[q])
                    add(l1 - 1, 1, q, n[q])
                    add(0, 0, q, p[q])
                    add(0, 1, q, RHO * p[q])
            elif level == 1:
                for q in range(2):
                    h0, h1 = n[q], n[2 + q]
                    add(l2 - 2, 0, q, -RHO * h0)
                    add(l2 - 2, 1, q, h0)
                    add(l2 - 1, 0, q, KAPPA * h0 - RHO * h1)
                    add(l2 - 1, 1, q, h1)
                    add(0, 0, q, p[q])
                    add(0, 1, q, p[2 + q])
                    add(1, 0, q, p[4 + q])
                    add(1, 1, q, RHO * p[4 + q])
            else:
                n, p = [halves(v) for v in n], [halves(v) for v in p]
                for q in range(2):
                    add(l3 - 2, 0, q, -RHO * n[0][q])
                    add(l3 - 2, 1, q, n[0][q])
                    add(l3 - 1, 0, q, n[1][q])
                    add(l3 - 1, 1, q, n[2][q])
                    add(0, 0, q, p[0][q])
                    add(0, 1, q, p[1][q])
                    add(1, 0, q, p[2][q])
                    add(1, 1, q, RHO * p[2][q])


def pack_y(sz, g, mp, mn):
    k1, k2, k3 = sz.ly
    at_p = at_n = 4 * sz.lx[0]
    for s in range(sz.lx[1]):
        for xb in range(2):
            mp[at_p : at_p + 2] = g.at(1, s, xb, 1)[0:2]
            mn[at_n : at_n + 2] = g.at(1, s, xb, 0)[k2 - 2 : k2]
            mn[at_n + 2 : at_n + 3] = g.at(1, s, xb, 1)[k2 - 2 : k2 - 1]
            at_p += 2
            at_n += 3
    for s in range(sz.lx[2]):
        for xb in range(2):
            mp[at_p : at_p + 2] = g.at(2, s, xb, 1)[0:2]
            mp[at_p + 2 : at_p + 3] = g.at(2, s, xb, 0)[1:2]
            mn[at_n : at_n + 2] = g.at(2, s, xb, 0)[k3 - 2 : k3]
            mn[at_n + 2 : at_n + 3] = g.at(2, s, xb, 1)[k3 - 2 : k3 - 1]
            at_p += 3
            at_n += 3
    if at_p < sz.yp:
        mp[at_p:] = jnp.zeros((sz.yp - at_p, LANES), jnp.float32)
    if at_n < sz.yn:
        mn[at_n:] = jnp.zeros((sz.yn - at_n, LANES), jnp.float32)


def fix_y_fine(sz, g, rn, rp, rows):
    last = sz.ly[0] - 1
    for s in rows:
        for xb in range(2):
            for tb in range(2):
                at = (2 * tb + xb) * sz.lx[0] + s
                high, low = rn[at : at + 1], rp[at : at + 1]
                g.at(0, s, xb, tb)[last : last + 1] += -RHO * high
                g.at(0, s, xb, 2 + tb)[last : last + 1] += high
                g.at(0, s, xb, tb)[0:1] += low
                g.at(0, s, xb, 2 + tb)[0:1] += RHO * low


def fix_y_coarse(sz, g, rn, rp):
    k1, k2, k3 = sz.ly
    at_p = at_n = 4 * sz.lx[0]

    for level in (1, 2):
        k = sz.ly[level]
        for s in range(sz.lx[level]):
            for xb in range(2):

                def add(q, row, first, second):
                    g.at(level, s, xb, q)[row : row + 2] += jnp.concatenate([first, second], axis=0)

                h0, h1 = rn[at_n : at_n + 1], rn[at_n + 1 : at_n + 2]
                if level == 1:
                    l1 = KAPPA * h0 - RHO * h1
                    at_n += 2
                else:
                    l1 = rn[at_n + 2 : at_n + 3]
                    at_n += 3
                add(0, k - 2, -RHO * h0, l1)
                add(1, k - 2, h0, h1)
                w0, w2, w1 = (rp[at_p + i : at_p + i + 1] for i in range(3))
                add(0, 0, w0, w2)
                add(1, 0, w1, RHO * w2)
                at_p += 3


def shrink(v):
    return v - jnp.clip(v, -THRESHOLD, THRESHOLD)


def y_synthesis(low, high, count, t_ref, v_ref, index, start):
    a = low + RHO * high
    b = RHO * low - high
    t_ref[0 : a.shape[0]] = a
    a = t_ref[1 : 1 + count]
    b = b[:count]
    v_ref[index + (pl.ds(start, count, stride=2), slice(None))] = a - R3 * b
    v_ref[index + (pl.ds(start + 1, count, stride=2), slice(None))] = R3 * a + b


def lane_below(limit, shape):
    return lax.broadcasted_iota(jnp.int32, shape, 1) < limit


def level_1_columns(sz, details, s, xb, tb, coarse, ta, v1, index):
    low = details(0, s, xb, tb, None) if coarse is None else coarse
    high = details(0, s, xb, 2 + tb, None)
    y_synthesis(low, high, sz.y // 2, ta.at[s, xb * 2 + tb], v1, index, 0)


def times_back(sz, v_low, v_high, i1):
    v = jnp.concatenate([v_low, v_high], axis=-1)
    return dot_parts(v.reshape(-1, sz.t), i1).reshape(v.shape)


def inner_inverse(sz, details, i1, ba, ta, v1):
    l1 = sz.lx[0]

    def rows(s):
        for xb in range(2):
            for tb in range(2):
                coarse = 0.0 if xb == 0 and tb == 0 else None
                level_1_columns(sz, details, s, xb, tb, coarse, ta, v1, (tb, s, xb))

    each(1, l1 - 1, rows)
    for s0 in range(1, l1 - 1, 15):
        n = min(15, l1 - 1 - s0)
        ba[s0 : s0 + n] = times_back(sz, v1[0, s0 : s0 + n], v1[1, s0 : s0 + n], i1)


def inverse(sz, details, emit, done, groups, ba, i1, i2, i3, ta1, ta, v3, b3, v2, b2, v1, b1, ve):
    y, t = sz.y, sz.t
    p1, p2, p3 = sz.py
    l1, l2, l3 = sz.lx
    third = lane_below(t // 8, (p3, LANES))

    for s in range(l3):
        for xb in range(2):
            low = details(2, s, xb, 0, third if xb == 0 else None)
            high = details(2, s, xb, 1, None)
            y_synthesis(low, high, sz.ly[1] // 2, ta.at[1, s, xb], v3, (s, xb), 0)
    b3[...] = dot_parts_narrow(v3[:, :, :p2].reshape(l3 * 2 * p2, LANES), i3).reshape(l3, 2, p2, LANES)

    second = lane_below(t // 4, (p2, LANES))
    for p in range(l2 // 2):
        even, odd = lattice_t(b3[p + 1, 0], b3[p + 1, 1], b3[p, 0], b3[p, 1])
        for s, coarse in ((2 * p, even), (2 * p + 1, odd)):
            for xb in range(2):
                low = details(1, s, xb, 0, None)
                if xb == 0:
                    low = jnp.where(second, coarse, low)
                high = details(1, s, xb, 1, None)
                y_synthesis(low, high, (sz.ly[0] + 1) // 2, ta.at[0, s, xb], v2, (s, xb), 7)
    b2[...] = dot_parts_narrow(v2[:, :, 8 : 8 + p1, :].reshape(l2 * 2 * p1, LANES), i2).reshape(l2, 2, p1, LANES)

    def coarse_rows(p):
        return lattice_t(b2[p + 1, 0], b2[p + 1, 1], b2[p, 0], b2[p, 1])

    n = t // 2
    half = jnp.concatenate([i1[0:n], i1[t : t + n], i1[2 * t : 2 * t + n]], axis=0)

    def coarse_columns(s, low):
        y_synthesis(low, 0.0, y // 2, ta1.at[s, 0], v1, (s,), 0)

    def pair_1(p):
        even, odd = coarse_rows(p)
        coarse_columns(2 * p - 1, even)
        if p < l2 - 2:
            coarse_columns(2 * p, odd)
        else:
            ends.append(odd)

    def rows_x(p):
        even, odd = lattice_t(b1[p + 1] + ba[p + 1, 0], ba[p + 1, 1], b1[p] + ba[p, 0], ba[p, 1])
        emit(p, even, odd)

    ends = [coarse_rows(0)[1]]
    step = sz.x // groups
    for x0 in range(0, sz.x, step):
        each(x0 // 4 + 1, (x0 + step) // 4 + 1, pair_1)
        s0, s1 = x0 // 2 + 1, min((x0 + step) // 2 + 1, l1 - 1)
        b1[s0:s1] = dot_parts(v1[s0:s1].reshape(-1, LANES), half).reshape(s1 - s0, y, t)
        if x0 == 0 or x0 + step == sz.x:
            e, s = (0, 0) if x0 == 0 else (1, l1 - 1)
            for xb in range(2):
                for tb in range(2):
                    coarse = ends[e] if xb == 0 and tb == 0 else None
                    level_1_columns(sz, details, s, xb, tb, coarse, ta1, ve, (tb, e, xb))
            ba[s] = times_back(sz, ve[0, e], ve[1, e], i1)
            b1[s] = jnp.zeros((y, t), jnp.float32)
        each(x0 // 2, (x0 + step) // 2, rows_x)
        done(x0, step)


def border(sz, u):
    zeros = jnp.zeros((2 * sz.y, LANES), jnp.float32)
    for h in range(2):
        u[h, 0 : 2 * sz.y, :] = zeros
        u[h, (sz.x + 2) * sz.y :, :] = zeros


def store_u(sz, u, x, value):
    for h in range(2):
        u[h, u_rows(u, x + 2, sz.y), :] = value[:, h * LANES : (h + 1) * LANES]


def scaled_and_weight(c):
    value = c.astype(jnp.float32) * (1.0 / 64.0)
    return value, 1.0 / (1.0 + jnp.abs(value))


def first_kernel(sz, c_hbm, ga, g2, g3, mp, mn, zh, f1, f2, f3, i1, i2, i3, c, sems, u, *scratch):
    step = 4
    copies = [pltpu.make_async_copy(c_hbm.at[x0 : x0 + step], c.at[x0 : x0 + step], sems.at[x0 // step])
              for x0 in range(0, sz.x, step)]
    for copy in copies:
        copy.start()
    border(sz, u)
    for level, (f, i) in enumerate(((f1, i1), (f2, i2), (f3, i3))):
        for m, transposed in ((f, False), (i, True)):
            n = LANES if level else sz.t
            high, low = split(time_matrix(sz.t >> level, n, transposed))
            m[0:n, 0:n] = high
            m[n : 2 * n, 0:n] = high
            if level:
                m[0:n, n:] = low
                m[n:, n:] = jnp.zeros_like(low)
            else:
                m[2 * n :] = low
    for x in range(sz.x):
        if x % step == 0:
            copies[x // step].wait()
        value, weight = scaled_and_weight(c[x])
        store_u(sz, u, x, weight * value)
    forward_coarse(sz, sz.lx[0], u, f1, f2, f3, Bands(ga, None, g2, g3), zh, mp, mn, *scratch)


def forward_fine_first_kernel(sz, c, zh, f1, gb, u, zl, a1, z1):
    border(sz, u)
    for x in range(sz.x):
        value, weight = scaled_and_weight(c[x])
        store_u(sz, u, x, weight * value)
    forward_fine_kernel(sz, u, zh, f1, gb, zl, a1, z1)


def edge_kernel(sz, gai, gbi, g2i, g3i, rn, rp, ga, gb, g2, g3, mp, mn):
    g = Bands(ga, gb, g2, g3)
    fix_y_coarse(sz, g, rn, rp)
    fix_y_fine(sz, g, rn, rp, (0, sz.lx[0] - 1))
    pack_x(sz, g, mp, mn)


def first_details(g):
    def details(level, s, xb, q, approx_lanes):
        value = g.at(level, s, xb, q)[...]
        small = shrink(value)
        return small if approx_lanes is None else jnp.where(approx_lanes, value, small)

    return details


def second_details(g, q_bands):
    def details(level, s, xb, q, approx_lanes):
        first = g.at(level, s, xb, q)[...]
        second = q_bands.at(level, s, xb, q)[...]
        small = shrink(shrink(first) + (first - second))
        if approx_lanes is None:
            return small
        return jnp.where(approx_lanes, first + (first - second), small)

    return details


def inner_first_kernel(sz, gai, gbi, rn, rp, i1, c, ga, gb, ba, w_ref, ta, v1):
    for x in range(sz.x):
        w_ref[x] = scaled_and_weight(c[x])[1]
    g = Bands(ga, gb, None, None)
    fix_y_fine(sz, g, rn, rp, range(1, sz.lx[0] - 1))
    inner_inverse(sz, first_details(g), i1, ba, ta, v1)


def inner_last_kernel(sz, qai, qbi, rn, rp, i1, ga, gb, qa, qb, ba, ta, v1):
    q = Bands(qa, qb, None, None)
    fix_y_fine(sz, q, rn, rp, range(1, sz.lx[0] - 1))
    inner_inverse(sz, second_details(Bands(ga, gb, None, None), q), i1, ba, ta, v1)


def middle_kernel(sz, gai, gbi, g2i, g3i, bai, rn, rp, w_ref, f1, f2, f3, i1, i2, i3,
                  ga, gb, g2, g3, ba, qa, q2, q3, mp, mn, u, zh, ta1, ta, v3, b3, v2, b2, v1, b1, ve, *scratch):
    g = Bands(ga, gb, g2, g3)
    fix_x(sz, g, rn, rp)
    border(sz, u)

    def emit(p, even, odd):
        store_u(sz, u, 2 * p, w_ref[2 * p] * even)
        store_u(sz, u, 2 * p + 1, w_ref[2 * p + 1] * odd)

    inverse(sz, first_details(g), emit, lambda x0, n: None, 2, ba, i1, i2, i3, ta1, ta, v3, b3, v2, b2, v1, b1, ve)
    forward_coarse(sz, 9, u, f1, f2, f3, Bands(qa, None, q2, q3), zh, mp, mn, *scratch)


def last_kernel(sz, qai, qbi, q2i, q3i, bai, rn, rp, ga, gb, g2, g3, i1, i2, i3,
                qa, qb, q2, q3, ba, out_hbm, out, sems, ta1, ta, v3, b3, v2, b2, v1, b1, ve):
    q = Bands(qa, qb, q2, q3)
    fix_x(sz, q, rn, rp)

    def emit(p, even, odd):
        out[2 * p] = even
        out[2 * p + 1] = odd

    details = second_details(Bands(ga, gb, g2, g3), q)
    copies = []

    def done(x0, n):
        copies.append(pltpu.make_async_copy(out.at[x0 : x0 + n], out_hbm.at[x0 : x0 + n], sems.at[len(copies)]))
        copies[-1].start()

    inverse(sz, details, emit, done, sz.x // 4, ba, i1, i2, i3, ta1, ta, v3, b3, v2, b2, v1, b1, ve)
    for copy in copies:
        copy.wait()


VMEM = pltpu.MemorySpace.VMEM
HBM = pltpu.MemorySpace.HBM


def call(kernel, sz, outs, scratch, aliases, *args, ins_hbm=(), outs_hbm=(), flops=0, limit=36):
    def specs(n, in_hbm):
        return [pl.BlockSpec(memory_space=HBM if k in in_hbm else VMEM) for k in range(n)]

    outs = [s if isinstance(s, jax.ShapeDtypeStruct) else jax.ShapeDtypeStruct(s, jnp.float32) for s in outs]
    return pl.pallas_call(
        functools.partial(kernel, sz),
        out_shape=outs,
        in_specs=specs(len(args), ins_hbm),
        out_specs=specs(len(outs), outs_hbm),
        scratch_shapes=scratch,
        input_output_aliases=aliases,
        cost_estimate=pl.CostEstimate(flops=flops, bytes_accessed=flops // 100, transcendentals=0) if flops else None,
        compiler_params=pltpu.CompilerParams(vmem_limit_bytes=limit * 2**20),
    )(*args)


def on_device(counts):
    sz = Sizes(*counts.shape)
    x, y, t = counts.shape
    l1, l2, l3 = sz.lx
    p1, p2, p3 = sz.py

    def f32(*shapes):
        return [pltpu.VMEM(s, jnp.float32) for s in shapes]

    parts = [jax.ShapeDtypeStruct(s, jnp.bfloat16) for s in ((3 * t, t), (2 * LANES,) * 2, (2 * LANES,) * 2)]
    u, zh = (2, (x + 4) * y, LANES), (l1, sz.zrows[0], LANES)
    sems = [pltpu.SemaphoreType.DMA((x // 4,))]
    fw = f32((2, l1, y, LANES), (l1, sz.zrows[0], LANES), (l2, 2, p1, LANES), (l2, 2, sz.zrows[1], LANES),
             (l3, 2, p2, LANES), (l3, 2, sz.zrows[2], LANES))
    fine = f32((sz.zrows[0], LANES), (2, l1, y, LANES), (l1, 2, sz.zrows[0], LANES))
    ta1 = f32((l1, 4, p1 + 8, LANES))
    bw = ta1 + f32((2, l2, 2, p2 + 8, LANES), (l3, 2, sz.vrows[0], LANES), (l3, 2, p2, LANES), (l2, 2, sz.vrows[1], LANES),
                   (l2, 2, p1, LANES), (l1, y, LANES), (l1, y, t), (2, 2, 2, y, LANES))
    to_prev, to_next = (sz.xp, LANES), (sz.xn, LANES)
    messages = [(sz.yp, LANES), (sz.yn, LANES)]
    halves = [(l1, 2, y, t)]
    inner = ta1 + f32((2, l1, 2, y, LANES))
    work = 6 * l1 * y * t * t
    ga, gb, g2, g3 = sz.g

    def exchange(ga, g2, g3, mp, mn, fine_kernel, fine_scratch, source, zh, f1):
        rn, rp = shifted(mp, "gy", -1), shifted(mn, "gy", 1)
        (gb,) = call(fine_kernel, sz, [sz.g[1]], fine_scratch, {}, source, zh, f1, flops=work)
        *g, mp, mn = call(edge_kernel, sz, sz.g + [to_prev, to_next], [], {k: k for k in range(4)},
                          ga, gb, g2, g3, rn, rp)
        return g, (rn, rp), shifted(mp, "gx", -1), shifted(mn, "gx", 1)

    *rest, z_, f1, f2, f3, i1, i2, i3 = call(
        first_kernel, sz, [ga, g2, g3] + messages + [zh] + parts + parts,
        [pltpu.VMEM((x, y, t), jnp.int32)] + sems + f32(u) + fw, {}, counts, ins_hbm=(0,), limit=50)
    f, i = [f1, f2, f3], [i1, i2, i3]
    g, ry, rn, rp = exchange(*rest, forward_fine_first_kernel, f32(u) + fine, counts, z_, f1)
    *kept, ba, weight = call(inner_first_kernel, sz, [ga, gb] + halves + [(x, y, t)], inner, {0: 0, 1: 1},
                                 g[0], g[1], *ry, i1, counts, flops=work)
    same = {k: k for k in range(5)}
    *rest, q_a, q_2, q_3, mp, mn, u_, zh_ = call(
        middle_kernel, sz, sz.g + halves + [ga, g2, g3] + messages + [u, zh], bw + fw, same,
        *kept, g[2], g[3], ba, rn, rp, weight, *f, *i)
    g = rest[:4]
    q, ry, rn, rp = exchange(q_a, q_2, q_3, mp, mn, forward_fine_kernel, fine, u_, zh_, f1)
    *kept, ba = call(inner_last_kernel, sz, [ga, gb] + halves, inner, {0: 0, 1: 1}, q[0], q[1], *ry, i[0], g[0], g[1],
                         flops=work)
    return call(last_kernel, sz, sz.g + halves + [(x, y, t)], f32((x, y, t)) + sems + bw, same,
                *kept, q[2], q[3], ba, rn, rp, *g, *i, outs_hbm=(5,))[5]


def solution(mesh):
    spec = P(("grp", "gx"), "gy", None)
    return jax.shard_map(on_device, mesh=mesh, in_specs=(spec,), out_specs=spec, check_vma=False)
```
